32 devices in a mesh: dp: 4 (over z), expert: 8 (over y, x, core).
Axes of the slice: x: 2, y: 2, z: 4, core: 2. Of those that a mesh axis runs over, the one named last changes fastest.
Arguments:
- inputs: bfloat16 [4, 3072, 768], P('dp', 'expert'), may hold values from -6 to 6
- gain_one: float32 [768], replicated, may hold values from 0.5 to 1.5
- w_query: bfloat16 [768, 768], replicated, may hold values from -0.21875 to 0.21875
- w_key: bfloat16 [768, 768], replicated, may hold values from -0.21875 to 0.21875
- w_value: bfloat16 [768, 768], replicated, may hold values from -0.21875 to 0.21875
- w_out_proj: bfloat16 [768, 768], replicated, may hold values from -1.25 to 1.25
- gain_two: float32 [768], replicated, may hold values from 0.5 to 1.5
- w_router: bfloat16 [768, 16], replicated, may hold values from -0.14941406 to 0.14941406
- w_in: bfloat16 [16, 768, 3072], P('expert'), may hold values from -0.21875 to 0.21875
- w_out: bfloat16 [16, 3072, 768], P('expert'), may hold values from -0.109375 to 0.109375
- routes: int32 [4, 3072, 2], P('dp', 'expert'), may hold values from 0 to 15, as said below
- slot_index: int32 [4, 3072, 2], P('dp', 'expert'), may hold values from 0 to 60, as said below
- prompt_of: int32 [4, 8], P('dp', 'expert'), may hold values from 0 to 1
- cotangent: bfloat16 [4, 3072, 768], P('dp', 'expert'), may hold values from -6 to 6
Outputs:
- outputs: bfloat16 [4, 3072, 768], P('dp', 'expert')
- grad_input: float32 [4, 3072, 768], P('dp', 'expert')
- grad_gain_one: float32 [768], replicated
- grad_query: float32 [768, 768], replicated
- grad_key: float32 [768, 768], replicated
- grad_value: float32 [768, 768], replicated
- grad_out_proj: float32 [768, 768], replicated
- grad_gain_two: float32 [768], replicated
- grad_router: float32 [768, 16], replicated
- grad_w_in: float32 [16, 768, 3072], P('expert', 'dp')
- grad_w_out: float32 [16, 3072, 768], P('expert', 'dp')
The draws below stay inside these ranges and needn't reach their ends.
Inputs may be any that keep to these rules, and one draw needn't show every extreme that they name: `routes`: the two experts of a row differ. slot_index[g, t, k] counts the pairs before (t, k) in the rows of the same device (384 rows in a row, pairs in order of row, then k) that name the same expert, or is 60 where that count is 60 or more; such a pair is dropped.
All inputs are finite; a program needn't handle non-finite values.
Results may differ from the reference program's by a relative error of at most 0.015.
Values may be sent and summed in bfloat16 or wider, within the bound.
No kernel may reach another device: no remote copies, remote signals or barrier semaphores. Data moves between devices by JAX's collectives and lax.ppermute only.
A program may use at most 256 MiB of HBM per device.

```python
import jax
import jax.numpy as jnp
from jax import lax

D = 768
H = 12
HD = 64
FF = 3072
TOP = 2
NPR = 2
CLEN = 128
PR_DEV = 128
GROUPS = 4
NCONT = 8
PLEN = 1024
ROWS_DEV = 384
TOK = 3072
SPECIALIST_COUNT = 16
CAP = 60
N_EXPERT = 8


def route_table(key):
    first, second, third = jax.random.split(key, 3)
    affinity_table = jax.random.randint(first, (GROUPS, N_EXPERT, ROWS_DEV, SPECIALIST_COUNT), 0, 65536)
    bias_preactivations = jax.random.randint(second, (GROUPS, 1, 1, SPECIALIST_COUNT), 0, 32768)
    preferred_specialist = jax.random.randint(third, (GROUPS, 1, 1, 1), 0, SPECIALIST_COUNT)
    field_position = jnp.arange(SPECIALIST_COUNT)[None, None, None, :]
    prior_filter = jnp.arange(ROWS_DEV)[None, None, :, None] <= CAP
    extra_increment = jnp.where(prior_filter & (field_position == preferred_specialist), 262144, 0)
    grand_aggregate = (affinity_table + bias_preactivations + extra_increment) * SPECIALIST_COUNT + field_position
    unused, chosen = lax.top_k(grand_aggregate.astype(jnp.int32), TOP)
    chosen = chosen.astype(jnp.int32)
    onehot = (chosen[..., None] == field_position[..., None, :]).astype(jnp.int32)
    flat = onehot.reshape(GROUPS, N_EXPERT, ROWS_DEV * TOP, SPECIALIST_COUNT)
    earlier = jnp.cumsum(flat, axis=2) - flat
    counted = jnp.sum(earlier * flat, axis=-1).reshape(GROUPS, N_EXPERT, ROWS_DEV, TOP)
    counted = jnp.minimum(counted, CAP).astype(jnp.int32)
    return (chosen.reshape(GROUPS, TOK, TOP), counted.reshape(GROUPS, TOK, TOP))


def draw_routes(key, part):
    return route_table(key)[0]


def draw_slot_index(key, part):
    return route_table(key)[1]


def set_ends(values, key, low, high):
    dims = values.shape
    index_at = [jax.random.randint(jax.random.fold_in(key, axis), (), 0, dims[axis]) for axis in range(len(dims))]
    values = values.at[tuple(index_at)].set(low)
    longest = dims.index(max(dims))
    index_at[longest] = (index_at[longest] + 1) % dims[longest]
    return values.at[tuple(index_at)].set(high)


def levels(stream_key, extent, shards, low, largest):
    def one(axis_at, shards_of):
        heights = jax.random.uniform(jax.random.fold_in(jax.random.fold_in(stream_key, 6), axis_at), (shards_of,), jnp.float32, low / len(shards), largest / len(shards))
        return jnp.repeat(jnp.exp(heights), extent[axis_at] // shards_of).reshape((-1,) + (1,) * (len(extent) - axis_at - 1))

    level = one(*shards[0])
    for cut in shards[1:]:
        level = level * one(*cut)
    return level


def centred(key, shape, scale, reach, pieces=(), kind=jnp.bfloat16):
    values = scale * jax.random.normal(key, shape, jnp.float32)
    if pieces:
        values = values * levels(key, shape, pieces, -0.22, 0.18)
    return jnp.clip(values, -reach, reach).astype(kind)


def setup_inputs(seed: int = 0) -> dict:
    arg_keys = jax.random.split(jax.random.key(seed), 15)
    return {
        "inputs": centred(arg_keys[0], (GROUPS, TOK, D), 1.0, 6.0, ((0, 4), (1, 8))),
        "gain_one": jnp.clip(1.0 + 0.1 * jax.random.normal(arg_keys[1], (D,), jnp.float32), 0.5, 1.5),
        "w_query": centred(arg_keys[2], (D, D), D ** -0.5, 0.21875),
        "w_key": centred(arg_keys[3], (D, D), D ** -0.5, 0.21875),
        "w_value": centred(arg_keys[4], (D, D), D ** -0.5, 0.21875),
        "w_out_proj": centred(arg_keys[5], (D, D), (D // 32) ** -0.5, 1.25),
        "gain_two": jnp.clip(1.0 + 0.1 * jax.random.normal(arg_keys[6], (D,), jnp.float32), 0.5, 1.5),
        "w_router": centred(arg_keys[7], (D, SPECIALIST_COUNT), 0.025, 0.14941406),
        "w_in": centred(arg_keys[8], (SPECIALIST_COUNT, D, FF), D ** -0.5, 0.21875, ((0, 8),)),
        "w_out": centred(arg_keys[9], (SPECIALIST_COUNT, FF, D), FF ** -0.5, 0.109375, ((0, 8),)),
        "routes": draw_routes(jax.random.fold_in(arg_keys[14], 71), 0),
        "slot_index": draw_slot_index(jax.random.fold_in(arg_keys[14], 71), 0),
        "prompt_of": set_ends(jax.random.randint(arg_keys[12], (GROUPS, NCONT), 0, NPR), jax.random.fold_in(arg_keys[12], 1), 0, NPR - 1).astype(jnp.int32),
        "cotangent": centred(arg_keys[13], (GROUPS, TOK, D), 1.0, 6.0, ((0, 4), (1, 8))),
    }


HIGHEST = lax.Precision.HIGHEST
NEGATIVE = -1e+30

@jax.custom_vjp
def low(v):
    return lax.optimization_barrier(v.astype(jnp.bfloat16)).astype(jnp.float32)

@jax.custom_vjp
def low_back(v):
    return v

def low_keep(v):
    return (low(v), None)

def low_pass(kept, grad):
    return (grad,)

def back_keep(v):
    return (v, None)

def back_low(kept, grad):
    return (low(grad),)
low.defvjp(low_keep, low_pass)
low_back.defvjp(back_keep, back_low)

def normed(values):
    return values * lax.rsqrt(lax.optimization_barrier(jnp.mean(values * values, axis=-1, keepdims=True)) + 1e-06)

def attend_group(queries, keyset, valueset, prompt_ids):
    score_scale = HD ** (-0.5)
    prompt_rows = NPR * PR_DEV

    def divide_rows(field):
        shaped = field.reshape(N_EXPERT, ROWS_DEV, D)
        return (shaped[:, :prompt_rows].reshape(PLEN, NPR, H, HD), shaped[:, prompt_rows:].reshape(N_EXPERT, CLEN, H, HD))
    query_p, query_c = divide_rows(queries)
    key_p, key_c = divide_rows(keyset)
    value_p, value_c = divide_rows(valueset)
    query_block = min(512, PLEN)
    blocks = PLEN // query_block
    positions = jnp.arange(PLEN)

    def prompt_block(packed):
        block_q, block_pos = packed
        affinity_table = low_back(jnp.einsum('qbhd,kbhd->bhqk', block_q, key_p, precision=HIGHEST) * score_scale)
        visible = positions[None, None, None, :] <= block_pos[None, None, :, None]
        probability = jax.nn.softmax(jnp.where(visible, affinity_table, NEGATIVE), axis=-1)
        return jnp.einsum('bhqk,kbhd->qbhd', low(probability), value_p, precision=HIGHEST)
    out_p = lax.map(jax.checkpoint(prompt_block), (query_p.reshape(blocks, query_block, NPR, H, HD), positions.reshape(blocks, query_block)))
    causal = jnp.arange(CLEN)[None, :] <= jnp.arange(CLEN)[:, None]
    visible_c = jnp.concatenate([jnp.ones((CLEN, PLEN), dtype=jnp.bool_), causal], axis=1)

    def cont_block(packed):
        own_query, own_key, own_value, chosen_prompt = packed
        keys_all = jnp.concatenate([jnp.take(key_p, chosen_prompt, axis=1), own_key], axis=0)
        values_all = jnp.concatenate([jnp.take(value_p, chosen_prompt, axis=1), own_value], axis=0)
        affinity_table = low_back(jnp.einsum('qhd,khd->hqk', own_query, keys_all, precision=HIGHEST) * score_scale)
        probability = jax.nn.softmax(jnp.where(visible_c[None], affinity_table, NEGATIVE), axis=-1)
        return jnp.einsum('hqk,khd->qhd', low(probability), values_all, precision=HIGHEST)
    out_c = lax.map(jax.checkpoint(cont_block), (query_c, key_c, value_c, prompt_ids))
    merged = jnp.concatenate([out_p.reshape(N_EXPERT, prompt_rows, D), out_c.reshape(N_EXPERT, CLEN, D)], axis=1)
    return merged.reshape(TOK, D)

def forward(inputs, gain_one, w_query, w_key, w_value, w_out_proj, gain_two, w_router, w_in, w_out, routes, slot_index, prompt_of):

    def attention_group(packed):
        tokens, prompt_ids = packed
        hidden = low(normed(tokens) * gain_one)
        queries = low_back(low(jnp.dot(hidden, w_query, precision=HIGHEST)))
        keyset = low_back(low(jnp.dot(hidden, w_key, precision=HIGHEST)))
        valueset = low_back(low(jnp.dot(hidden, w_value, precision=HIGHEST)))
        attended = low_back(low(attend_group(queries, keyset, valueset, prompt_ids)))
        return tokens + low_back(jnp.dot(attended, w_out_proj, precision=HIGHEST))
    middle = lax.map(jax.checkpoint(attention_group), (inputs, prompt_of))
    second = low(normed(middle) * gain_two)
    logits = low_back(jnp.einsum('gtd,de->gte', second, w_router, precision=HIGHEST))
    gates = jax.nn.softmax(jnp.take_along_axis(logits, routes, axis=-1), axis=-1)
    kept = (slot_index < CAP).astype(jnp.float32)
    per_expert = GROUPS * N_EXPERT * CAP
    source = jnp.arange(TOK) // ROWS_DEV
    group_ids = jnp.arange(GROUPS)
    target = routes * per_expert + (group_ids[:, None, None] * N_EXPERT + source[None, :, None]) * CAP + slot_index
    target = jnp.where(slot_index < CAP, target, SPECIALIST_COUNT * per_expert).astype(jnp.int32)
    paired = jnp.broadcast_to(second[:, :, None, :], (GROUPS, TOK, TOP, D)).reshape(-1, D)
    scattered = jnp.zeros((SPECIALIST_COUNT * per_expert, D), jnp.float32).at[target.reshape(-1)].set(paired, mode='drop')
    expert_in = low_back(scattered).reshape(SPECIALIST_COUNT, per_expert, D)

    def expert_ffn(packed):
        rows_in, weight_in, weight_out = packed
        pre_act = low_back(jnp.dot(rows_in, weight_in, precision=HIGHEST))
        activated = low(jax.nn.gelu(pre_act))
        return low_back(low(jnp.dot(activated, weight_out, precision=HIGHEST)))
    expert_out = lax.map(jax.checkpoint(expert_ffn), (expert_in, w_in, w_out)).reshape(SPECIALIST_COUNT * per_expert, D)
    fetched = jnp.take(expert_out, jnp.minimum(target, SPECIALIST_COUNT * per_expert - 1).astype(jnp.int32), axis=0)
    mixture = lax.optimization_barrier(jnp.sum((gates * kept)[..., None] * fetched, axis=2))
    return middle + mixture

def reference(inputs, gain_one, w_query, w_key, w_value, w_out_proj, gain_two, w_router, w_in, w_out, routes, slot_index, prompt_of, cotangent):
    floats = (inputs.astype(jnp.float32), gain_one.astype(jnp.float32), w_query.astype(jnp.float32), w_key.astype(jnp.float32), w_value.astype(jnp.float32), w_out_proj.astype(jnp.float32), gain_two.astype(jnp.float32), w_router.astype(jnp.float32), w_in.astype(jnp.float32), w_out.astype(jnp.float32))

    def wrapped(*params):
        return forward(*params, routes, slot_index, prompt_of)
    result, pullback = jax.vjp(wrapped, *floats)
    grads = pullback(cotangent.astype(jnp.float32))
    return (result.astype(jnp.bfloat16), grads[0], grads[1], grads[2], grads[3], grads[4], grads[5], grads[6], grads[7], grads[8], grads[9])
```

```python
import functools

import jax
import jax.numpy as jnp
from jax import lax
from jax.experimental import pallas as pl
from jax.experimental.pallas import tpu as pltpu
from jax.sharding import PartitionSpec as P

H = 12
HD = 64
TOP = 2
NPR = 2
CLEN = 128
PR_DEV = 128
PAIR = 2 * HD
TWO = 2 * PR_DEV

NEGATIVE = -1e30
BF = jnp.bfloat16
F32 = jnp.float32
SCALE = HD ** (-0.5)

NN = ((1,), (0,))
NT = ((1,), (1,))
TN = ((0,), (0,))


def dot(a, b, dims=NN, out=F32):
    return lax.dot_general(a, b, (dims, ((), ())), preferred_element_type=out)


def iota(shape, dim):
    return lax.broadcasted_iota(jnp.int32, shape, dim)


def fill_bias(bias_ref, device, blocks):
    for m in range(blocks):
        offset = (jnp.bitwise_xor(device, m) - device) * PR_DEV
        seen = iota((PR_DEV, PR_DEV), 0) + offset <= iota((PR_DEV, PR_DEV), 1)
        bias_ref[m * PR_DEV : (m + 1) * PR_DEV, :] = jnp.where(seen, 0.0, NEGATIVE)


def two_heads(rows):
    keep = (iota((TWO, PAIR), 0) < PR_DEV) == (iota((TWO, PAIR), 1) < HD)
    return jnp.where(keep, jnp.concatenate([rows, rows], axis=0), jnp.zeros((), rows.dtype))


def join_heads(both):
    first = iota((PAIR, PR_DEV), 0) < HD
    return jnp.where(first, both[:, :PR_DEV], both[:, PR_DEV:]).T


def twice(block):
    return jnp.concatenate([block, block], axis=1)


def attention_forward_kernel(info, q_ref, k_ref, v_ref, kc_ref, vc_ref, o_ref, lse_ref, bias_ref):
    blocks = k_ref.shape[0]
    keys = blocks * PR_DEV
    device, chosen = info[0], info[1]

    @pl.when(pl.program_id(0) == 0)
    def _():
        fill_bias(bias_ref, device, blocks)

    for group in range(3):
        rows = slice(group * PR_DEV, (group + 1) * PR_DEV)
        q2 = two_heads(q_ref[rows, :] * jnp.asarray(SCALE, BF))
        which = group if group < NPR else chosen
        k = k_ref[:, which].reshape(keys, PAIR)
        v = v_ref[:, which].reshape(keys, PAIR)
        st = dot(k, q2, NT)
        if group < NPR:
            st = st + twice(bias_ref[...])
            top = jnp.max(st, axis=0, keepdims=True)
            p = jnp.exp(st - top)
            total = jnp.sum(p, axis=0, keepdims=True)
            both = dot(v, p.astype(BF), TN)
        else:
            own = dot(kc_ref[...], q2, NT) + twice(bias_ref[:PR_DEV, :])
            top = jnp.maximum(
                jnp.max(st, axis=0, keepdims=True), jnp.max(own, axis=0, keepdims=True)
            )
            p = jnp.exp(st - top)
            p_own = jnp.exp(own - top)
            total = jnp.sum(p, axis=0, keepdims=True) + jnp.sum(p_own, axis=0, keepdims=True)
            both = dot(v, p.astype(BF), TN) + dot(vc_ref[...], p_own.astype(BF), TN)
        both = both * (1.0 / total)
        o_ref[rows, :] = join_heads(both).astype(BF)
        lse_ref[0, group : group + 1, :] = top + jnp.log(total)


def attention_backward_kernel(
    info, q_ref, k_ref, v_ref, kc_ref, vc_ref, do_ref, lse_ref,
    dq_ref, dk_ref, dv_ref, dkc_ref, dvc_ref, bias_ref, dk_acc, dv_acc,
):
    blocks = k_ref.shape[0]
    keys = blocks * PR_DEV
    device, chosen = info[0], info[1]

    @pl.when(pl.program_id(0) == 0)
    def _():
        fill_bias(bias_ref, device, blocks)

    for group in range(3):
        rows = slice(group * PR_DEV, (group + 1) * PR_DEV)
        q2 = two_heads(q_ref[rows, :] * jnp.asarray(SCALE, BF))
        do2 = two_heads(do_ref[rows, :])
        lse = lse_ref[0, group : group + 1, :]
        which = group if group < NPR else chosen
        k = k_ref[:, which].reshape(keys, PAIR)
        v = v_ref[:, which].reshape(keys, PAIR)
        st = dot(k, q2, NT)
        if group < NPR:
            st = st + twice(bias_ref[...])
        p = jnp.exp(st - lse)
        dp = dot(v, do2, NT)
        delta = jnp.sum(p * dp, axis=0, keepdims=True)
        if group == NPR:
            kc, vc = kc_ref[...], vc_ref[...]
            p_own = jnp.exp(dot(kc, q2, NT) + twice(bias_ref[:PR_DEV, :]) - lse)
            dp_own = dot(vc, do2, NT)
            delta = delta + jnp.sum(p_own * dp_own, axis=0, keepdims=True)
        ds = (p * (dp - delta)).astype(BF)
        dk = dot(ds, q2)
        dv = dot(p.astype(BF), do2)
        dq = dot(k, ds, TN)
        if group < NPR:
            dk_acc[:, group] = dk.reshape(blocks, PR_DEV, PAIR)
            dv_acc[:, group] = dv.reshape(blocks, PR_DEV, PAIR)
        else:
            ds_own = (p_own * (dp_own - delta)).astype(BF)
            dq = dq + dot(kc, ds_own, TN)
            dkc_ref[...] = dot(ds_own, q2).astype(BF)
            dvc_ref[...] = dot(p_own.astype(BF), do2).astype(BF)
            dk_acc[:, chosen] += dk.reshape(blocks, PR_DEV, PAIR)
            dv_acc[:, chosen] += dv.reshape(blocks, PR_DEV, PAIR)
        dq_ref[rows, :] = (join_heads(dq) * SCALE).astype(BF)
    dk_ref[...] = dk_acc[...].astype(BF)
    dv_ref[...] = dv_acc[...].astype(BF)


def attention_specs(blocks, rows):
    q_spec = pl.BlockSpec((rows, PAIR), lambda h, info: (0, h))
    k_spec = pl.BlockSpec((blocks, NPR, PR_DEV, PAIR), lambda h, info: (0, 0, 0, h))
    c_spec = pl.BlockSpec((CLEN, PAIR), lambda h, info: (0, h))
    l_spec = pl.BlockSpec((1, 3, TWO), lambda h, info: (h, 0, 0))
    return q_spec, k_spec, c_spec, l_spec


def attention_forward(info, q, k, v, kc, vc):
    blocks, rows, pairs = k.shape[0], q.shape[0], q.shape[1] // PAIR
    q_spec, k_spec, c_spec, l_spec = attention_specs(blocks, rows)
    flops = pairs * 3 * 4 * TWO * blocks * PR_DEV * PAIR
    return pl.pallas_call(
        attention_forward_kernel,
        grid_spec=pltpu.PrefetchScalarGridSpec(
            num_scalar_prefetch=1,
            grid=(pairs,),
            in_specs=[q_spec, k_spec, k_spec, c_spec, c_spec],
            out_specs=[q_spec, l_spec],
            scratch_shapes=[pltpu.VMEM((blocks * PR_DEV, PR_DEV), F32)],
        ),
        out_shape=[
            jax.ShapeDtypeStruct(q.shape, BF),
            jax.ShapeDtypeStruct((pairs, 3, TWO), F32),
        ],
        compiler_params=pltpu.CompilerParams(vmem_limit_bytes=56 * 1024 * 1024),
        cost_estimate=pl.CostEstimate(flops=4 * flops, bytes_accessed=2 * k.size * 2, transcendentals=0),
        name="attention_forward",
    )(info, q, k, v, kc, vc)


def attention_backward(info, q, k, v, kc, vc, do, lse):
    blocks, rows, pairs = k.shape[0], q.shape[0], q.shape[1] // PAIR
    q_spec, k_spec, c_spec, l_spec = attention_specs(blocks, rows)
    flops = pairs * 3 * 10 * TWO * blocks * PR_DEV * PAIR
    return pl.pallas_call(
        attention_backward_kernel,
        grid_spec=pltpu.PrefetchScalarGridSpec(
            num_scalar_prefetch=1,
            grid=(pairs,),
            in_specs=[q_spec, k_spec, k_spec, c_spec, c_spec, q_spec, l_spec],
            out_specs=[q_spec, k_spec, k_spec, c_spec, c_spec],
            scratch_shapes=[
                pltpu.VMEM((blocks * PR_DEV, PR_DEV), F32),
                pltpu.VMEM((blocks, NPR, PR_DEV, PAIR), F32),
                pltpu.VMEM((blocks, NPR, PR_DEV, PAIR), F32),
            ],
        ),
        out_shape=[
            jax.ShapeDtypeStruct(q.shape, BF),
            jax.ShapeDtypeStruct(k.shape, BF),
            jax.ShapeDtypeStruct(k.shape, BF),
            jax.ShapeDtypeStruct(kc.shape, BF),
            jax.ShapeDtypeStruct(kc.shape, BF),
        ],
        compiler_params=pltpu.CompilerParams(vmem_limit_bytes=60 * 1024 * 1024),
        cost_estimate=pl.CostEstimate(flops=4 * flops, bytes_accessed=4 * k.size * 2, transcendentals=0),
        name="attention_backward",
    )(info, q, k, v, kc, vc, do, lse)


def swap(value, axis, mask):
    size = lax.axis_size(axis)
    return lax.ppermute(value, axis, [(i, i ^ mask) for i in range(size)])


def gather_relative(own, axis):
    size = lax.axis_size(axis)
    chips = [own] + [swap(own, axis, mask) for mask in range(2, size, 2)]
    stacked = jnp.stack(chips)
    other = swap(stacked, axis, 1)
    return jnp.stack([stacked, other], axis=1).reshape((size,) + own.shape)


def scatter_relative(parts, axis):
    size = lax.axis_size(axis)
    halves = parts.reshape((size // 2, 2) + parts.shape[1:])
    came = swap(halves[:, 1], axis, 1)
    summed = (halves[:, 0].astype(F32) + came.astype(F32)).astype(BF)
    total = summed[0].astype(F32)
    for chip in range(1, size // 2):
        total = total + swap(summed[chip], axis, 2 * chip).astype(F32)
    return total


def at(value, index):
    return lax.dynamic_index_in_dim(value, index, 0, keepdims=False)


def all_reduce(rows):
    dp, size = lax.axis_size("dp"), lax.axis_size("expert")
    z, e = lax.axis_index("dp"), lax.axis_index("expert")
    chips = size // 2
    core, chip = lax.rem(e, 2), lax.div(e, 2)
    width = rows.shape[1]
    part = rows.shape[0] // (dp * size)
    value = rows.reshape(2, chips, dp, part, width)
    value = (at(value, core).astype(F32) + swap(at(value, 1 - core), "expert", 1).astype(F32)).astype(BF)
    total = at(value, chip).astype(F32)
    for m in range(1, chips):
        total = total + swap(at(value, jnp.bitwise_xor(chip, m)), "expert", 2 * m).astype(F32)
    value = total.astype(BF)
    total = at(value, z).astype(F32)
    for m in range(1, dp):
        total = total + swap(at(value, jnp.bitwise_xor(z, m)), "dp", m).astype(F32)
    own = total.astype(BF)

    def spread(own, axis, index, count, step):
        full = jnp.zeros((count,) + own.shape, own.dtype)
        full = lax.dynamic_update_index_in_dim(full, own, index, 0)
        for m in range(1, count):
            full = lax.dynamic_update_index_in_dim(
                full, swap(own, axis, m * step), jnp.bitwise_xor(index, m), 0
            )
        return full

    own = spread(own, "dp", z, dp, 1)
    own = spread(own, "expert", chip, chips, 2)
    own = spread(own, "expert", core, 2, 1)
    return own.reshape(rows.shape)


def to_experts(slots):
    return lax.all_to_all(slots, "expert", split_axis=0, concat_axis=0, tiled=True)


def gelu_parts(a):
    inner = 0.7978845608 * (a + 0.044715 * a * a * a)
    t = jnp.tanh(inner)
    value = 0.5 * a * (1.0 + t)
    slope = 0.5 * (1.0 + t) + 0.5 * a * (1.0 - t * t) * (
        0.7978845608 * (1.0 + 3.0 * 0.044715 * a * a)
    )
    return value, slope


def root(values):
    return lax.rsqrt(jnp.mean(values * values, axis=-1, keepdims=True) + 1e-06)


def norm_back(norm, scale, grad):
    return scale * (grad - norm * jnp.mean(grad * norm, axis=-1, keepdims=True))


def per_device(
    inputs,
    gain_one,
    w_query,
    w_key,
    w_value,
    w_out_proj,
    gain_two,
    w_router,
    w_in,
    w_out,
    routes,
    slot_index,
    prompt_of,
    cotangent,
):
    row_count, width = inputs.shape[1], inputs.shape[2]
    dp, devices = lax.axis_size("dp"), lax.axis_size("expert")
    z, device = lax.axis_index("dp"), lax.axis_index("expert")
    prompt_rows = NPR * PR_DEV
    expert_count, local = w_router.shape[1], w_in.shape[0]
    hidden_units = w_in.shape[2]
    capacity = max(2, 5 * row_count * TOP // (4 * expert_count))
    room = -(-capacity // 16) * 16
    slots = expert_count * room
    info = jnp.stack([device, prompt_of[0, 0]]).astype(jnp.int32)

    row = jnp.arange(row_count)
    source = jnp.where(row < prompt_rows, (row % PR_DEV) * NPR + row // PR_DEV, row)
    order = (source[:, None] == jnp.arange(row_count)[None, :]).astype(BF)
    tokens = dot(order, inputs[0])
    cot = dot(order, cotangent[0])
    cot_low = cot.astype(BF)
    table = jnp.concatenate([routes[0], slot_index[0]], axis=1).astype(BF)
    table_rows = dot(table, order, ((0,), (1,)))
    table_cols = dot(order, table)

    scale_one = root(tokens)
    norm_one = tokens * scale_one
    hidden = (norm_one * gain_one).astype(BF)
    hidden_all = gather_relative(hidden[:prompt_rows], "expert")
    hidden_all = hidden_all.reshape(devices * prompt_rows, width)
    key_all = dot(hidden_all, w_key).astype(BF).reshape(devices, NPR, PR_DEV, width)
    value_all = dot(hidden_all, w_value).astype(BF).reshape(devices, NPR, PR_DEV, width)
    queries = dot(hidden, w_query).astype(BF)
    hidden_c = hidden[prompt_rows:]
    key_c = dot(hidden_c, w_key).astype(BF)
    value_c = dot(hidden_c, w_value).astype(BF)
    attended, lse = attention_forward(info, queries, key_all, value_all, key_c, value_c)

    message = jnp.concatenate(
        [cot_low, jnp.pad(table_rows.astype(BF), ((0, 12), (0, width - row_count)))], axis=0
    )
    cots, tables = [cot_low], [table_rows]
    for m in range(1, dp):
        came = swap(message, "dp", m)
        cots.append(came[:row_count])
        tables.append(came[row_count : row_count + 4, :row_count].astype(F32))

    slot_no = jnp.arange(slots, dtype=F32)[:, None]

    def choices(rows):
        picks = []
        for k in range(TOP):
            target = jnp.where(rows[TOP + k] < capacity, rows[k] * room + rows[TOP + k], -1.0)
            picks.append((slot_no == target[None, :]).astype(BF))
        return picks

    picks = [choices(rows) for rows in tables]
    pick_any = [a + b for a, b in picks]
    others = jnp.stack(
        [
            jnp.sum(a.astype(F32) * rows[1][None, :] + b.astype(F32) * rows[0][None, :], axis=1)
            for (a, b), rows in zip(picks, tables)
        ]
    )
    others = others.reshape(dp, devices, local * room).transpose(1, 0, 2)
    others = to_experts(others).reshape(devices, dp, local, room)
    others = others.transpose(1, 2, 0, 3).reshape(dp, local, devices * room, 1)

    def dispatch(pick, values):
        outgoing = dot(pick, values, out=F32).astype(BF).reshape(devices, local * room, width)
        arrived = to_experts(outgoing).reshape(devices, local, room, width)
        return arrived.transpose(1, 0, 2, 3).reshape(local, devices * room, width)

    cot_slots = [dispatch(pick, values) for pick, values in zip(pick_any, cots)]

    middle = tokens + dot(attended, w_out_proj)
    scale_two = root(middle)
    norm_two = middle * scale_two
    second = (norm_two * gain_two).astype(BF)
    logits = dot(second, w_router)
    columns = jnp.arange(expert_count, dtype=F32)[None, :]
    chosen = [table_cols[:, k : k + 1] == columns for k in range(TOP)]
    chosen_logits = [jnp.sum(jnp.where(c, logits, 0.0), axis=1, keepdims=True) for c in chosen]
    gate0 = jax.nn.sigmoid(chosen_logits[0] - chosen_logits[1])
    gate1 = jax.nn.sigmoid(chosen_logits[1] - chosen_logits[0])

    def gate_of(rows_in, other, expert):
        own_logits = dot(rows_in, w_router)
        mine = jnp.sum(jnp.where(columns == expert, own_logits, 0.0), axis=1, keepdims=True)
        theirs = jnp.sum(jnp.where(columns == other, own_logits, 0.0), axis=1, keepdims=True)
        return jax.nn.sigmoid(mine - theirs)

    def weighted(rows_in, other, cot_rows):
        return jnp.stack(
            [
                (
                    gate_of(rows_in[l], other[l], (device * local + l).astype(F32))
                    * cot_rows[l].astype(F32)
                ).astype(BF)
                for l in range(local)
            ]
        )

    expert_in = dispatch(pick_any[0], second)
    grad_expert = weighted(expert_in, others[0], cot_slots[0])
    pre_act = jnp.einsum("erd,edf->erf", expert_in, w_in, preferred_element_type=F32)
    active, slope = gelu_parts(pre_act)
    expert_out = jnp.einsum(
        "erf,efd->erd", active.astype(BF), w_out, preferred_element_type=F32
    ).astype(BF)

    def back(rows_out):
        outgoing = rows_out.reshape(local, devices, room, width).transpose(1, 0, 2, 3)
        return to_experts(outgoing.reshape(devices, local * room, width)).reshape(slots, width)

    returned = back(expert_out)
    grad_act = jnp.einsum("erd,efd->erf", grad_expert, w_out, preferred_element_type=F32)
    grad_pre = (grad_act * slope).astype(BF)
    grad_in = jnp.einsum("erf,edf->erd", grad_pre, w_in, preferred_element_type=F32).astype(BF)
    grad_returned = back(grad_in)

    ins, grads = [expert_in], [grad_expert]
    for m in range(1, dp):
        rows_in = dispatch(pick_any[m], swap(second, "dp", m))
        ins.append(rows_in)
        grads.append(weighted(rows_in, others[m], cot_slots[m]))
    all_in = jnp.concatenate(ins, axis=1)
    all_grad = jnp.concatenate(grads, axis=1)
    part = hidden_units // dp
    w_in_part = lax.dynamic_slice_in_dim(w_in, z * part, part, 2)
    w_out_part = lax.dynamic_slice_in_dim(w_out, z * part, part, 1)
    pre_part = jnp.einsum("erd,edf->erf", all_in, w_in_part, preferred_element_type=F32)
    active_part, slope_part = gelu_parts(pre_part)
    grad_act_part = jnp.einsum("erd,efd->erf", all_grad, w_out_part, preferred_element_type=F32)
    grad_pre_part = (grad_act_part * slope_part).astype(BF)
    grad_w_in = jnp.einsum("erd,erf->edf", all_in, grad_pre_part, preferred_element_type=F32)
    grad_w_out = jnp.einsum(
        "erf,erd->efd", active_part.astype(BF), all_grad, preferred_element_type=F32
    )
    share = width // dp
    grad_w_in = grad_w_in.astype(BF).reshape(local, dp, share, part)
    grad_w_in = lax.all_to_all(
        grad_w_in.transpose(1, 0, 2, 3), "dp", split_axis=0, concat_axis=0, tiled=True
    )
    grad_w_in = grad_w_in.transpose(1, 2, 0, 3).reshape(local, share, hidden_units).astype(F32)

    fetched = [dot(pick, returned, TN) for pick in picks[0]]
    outputs = (middle + (gate0 * fetched[0] + gate1 * fetched[1])).astype(BF)
    outputs = dot(order, outputs, TN).astype(BF)
    grad_gate0 = jnp.sum(cot * fetched[0], axis=1, keepdims=True)
    grad_gate1 = jnp.sum(cot * fetched[1], axis=1, keepdims=True)
    mean_gate = gate0 * grad_gate0 + gate1 * grad_gate1
    grad_logits = (
        jnp.where(chosen[0], gate0 * (grad_gate0 - mean_gate), 0.0)
        + jnp.where(chosen[1], gate1 * (grad_gate1 - mean_gate), 0.0)
    ).astype(BF)
    grad_second = dot(pick_any[0], grad_returned, TN) + dot(grad_logits, w_router, NT)
    grad_router_t = dot(grad_logits, second, TN)
    grad_gain_two = jnp.sum(grad_second * norm_two, axis=0, keepdims=True)
    grad_middle = cot + norm_back(norm_two, scale_two, grad_second * gain_two)
    grad_attn = grad_middle.astype(BF)
    grad_out_proj = dot(attended, grad_attn, TN)
    grad_attended = dot(grad_attn, w_out_proj, NT).astype(BF)

    grad_q, part_k, part_v, grad_kc, grad_vc = attention_backward(
        info, queries, key_all, value_all, key_c, value_c, grad_attended, lse
    )
    part_k = part_k.reshape(devices * prompt_rows, width)
    part_v = part_v.reshape(devices * prompt_rows, width)
    grad_query = dot(hidden, grad_q, TN)
    grad_key = dot(hidden_all, part_k, TN) + dot(hidden_c, grad_kc, TN)
    grad_value = dot(hidden_all, part_v, TN) + dot(hidden_c, grad_vc, TN)
    part_hidden = (dot(part_k, w_key, NT) + dot(part_v, w_value, NT)).astype(BF)
    share_hidden = scatter_relative(part_hidden.reshape(devices, prompt_rows, width), "expert")
    grad_hidden = dot(grad_q, w_query, NT) + jnp.concatenate(
        [share_hidden, dot(grad_kc, w_key, NT) + dot(grad_vc, w_value, NT)], axis=0
    )
    grad_gain_one = jnp.sum(grad_hidden * norm_one, axis=0, keepdims=True)
    grad_input = grad_middle + norm_back(norm_one, scale_one, grad_hidden * gain_one)
    grad_input = jnp.concatenate(
        [
            grad_input[:prompt_rows]
            .reshape(NPR, PR_DEV, width)
            .transpose(1, 0, 2)
            .reshape(prompt_rows, width),
            grad_input[prompt_rows:],
        ],
        axis=0,
    )

    unit = 16 * dp * devices

    def summed(pieces):
        rows = jnp.concatenate(pieces, axis=0).astype(BF)
        count = rows.shape[0]
        rows = jnp.pad(rows, ((0, -count % unit), (0, 0)))
        return all_reduce(rows).astype(F32)

    first = summed([grad_out_proj, grad_router_t, grad_gain_two])
    last = summed([grad_query, grad_key, grad_value, grad_gain_one])
    return (
        outputs[None],
        grad_input[None],
        last[3 * width],
        last[:width],
        last[width : 2 * width],
        last[2 * width : 3 * width],
        first[:width],
        first[width + expert_count],
        first[width : width + expert_count].T,
        grad_w_in,
        grad_w_out,
    )


def solution(mesh):
    return jax.shard_map(
        per_device,
        mesh=mesh,
        in_specs=(
            P("dp", "expert", None),
            P(),
            P(),
            P(),
            P(),
            P(),
            P(),
            P(),
            P("expert", None, None),
            P("expert", None, None),
            P("dp", "expert", None),
            P("dp", "expert", None),
            P("dp", "expert"),
            P("dp", "expert", None),
        ),
        out_specs=(
            P("dp", "expert", None),
            P("dp", "expert", None),
            P(),
            P(),
            P(),
            P(),
            P(),
            P(),
            P(),
            P("expert", "dp", None),
            P("expert", "dp", None),
        ),
        check_vma=False,
    )
```

```python
import jax
import jax.numpy as jnp
from jax import lax
from jax.experimental import pallas as pl
from jax.experimental.pallas import tpu as pltpu
from jax.sharding import PartitionSpec as P

H = 12
HD = 64
TOP = 2
NPR = 2
CLEN = 128
PR_DEV = 128
PAIR = 2 * HD
TWO = 2 * PR_DEV

NEGATIVE = -1e30
BF = jnp.bfloat16
F32 = jnp.float32
SCALE = HD ** (-0.5)
MIB = 1024 * 1024

NN = ((1,), (0,))
NT = ((1,), (1,))
TN = ((0,), (0,))

HIGH, LOW, ROUTE = 0, 2, 4
TABLE = 16


def dot(a, b, dims=NN):
    return lax.dot_general(a, b, (dims, ((), ())), preferred_element_type=F32)


def iota(shape, dim):
    return lax.broadcasted_iota(jnp.int32, shape, dim)


def shape_of(shape, dtype):
    return jax.ShapeDtypeStruct(shape, dtype)


WEIGHT = 1.0
TIMES = {
    "norm": 2.7,
    "table": 4.5,
    "attention_forward": 15.0,
    "middle": 5.1,
    "dispatch_cot": 7.0,
    "expert_forward": 20.0,
    "expert_backward": 20.0,
    "dispatch": 6.5,
    "expert_weights": 9.0,
    "combine": 9.6,
    "attention_backward": 15.0,
    "sum_cores": 4.0,
    "halves": 3.1,
    "expert_weights_last": 30.0,
    "sum_chips": 2.6,
    "sum_groups": 1.8,
    "input": 1.0,
    "spread_sums": 9.0,
    "columns": 4.1,
}


def cost(name):
    flops = int(TIMES[name] * WEIGHT * 1.1e9)
    return pl.CostEstimate(flops=flops, bytes_accessed=0, transcendentals=0)


def run(kernel, name, info, operands, outs, deps=(), scratch=()):
    n_in, n_dep, n_out = len(operands), len(deps), len(outs)

    def body(info_ref, *refs):
        ins = refs[:n_in]
        results = refs[n_in + n_dep : n_in + n_dep + n_out]
        kernel(info_ref, ins, results, refs[n_in + n_dep + n_out :])

    vmem = pl.BlockSpec(memory_space=pltpu.VMEM)
    return pl.pallas_call(
        body,
        in_specs=[pl.BlockSpec(memory_space=pltpu.SMEM)]
        + [vmem] * n_in
        + [pl.BlockSpec(memory_space=pl.ANY)] * n_dep,
        out_specs=[vmem] * n_out,
        out_shape=list(outs),
        scratch_shapes=list(scratch),
        compiler_params=pltpu.CompilerParams(vmem_limit_bytes=56 * MIB),
        cost_estimate=cost(name),
        name=name,
    )(info, *operands, *deps)


def fill_bias(bias_ref, device, chips):
    for b in range(2 * chips):
        mask = 2 * (b % chips) + b // chips
        offset = (jnp.bitwise_xor(device, mask) - device) * PR_DEV
        seen = iota((PR_DEV, PR_DEV), 0) + offset <= iota((PR_DEV, PR_DEV), 1)
        bias_ref[b * PR_DEV : (b + 1) * PR_DEV, :] = jnp.where(seen, 0.0, NEGATIVE)


def two_heads(rows):
    keep = (iota((TWO, PAIR), 0) < PR_DEV) == (iota((TWO, PAIR), 1) < HD)
    return jnp.where(keep, jnp.concatenate([rows, rows], axis=0), jnp.zeros((), rows.dtype))


def join_heads(both):
    first = iota((PAIR, PR_DEV), 0) < HD
    return jnp.where(first, both[:, :PR_DEV], both[:, PR_DEV:]).T


def twice(block):
    return jnp.concatenate([block, block], axis=1)


def top_of(parts):
    top = jnp.max(parts[0], axis=0, keepdims=True)
    for part in parts[1:]:
        top = jnp.maximum(top, jnp.max(part, axis=0, keepdims=True))
    return top


def sum_of(parts):
    total = jnp.sum(parts[0], axis=0, keepdims=True)
    for part in parts[1:]:
        total = total + jnp.sum(part, axis=0, keepdims=True)
    return total


def added(parts):
    total = parts[0]
    for part in parts[1:]:
        total = total + part
    return total


def scores_of(keys, q2, bias_ref, group, span):
    parts = []
    for i, k in enumerate(keys):
        st = dot(k, q2, NT)
        if group < NPR:
            st = st + twice(bias_ref[i * span : (i + 1) * span, :])
        elif i == 2:
            st = st + twice(bias_ref[:PR_DEV, :])
        parts.append(st)
    return parts


def attention_forward_kernel(
    info, q_ref, ka_ref, kb_ref, va_ref, vb_ref, kc_ref, vc_ref, o_ref, lse_ref, bias_ref
):
    chips = ka_ref.shape[0]
    span = chips * PR_DEV
    device, chosen = info[0], info[1]

    @pl.when(pl.program_id(0) == 0)
    def _():
        fill_bias(bias_ref, device, chips)

    for group in range(3):
        rows = slice(group * PR_DEV, (group + 1) * PR_DEV)
        q2 = two_heads(q_ref[rows, :] * jnp.asarray(SCALE, BF))
        which = group if group < NPR else chosen
        keys = [ref[:, which].reshape(span, PAIR) for ref in (ka_ref, kb_ref)]
        values = [ref[:, which].reshape(span, PAIR) for ref in (va_ref, vb_ref)]
        if group == NPR:
            keys.append(kc_ref[...])
            values.append(vc_ref[...])
        scores = scores_of(keys, q2, bias_ref, group, span)
        top = top_of(scores)
        probs = [jnp.exp(st - top) for st in scores]
        total = sum_of(probs)
        both = added([dot(v, p.astype(BF), TN) for v, p in zip(values, probs)])
        both = both * (1.0 / total)
        o_ref[rows, :] = join_heads(both).astype(BF)
        lse_ref[0, group : group + 1, :] = top + jnp.log(total)


def attention_backward_kernel(
    info, q_ref, ka_ref, kb_ref, va_ref, vb_ref, kc_ref, vc_ref, do_ref, lse_ref,
    dq_ref, dka_ref, dkb_ref, dva_ref, dvb_ref, dkc_ref, dvc_ref, bias_ref, dk_acc, dv_acc,
):
    chips = ka_ref.shape[0]
    span = chips * PR_DEV
    device, chosen = info[0], info[1]

    @pl.when(pl.program_id(0) == 0)
    def _():
        fill_bias(bias_ref, device, chips)

    for group in range(3):
        rows = slice(group * PR_DEV, (group + 1) * PR_DEV)
        q2 = two_heads(q_ref[rows, :] * jnp.asarray(SCALE, BF))
        do2 = two_heads(do_ref[rows, :])
        lse = lse_ref[0, group : group + 1, :]
        which = group if group < NPR else chosen
        keys = [ref[:, which].reshape(span, PAIR) for ref in (ka_ref, kb_ref)]
        values = [ref[:, which].reshape(span, PAIR) for ref in (va_ref, vb_ref)]
        if group == NPR:
            keys.append(kc_ref[...])
            values.append(vc_ref[...])
        probs = [jnp.exp(st - lse) for st in scores_of(keys, q2, bias_ref, group, span)]
        grads = [dot(v, do2, NT) for v in values]
        delta = sum_of([p * g for p, g in zip(probs, grads)])
        ds = [(p * (g - delta)).astype(BF) for p, g in zip(probs, grads)]
        dq = added([dot(k, d, TN) for k, d in zip(keys, ds)])
        dq_ref[rows, :] = (join_heads(dq) * SCALE).astype(BF)
        for i in range(2):
            dk = dot(ds[i], q2).reshape(chips, PR_DEV, PAIR)
            dv = dot(probs[i].astype(BF), do2).reshape(chips, PR_DEV, PAIR)
            at = slice(i * chips, (i + 1) * chips)
            if group < NPR:
                dk_acc[at, group] = dk
                dv_acc[at, group] = dv
            else:
                dk_acc[at, chosen] += dk
                dv_acc[at, chosen] += dv
        if group == NPR:
            dkc_ref[...] = dot(ds[2], q2).astype(BF)
            dvc_ref[...] = dot(probs[2].astype(BF), do2).astype(BF)
    dka_ref[...] = dk_acc[:chips].astype(BF)
    dkb_ref[...] = dk_acc[chips:].astype(BF)
    dva_ref[...] = dv_acc[:chips].astype(BF)
    dvb_ref[...] = dv_acc[chips:].astype(BF)


def attention_specs(chips, rows, first=0):
    q_spec = pl.BlockSpec((rows, PAIR), lambda h, info: (0, first + h))
    k_spec = pl.BlockSpec((chips, NPR, PR_DEV, PAIR), lambda h, info: (0, 0, 0, first + h))
    c_spec = pl.BlockSpec((CLEN, PAIR), lambda h, info: (0, first + h))
    l_spec = pl.BlockSpec((1, 3, TWO), lambda h, info: (first + h, 0, 0))
    return q_spec, k_spec, c_spec, l_spec


def drop_refs(kernel, n_in, n_dep):
    def body(info, *refs):
        kernel(info, *refs[:n_in], *refs[n_in + n_dep :])

    return body


def attention_forward(info, q, keys, values, kc, vc, deps=()):
    k = keys[0]
    chips, rows, pairs = k.shape[0], q.shape[0], q.shape[1] // PAIR
    q_spec, k_spec, c_spec, l_spec = attention_specs(chips, rows)
    return pl.pallas_call(
        drop_refs(attention_forward_kernel, 7, len(deps)),
        grid_spec=pltpu.PrefetchScalarGridSpec(
            num_scalar_prefetch=1,
            grid=(pairs,),
            in_specs=[q_spec] + [k_spec] * 4 + [c_spec, c_spec]
            + [pl.BlockSpec(memory_space=pl.ANY)] * len(deps),
            out_specs=[q_spec, l_spec],
            scratch_shapes=[pltpu.VMEM((2 * chips * PR_DEV, PR_DEV), F32)],
        ),
        out_shape=[shape_of(q.shape, BF), shape_of((pairs, 3, TWO), F32)],
        compiler_params=pltpu.CompilerParams(vmem_limit_bytes=56 * MIB),
        cost_estimate=cost("attention_forward"),
        name="attention_forward",
    )(info, q, *keys, *values, kc, vc, *deps)


def attention_backward(info, q, keys, values, kc, vc, do, lse, first, pairs, before=(), deps=()):
    k = keys[0]
    chips, rows = k.shape[0], q.shape[0]
    q_spec, k_spec, c_spec, l_spec = attention_specs(chips, rows, first)
    deps = list(before) + list(deps)
    return pl.pallas_call(
        drop_refs(attention_backward_kernel, 9, len(deps)),
        grid_spec=pltpu.PrefetchScalarGridSpec(
            num_scalar_prefetch=1,
            grid=(pairs,),
            in_specs=[q_spec] + [k_spec] * 4 + [c_spec, c_spec, q_spec, l_spec]
            + [pl.BlockSpec(memory_space=pl.ANY)] * len(deps),
            out_specs=[q_spec] + [k_spec] * 4 + [c_spec, c_spec],
            scratch_shapes=[
                pltpu.VMEM((2 * chips * PR_DEV, PR_DEV), F32),
                pltpu.VMEM((2 * chips, NPR, PR_DEV, PAIR), F32),
                pltpu.VMEM((2 * chips, NPR, PR_DEV, PAIR), F32),
            ],
        ),
        out_shape=[shape_of(q.shape, BF)]
        + [shape_of(k.shape, BF)] * 4
        + [shape_of(kc.shape, BF)] * 2,
        input_output_aliases={10 + i: i for i in range(len(before))},
        compiler_params=pltpu.CompilerParams(vmem_limit_bytes=60 * MIB),
        cost_estimate=cost("attention_backward"),
        name="attention_backward",
    )(info, q, *keys, *values, kc, vc, do, lse, *deps)


def swap(value, axis, mask):
    size = lax.axis_size(axis)
    return lax.ppermute(value, axis, [(i, i ^ mask) for i in range(size)])


def far_groups(own, dp):
    return [swap(own, "dp", m) for m in range(2, dp, 2)]


def with_neighbours(far):
    return [tokens for even in far for tokens in (even, swap(even, "dp", 1))]


def exchange(blocks):
    return lax.all_to_all(blocks, "expert", split_axis=0, concat_axis=0, tiled=True)


def root(values):
    return lax.rsqrt(jnp.mean(values * values, axis=-1, keepdims=True) + 1e-06)


def norm_back(norm, scale, grad):
    return scale * (grad - norm * jnp.mean(grad * norm, axis=-1, keepdims=True))


def source_row(row):
    inner = jnp.bitwise_and(row, PR_DEV - 1) * NPR + lax.shift_right_logical(row, 7)
    return jnp.where(row < NPR * PR_DEV, inner, row)


def order_matrix(n):
    return (source_row(iota((n, n), 0)) == iota((n, n), 1)).astype(BF)


def order_matrix_t(n):
    return (source_row(iota((n, n), 1)) == iota((n, n), 0)).astype(BF)


def norm_kernel(info, ins, outs, scratch):
    x, gain = ins
    prompt, hidden_ref, ordered = outs
    tokens = dot(order_matrix(x.shape[0]), x[...])
    hidden = (tokens * root(tokens) * gain[...]).astype(BF)
    prompt[...] = hidden[: NPR * PR_DEV]
    hidden_ref[...] = hidden
    ordered[...] = tokens.astype(BF)


def target(rows, k):
    return (rows[HIGH + k : HIGH + k + 1] * 16.0 + rows[LOW + k : LOW + k + 1]).astype(jnp.int32)


def picks_of(rows, slots):
    at = iota((slots, rows.shape[1]), 0)
    return [at == target(rows, k) for k in range(TOP)]


def low(mask):
    return jnp.where(mask, 1.0, 0.0).astype(BF)


def other_routes(rows, picks):
    low_rows = rows[:8].astype(BF)
    first = dot(low_rows, low(picks[0]), NT)[ROUTE + 1 : ROUTE + 2]
    return first + dot(low_rows, low(picks[1]), NT)[ROUTE : ROUTE + 1]


def send_slots(out, sent, per, at=0):
    for m in range(out.shape[0]):
        out[m, at : at + per, :] = sent[m * per : (m + 1) * per]


def clear_others(out):
    for m in range(out.shape[0]):
        out[m, out.shape[1] - TABLE :, :] = jnp.zeros((TABLE, out.shape[2]), BF)


def send_others(out, others, per, at=0):
    row = out.shape[1] - TABLE
    for m in range(out.shape[0]):
        out[m, row:, at : at + per] = jnp.broadcast_to(
            others[:, m * per : (m + 1) * per], (TABLE, per)
        ).astype(BF)


def table_kernel(per, room, capacity):
    def kernel(info, ins, outs, scratch):
        cot, route, slot = ins
        message, cols, out = outs
        n, width = cot.shape
        order = order_matrix(n)
        ordered = dot(order, cot[...]).astype(BF)
        r, s = route[...], slot[...]
        where = jnp.where(s < capacity, r * room + s, -16)
        high = lax.shift_right_arithmetic(where, 4).astype(F32)
        rest = jnp.bitwise_and(where, 15).astype(F32)
        r = r.astype(F32)
        lane = iota((n, 128), 1)
        table = jnp.zeros((n, 128), F32)
        for first, values in ((HIGH, high), (LOW, rest), (ROUTE, r)):
            for k in range(TOP):
                table = jnp.where(lane == first + k, values[:, k : k + 1], table)
        table = dot(order, table.astype(BF))
        cols[...] = table
        rows = table.T[:TABLE]
        message[:n, :] = ordered
        message[n:, :] = jnp.zeros((TABLE, width), BF)
        message[n:, :n] = rows.astype(BF)
        picks = picks_of(rows, per * out.shape[0])
        send_slots(out, dot(low(jnp.logical_or(*picks)), ordered).astype(BF), per)
        clear_others(out)
        send_others(out, other_routes(rows, picks), per)

    return kernel


def table_rows(message):
    n = message.shape[0] - TABLE
    return message[n:, :n].astype(F32)


def dispatch_cot_kernel(per):
    def kernel(info, ins, outs, scratch):
        out, = outs
        n = ins[0].shape[0] - TABLE
        clear_others(out)
        for g, message in enumerate(ins):
            rows = table_rows(message)
            picks = picks_of(rows, per * out.shape[0])
            sent = dot(low(jnp.logical_or(*picks)), message[:n, :]).astype(BF)
            send_slots(out, sent, per, g * per)
            send_others(out, other_routes(rows, picks), per, g * per)

    return kernel


def dispatch_kernel(per):
    def kernel(info, ins, outs, scratch):
        out, = outs
        groups = len(ins) // 2
        for g in range(groups):
            picks = picks_of(table_rows(ins[g]), per * out.shape[0])
            sent = dot(low(jnp.logical_or(*picks)), ins[groups + g][...]).astype(BF)
            send_slots(out, sent, per, g * per)

    return kernel


def middle_kernel(per):
    def kernel(info, ins, outs, scratch):
        ordered, attended, w_out_proj, gain, w_router, cols, message = ins
        middle_ref, second_ref, gates_ref, out = outs
        middle = ordered[...].astype(F32) + dot(attended[...], w_out_proj[...])
        middle_ref[...] = middle
        second = (middle * root(middle) * gain[...]).astype(BF)
        second_ref[...] = second
        picks = picks_of(table_rows(message), per * out.shape[0])
        send_slots(out, dot(low(jnp.logical_or(*picks)), second).astype(BF), per)
        logits = dot(second, w_router[...])
        column = iota(logits.shape, 1).astype(F32)
        chosen = [
            jnp.sum(
                jnp.where(column == cols[:, ROUTE + k : ROUTE + k + 1], logits, 0.0),
                axis=1,
                keepdims=True,
            )
            for k in range(TOP)
        ]
        lane = iota(gates_ref.shape, 1)
        first = 1.0 / (1.0 + jnp.exp(chosen[1] - chosen[0]))
        then = 1.0 / (1.0 + jnp.exp(chosen[0] - chosen[1]))
        gates_ref[...] = jnp.where(lane == 0, first, then)

    return kernel


def combine_kernel():
    def kernel(info, ins, outs, scratch):
        middle_ref, second_ref, gates, cols, message, attended, w_out_proj, w_router, gain = ins[:9]
        came, came_grad = ins[9:]
        out_ref, grad_middle_ref, grad_attended_ref, grad_proj_ref, few_ref = outs
        n, width = middle_ref.shape
        slots = came.shape[0] * came.shape[1]
        middle, second = middle_ref[...], second_ref[...]
        cot = message[:n, :].astype(F32)
        table = cols[...]
        at = iota((n, slots), 1)
        picks = []
        for k in range(TOP):
            where = table[:, HIGH + k : HIGH + k + 1] * 16.0 + table[:, LOW + k : LOW + k + 1]
            picks.append(at == where.astype(jnp.int32))
        returned = came[...].reshape(slots, width)
        fetched = [dot(low(pick), returned) for pick in picks]
        gate = [gates[:, k : k + 1] for k in range(TOP)]
        outputs = (middle + (gate[0] * fetched[0] + gate[1] * fetched[1])).astype(BF)
        out_ref[...] = dot(order_matrix_t(n), outputs).astype(BF)
        grad_gate = [jnp.sum(cot * f, axis=1, keepdims=True) for f in fetched]
        mean_gate = gate[0] * grad_gate[0] + gate[1] * grad_gate[1]
        experts = w_router.shape[1]
        column = iota((n, experts), 1).astype(F32)
        grad_logits = jnp.zeros((n, experts), F32)
        for k in range(TOP):
            grad_logits = jnp.where(
                column == table[:, ROUTE + k : ROUTE + k + 1],
                gate[k] * (grad_gate[k] - mean_gate),
                grad_logits,
            )
        grad_logits = grad_logits.astype(BF)
        grad_second = dot(
            low(jnp.logical_or(*picks)), came_grad[...].reshape(slots, width)
        ) + dot(
            grad_logits, w_router[...], NT
        )
        scale = root(middle)
        norm = middle * scale
        few_ref[:experts, :] = dot(grad_logits, second, TN).astype(BF)
        few_ref[experts:, :] = jnp.broadcast_to(
            jnp.sum(grad_second * norm, axis=0, keepdims=True), (16, width)
        ).astype(BF)
        grad_middle = cot + norm_back(norm, scale, grad_second * gain[...])
        grad_middle_ref[...] = grad_middle
        grad_attn = grad_middle.astype(BF)
        grad_attended_ref[...] = dot(grad_attn, w_out_proj[...], NT).astype(BF)
        grad_proj_ref[...] = dot(attended[...], grad_attn, TN).astype(BF)

    return kernel


def input_kernel(info, ins, outs, scratch):
    grad_q, grad_kc, grad_vc, w_query, w_key, w_value, ordered, gain, grad_middle = ins[:9]
    parts = ins[9:]
    out, = outs
    shares = parts[0][...].astype(F32)
    for part in parts[1:]:
        shares = shares + part[...].astype(F32)
    grad_hidden = dot(grad_q[...], w_query[...], NT) + jnp.concatenate(
        [shares, dot(grad_kc[...], w_key[...], NT) + dot(grad_vc[...], w_value[...], NT)], axis=0
    )
    tokens = ordered[...].astype(F32)
    scale = root(tokens)
    grad = grad_middle[...] + norm_back(tokens * scale, scale, grad_hidden * gain[...])
    back = order_matrix_t(grad.shape[0])
    high = grad.astype(BF)
    rest = grad - high.astype(F32)
    mid = rest.astype(BF)
    last = (rest - mid.astype(F32)).astype(BF)
    out[...] = (dot(back, high) + dot(back, mid)) + dot(back, last)


def halves_kernel(info, ins, outs, scratch):
    kept, came = ins
    for m, out in enumerate(outs):
        out[...] = (kept[m].astype(F32) + came[m].astype(F32)).astype(BF)


def gelu_parts(a):
    square = a * a
    t = jnp.tanh(a * (0.7978845608 + (0.7978845608 * 0.044715) * square))
    half = 0.5 * a
    value = half + half * t
    slope = (0.5 + 0.5 * t) + half * (1.0 - t * t) * (
        0.7978845608 + (0.7978845608 * 3.0 * 0.044715) * square
    )
    return value, slope


def gather_rows(into, blocks, first, room):
    for m in range(blocks.shape[0]):
        into[m * room : (m + 1) * room, :] = blocks[m, pl.ds(pl.multiple_of(first, 16), room), :]


def other_column(others, blocks, first, room):
    at = blocks.shape[1] - TABLE
    span = min(blocks.shape[2], -(-at // 128) * 128)
    eye = iota((room, span), 1) == iota((room, span), 0) + first
    for m in range(blocks.shape[0]):
        row = blocks[m, at : at + TABLE, :span][:1].astype(F32)
        column = jnp.sum(jnp.where(eye, row, 0.0), axis=1, keepdims=True)
        others[m * room : (m + 1) * room, :] = jnp.broadcast_to(column, (room, 128))


def gated(rows, cots, others, w_router, mine):
    logits = dot(rows, w_router)
    column = iota(logits.shape, 1)
    own = jnp.sum(jnp.where(column == mine, logits, 0.0), axis=1, keepdims=True)
    other = others[:, : logits.shape[1]].astype(jnp.int32)
    theirs = jnp.sum(jnp.where(column == other, logits, 0.0), axis=1, keepdims=True)
    gate = 1.0 / (1.0 + jnp.exp(theirs - own))
    return (gate * cots.astype(F32)).astype(BF)


def expert_forward(x_slots, w_in, w_out, room, deps=()):
    devices, per, _ = x_slots.shape
    local, width, units = w_in.shape
    rows = devices * room
    chunk = min(units, 768)
    steps = units // chunk

    def kernel(x_ref, w_in_ref, w_out_ref, *refs):
        slope_ref, out, x, total = refs[len(deps) :]
        l, f = pl.program_id(0), pl.program_id(1)

        @pl.when(f == 0)
        def _():
            gather_rows(x, x_ref, l * room, room)
            total[...] = jnp.zeros_like(total)

        value, slope = gelu_parts(dot(x[...], w_in_ref[0]))
        slope_ref[0] = slope.astype(BF)
        total[...] += dot(value.astype(BF), w_out_ref[0])

        @pl.when(f == steps - 1)
        def _():
            for m in range(devices):
                out[m, pl.ds(pl.multiple_of(l * room, 16), room), :] = total[
                    m * room : (m + 1) * room, :
                ].astype(BF)

    slots = pl.BlockSpec(x_slots.shape, lambda l, f: (0, 0, 0))
    return pl.pallas_call(
        kernel,
        grid=(local, steps),
        in_specs=[
            slots,
            pl.BlockSpec((1, width, chunk), lambda l, f: (l, 0, f)),
            pl.BlockSpec((1, chunk, width), lambda l, f: (l, f, 0)),
        ]
        + [pl.BlockSpec(memory_space=pl.ANY)] * len(deps),
        out_specs=[pl.BlockSpec((1, rows, chunk), lambda l, f: (l, 0, f)), slots],
        out_shape=[shape_of((local, rows, units), BF), shape_of(x_slots.shape, BF)],
        scratch_shapes=[pltpu.VMEM((rows, width), BF), pltpu.VMEM((rows, width), F32)],
        compiler_params=pltpu.CompilerParams(vmem_limit_bytes=56 * MIB),
        cost_estimate=cost("expert_forward"),
        name="expert_forward",
    )(x_slots, w_in, w_out, *deps)


def expert_backward(info, x_slots, c_slots, slope, w_router, w_in, w_out, room, deps=()):
    devices, per, _ = x_slots.shape
    local, width, units = w_in.shape
    rows = devices * room
    chunk = min(units, 768)
    steps = units // chunk

    def kernel(info_ref, x_ref, c_ref, router_ref, slope_ref, w_in_ref, w_out_ref, *refs):
        out, x, grad, others, total = refs[len(deps) :]
        l, f = pl.program_id(0), pl.program_id(1)

        @pl.when(f == 0)
        def _():
            gather_rows(x, x_ref, l * room, room)
            gather_rows(grad, c_ref, l * room, room)
            other_column(others, c_ref, l * room, room)
            grad[...] = gated(
                x[...], grad[...], others[...], router_ref[...], info_ref[0] * local + l
            )
            total[...] = jnp.zeros_like(total)

        grad_act = dot(grad[...], w_out_ref[0], NT)
        grad_pre = (grad_act * slope_ref[0].astype(F32)).astype(BF)
        total[...] += dot(grad_pre, w_in_ref[0], NT)

        @pl.when(f == steps - 1)
        def _():
            for m in range(devices):
                out[m, pl.ds(pl.multiple_of(l * room, 16), room), :] = total[
                    m * room : (m + 1) * room, :
                ].astype(BF)

    slots = pl.BlockSpec(x_slots.shape, lambda l, f, info: (0, 0, 0))
    return pl.pallas_call(
        kernel,
        grid_spec=pltpu.PrefetchScalarGridSpec(
            num_scalar_prefetch=1,
            grid=(local, steps),
            in_specs=[
                slots,
                pl.BlockSpec(c_slots.shape, lambda l, f, info: (0, 0, 0)),
                pl.BlockSpec(w_router.shape, lambda l, f, info: (0, 0)),
                pl.BlockSpec((1, rows, chunk), lambda l, f, info: (l, 0, f)),
                pl.BlockSpec((1, width, chunk), lambda l, f, info: (l, 0, f)),
                pl.BlockSpec((1, chunk, width), lambda l, f, info: (l, f, 0)),
            ]
            + [pl.BlockSpec(memory_space=pl.ANY)] * len(deps),
            out_specs=slots,
            scratch_shapes=[
                pltpu.VMEM((rows, width), BF),
                pltpu.VMEM((rows, width), BF),
                pltpu.VMEM((rows, 128), F32),
                pltpu.VMEM((rows, width), F32),
            ],
        ),
        out_shape=shape_of(x_slots.shape, BF),
        compiler_params=pltpu.CompilerParams(vmem_limit_bytes=56 * MIB),
        cost_estimate=cost("expert_backward"),
        name="expert_backward",
    )(info, x_slots, c_slots, w_router, slope, w_in, w_out, *deps)


def expert_weights(info, groups, w_router, w_in, w_out, room, dp, before=None, last=False, deps=()):
    devices = groups[0][0].shape[0]
    local, width, units = w_in.shape
    part, share = units // dp, width // dp
    per = local * room
    rows = devices * room
    flat = [array for pair in groups for array in pair]
    places = [
        (2 * i, base) for i, (x, _) in enumerate(groups) for base in range(0, x.shape[1], per)
    ]
    n_flat = len(flat)
    sums = [] if before is None else list(before)

    def kernel(info_ref, *refs):
        slots = refs[:n_flat]
        router_ref, w_in_ref, w_out_ref = refs[n_flat : n_flat + 3]
        refs = refs[n_flat + 3 :]
        earlier = refs[: len(sums)]
        refs = refs[len(sums) + len(deps) :]
        out_ref, in_refs = refs[0], refs[1:-4]
        x, grad, others, total = refs[-4:]
        l = pl.program_id(0)
        for g, (place, base) in enumerate(places):
            gather_rows(x, slots[place], base + l * room, room)
            gather_rows(grad, slots[place + 1], base + l * room, room)
            other_column(others, slots[place + 1], base + l * room, room)
            grad[...] = gated(
                x[...], grad[...], others[...], router_ref[...], info_ref[0] * local + l
            )
            value, slope = gelu_parts(dot(x[...], w_in_ref[0]))
            grad_act = dot(grad[...], w_out_ref[0], NT)
            grad_pre = (grad_act * slope).astype(BF)
            part_in = dot(x[...], grad_pre, TN)
            part_out = dot(value.astype(BF), grad[...], TN)
            if g > 0:
                total[...] += part_in
                out_ref[0] += part_out
            elif earlier:
                total[...] = earlier[1][0] + part_in
                out_ref[0] = earlier[0][0] + part_out
            else:
                total[...] = part_in
                out_ref[0] = part_out
        if last:
            for k in range(dp):
                in_refs[0][k, 0] = total[k * share : (k + 1) * share, :].astype(BF)
        else:
            in_refs[0][0] = total[...]

    def const(shape):
        return pl.BlockSpec(shape, lambda l, info: (0,) * len(shape), pipeline_mode=pl.Buffered(1))

    square = pl.BlockSpec((1, part, width), lambda l, info: (l, 0, 0))
    square_in = pl.BlockSpec((1, width, part), lambda l, info: (l, 0, 0))
    if last:
        in_specs = [pl.BlockSpec((dp, 1, share, part), lambda l, info: (0, l, 0, 0))]
        in_shapes = [shape_of((dp, local, share, part), BF)]
    else:
        in_specs = [square_in]
        in_shapes = [shape_of((local, width, part), F32)]
    got = pl.pallas_call(
        kernel,
        grid_spec=pltpu.PrefetchScalarGridSpec(
            num_scalar_prefetch=1,
            grid=(local,),
            in_specs=[const(x.shape) for x in flat]
            + [
                const(w_router.shape),
                pl.BlockSpec((1, width, part), lambda l, info: (l, 0, info[2])),
                pl.BlockSpec((1, part, width), lambda l, info: (l, info[2], 0)),
            ]
            + [square, square_in][: len(sums)]
            + [pl.BlockSpec(memory_space=pl.ANY)] * len(deps),
            out_specs=[square] + in_specs,
            scratch_shapes=[
                pltpu.VMEM((rows, width), BF),
                pltpu.VMEM((rows, width), BF),
                pltpu.VMEM((rows, 128), F32),
                pltpu.VMEM((width, part), F32),
            ],
        ),
        out_shape=[shape_of((local, part, width), F32)] + in_shapes,
        compiler_params=pltpu.CompilerParams(vmem_limit_bytes=60 * MIB),
        cost_estimate=cost("expert_weights_last" if last else "expert_weights"),
        name="expert_weights_last" if last else "expert_weights",
    )(info, *flat, w_router, w_in, w_out, *sums, *deps)
    return got[0], got[1:]


def columns_kernel(info, ins, outs, scratch):
    out, = outs
    pieces, = ins
    part = pieces.shape[3]
    for k in range(pieces.shape[0]):
        out[:, :, k * part : (k + 1) * part] = pieces[k].astype(F32)


class Sums:
    def __init__(self, info, mats, few, dp, devices):
        self.info, self.n, self.dp, self.devices = info, len(mats), dp, devices
        self.rows, self.width = mats[0].shape
        self.chips = devices // 2
        self.half, self.tall = self.width // 2, self.rows // self.chips
        self.short = self.tall // dp
        self.extra = few.shape[0] if few is not None else 0
        self.value = jnp.concatenate(list(mats) + ([few] if self.extra else []), axis=0)
        core = lax.rem(lax.axis_index("expert"), 2)
        self.came = swap(
            lax.dynamic_slice_in_dim(self.value, (1 - core) * self.half, self.half, 1), "expert", 1
        )

    @staticmethod
    def fits(rows, width, dp, devices):
        short = rows // (devices // 2) // dp
        return short % 16 == 0 and width % 256 == 0 and short * dp * (devices // 2) == rows

    def cores(self, deps=()):
        n, rows, tall, half, extra = self.n, self.rows, self.tall, self.half, self.extra

        def kernel(info_ref, ins, outs, scratch):
            kept, got = ins
            lanes = pl.ds(pl.multiple_of(info_ref[3] * half, 128), half)
            for m, out in enumerate(outs):
                for i in range(n):
                    start = i * rows + jnp.bitwise_xor(info_ref[4], m) * tall
                    at = pl.ds(pl.multiple_of(start, 16), tall)
                    out[i * tall : (i + 1) * tall, :] = (
                        kept[at, lanes].astype(F32) + got[at, :].astype(F32)
                    ).astype(BF)
                if extra:
                    out[n * tall :, :] = (
                        kept[n * rows :, lanes].astype(F32) + got[n * rows :, :].astype(F32)
                    ).astype(BF)

        pieces = run(
            kernel, "sum_cores", self.info, [self.value, self.came],
            [shape_of((n * tall + extra, half), BF)] * self.chips, deps=deps,
        )
        self.pieces = [pieces[0]] + [
            swap(pieces[m], "expert", 2 * m) for m in range(1, self.chips)
        ]
        return pieces[0]

    def planes(self, deps=()):
        n, tall, short, half, extra = self.n, self.tall, self.short, self.half, self.extra

        def kernel(info_ref, ins, outs, scratch):
            total, = scratch
            total[...] = added([piece[...].astype(F32) for piece in ins]).astype(BF)
            for k, out in enumerate(outs):
                for i in range(n):
                    start = i * tall + jnp.bitwise_xor(info_ref[2], k) * short
                    out[i * short : (i + 1) * short, :] = total[
                        pl.ds(pl.multiple_of(start, 16), short), :
                    ]
                if extra:
                    out[n * short :, :] = total[n * tall :, :]

        pieces = run(
            kernel, "sum_chips", self.info, self.pieces,
            [shape_of((n * short + extra, half), BF)] * self.dp,
            scratch=[pltpu.VMEM((n * tall + extra, half), BF)], deps=deps,
        )
        self.pieces = [pieces[0]] + [swap(pieces[k], "dp", k) for k in range(1, self.dp)]
        return pieces[0]

    def groups(self, deps=()):
        n, short, half, extra = self.n, self.short, self.half, self.extra

        def kernel(info_ref, ins, outs, scratch):
            value = added([piece[...].astype(F32) for piece in ins]).astype(BF)
            outs[0][...] = value[: n * short]
            if extra:
                outs[1][...] = value[n * short :]

        got = run(
            kernel, "sum_groups", self.info, self.pieces,
            [shape_of((n * short, half), BF)] + ([shape_of((extra, half), BF)] if extra else []),
            deps=deps,
        )
        self.few = list(got[1:])
        self.own = [got[0]] + [swap(got[0], "dp", k) for k in range(1, self.dp)]
        return got[0]

    def gather(self):
        spread = jnp.concatenate(self.own, axis=0)
        self.spread = jnp.concatenate(
            [spread] + [swap(spread, "expert", 2 * m) for m in range(1, self.chips)] + self.few, axis=0
        )
        self.other = swap(self.spread, "expert", 1)

    def finish(self, columns, gain, weights, deps=()):
        n, short, tall, half, extra = self.n, self.short, self.tall, self.half, self.extra
        chips, dp, rows = self.chips, self.dp, self.rows

        def kernel(info_ref, ins, outs, scratch):
            for c, ref in enumerate(ins[:2]):
                lanes = pl.ds(pl.multiple_of(jnp.bitwise_xor(info_ref[3], c) * half, 128), half)
                for m in range(chips):
                    for k in range(dp):
                        start = jnp.bitwise_xor(info_ref[4], m) * tall
                        start = start + jnp.bitwise_xor(info_ref[2], k) * short
                        at = pl.ds(pl.multiple_of(start, 16), short)
                        for i in range(n):
                            place = ((m * dp + k) * n + i) * short
                            outs[i][at, lanes] = ref[place : place + short, :].astype(F32)
                scratch[0][:, lanes] = ref[chips * dp * n * short :, :].astype(F32)
            outs[n][...] = scratch[0][:columns, :].T
            outs[n + 1][...] = scratch[0][columns : columns + 1, :]
            outs[n + 2][...] = gained(zip(ins[3:], outs), ins[2][...])

        row = shape_of((1, self.width), F32)
        return run(
            kernel, "spread_sums", self.info, [self.spread, self.other, gain] + list(weights),
            [shape_of((rows, self.width), F32)] * n + [shape_of((self.width, columns), F32), row, row],
            scratch=[pltpu.VMEM((extra, self.width), F32)], deps=deps,
        )


def gained(pairs, gain):
    total = 0.0
    for weight, grad in pairs:
        total = total + jnp.sum(weight[...].astype(F32) * grad[...], axis=1, keepdims=True)
    return jnp.broadcast_to(total, (total.shape[0], 128)).T[:1] / gain


def per_device(
    inputs,
    gain_one,
    w_query,
    w_key,
    w_value,
    w_out_proj,
    gain_two,
    w_router,
    w_in,
    w_out,
    routes,
    slot_index,
    prompt_of,
    cotangent,
):
    row_count, width = inputs.shape[1], inputs.shape[2]
    dp, devices = lax.axis_size("dp"), lax.axis_size("expert")
    z, device = lax.axis_index("dp"), lax.axis_index("expert")
    chips = devices // 2
    prompt_rows = NPR * PR_DEV
    expert_count, local = w_router.shape[1], w_in.shape[0]
    capacity = max(2, 5 * row_count * TOP // (4 * expert_count))
    room = -(-capacity // 16) * 16
    per = local * room
    info = jnp.stack(
        [device, prompt_of[0, 0], z, lax.rem(device, 2), lax.div(device, 2)]
    ).astype(jnp.int32)
    gain_one = gain_one[None, :]
    gain_two = gain_two[None, :]
    wide = shape_of((row_count, width), BF)
    wide32 = shape_of((row_count, width), F32)
    narrow = shape_of((row_count, 128), F32)
    x_shape = shape_of((devices, per, width), BF)
    c_shape = shape_of((devices, per + TABLE, width), BF)

    hidden_p, hidden, ordered = run(
        norm_kernel, "norm", info, [inputs[0], gain_one],
        [shape_of((prompt_rows, width), BF), wide, wide],
    )
    near = [hidden_p] + [swap(hidden_p, "expert", 2 * m) for m in range(1, chips)]

    message, cols, c_sent = run(
        table_kernel(per, room, capacity), "table", info,
        [cotangent[0], routes[0], slot_index[0]],
        [shape_of((row_count + TABLE, width), BF), narrow, c_shape],
        deps=[hidden_p],
    )
    near, message = lax.optimization_barrier((near, message))
    near = jnp.concatenate(near, axis=0)
    far = swap(near, "expert", 1)
    messages = far_groups(message, dp)
    c_sent, near = lax.optimization_barrier((c_sent, near))
    c_slots = [exchange(c_sent)]

    queries = dot(hidden, w_query).astype(BF)
    hidden_c = hidden[prompt_rows:]
    key_c = dot(hidden_c, w_key).astype(BF)
    value_c = dot(hidden_c, w_value).astype(BF)

    def heads(rows, weight):
        return dot(rows, weight).astype(BF).reshape(chips, NPR, PR_DEV, width)

    keys = [heads(near, w_key), heads(far, w_key)]
    values = [heads(near, w_value), heads(far, w_value)]
    attended, lse = attention_forward(info, queries, keys, values, key_c, value_c)
    c_slots, messages, attended = lax.optimization_barrier((c_slots, messages, attended))
    messages = with_neighbours(messages)
    c_odd = [swap(c_slots[0], "dp", 1)]

    middle, second, gates, x_sent = run(
        middle_kernel(per), "middle", info,
        [ordered, attended, w_out_proj, gain_two, w_router, cols, message],
        [wide32, wide, narrow, x_shape],
    )
    x_slots = [exchange(x_sent)]
    seconds = far_groups(second, dp)
    c_rest = run(
        dispatch_cot_kernel(per), "dispatch_cot", info, messages,
        [shape_of((devices, (dp - 2) * per + TABLE, width), BF)], deps=[middle],
    )
    x_slots, c_rest = lax.optimization_barrier((x_slots, c_rest))
    c_slots = c_slots + [exchange(sent) for sent in c_rest]
    x_odd = [swap(x_slots[0], "dp", 1)]

    slope, out_sent = expert_forward(x_slots[0], w_in, w_out, room)
    seconds, slope = lax.optimization_barrier((seconds, slope))
    seconds = with_neighbours(seconds)
    returned = exchange(out_sent)
    grad_sent = expert_backward(
        info, x_slots[0], c_slots[0], slope, w_router, w_in, w_out, room, deps=c_slots[1:]
    )
    returned, grad_sent = lax.optimization_barrier((returned, grad_sent))
    grad_returned = exchange(grad_sent)

    sums = expert_weights(
        info, [(x_slots[0], c_slots[0])], w_router, w_in, w_out, room, dp,
        deps=[grad_sent],
    )
    x_rest = run(
        dispatch_kernel(per), "dispatch", info, messages + seconds,
        [shape_of((devices, (dp - 2) * per, width), BF)], deps=[sums[0]],
    )

    outputs, grad_middle, grad_attended, grad_proj, few = run(
        combine_kernel(), "combine", info,
        [middle, second, gates, cols, message, attended, w_out_proj, w_router, gain_two]
        + [returned, grad_returned],
        [wide, wide32, wide, shape_of((width, width), BF), shape_of((expert_count + 16, width), BF)],
        deps=x_rest,
    )
    x_slots = x_slots + [exchange(sent) for sent in x_rest]

    pairs = width // PAIR

    def back(first, count, before=(), deps=()):
        return attention_backward(
            info, queries, keys, values, key_c, value_c, grad_attended, lse, first, count,
            before=before, deps=deps,
        )

    got = back(0, pairs, deps=c_odd + x_odd)
    grad_q, dk_near, dk_far, dv_near, dv_far, grad_kc, grad_vc = got
    grad_q, dk_near, dk_far, dv_near, dv_far, x_slots[1] = lax.optimization_barrier(
        (grad_q, dk_near, dk_far, dv_near, dv_far, x_slots[1])
    )
    dk_near, dk_far, dv_near, dv_far = [
        part.reshape(chips * prompt_rows, width) for part in (dk_near, dk_far, dv_near, dv_far)
    ]
    grad_query = dot(hidden, grad_q, TN).astype(BF)
    grad_key = (dot(near, dk_near, TN) + dot(far, dk_far, TN) + dot(hidden_c, grad_kc, TN)).astype(BF)
    grad_value = (dot(near, dv_near, TN) + dot(far, dv_far, TN) + dot(hidden_c, grad_vc, TN)).astype(BF)
    dense = [grad_query, grad_key, grad_value, grad_proj]
    stepwise = Sums.fits(width, width, dp, devices)
    if stepwise:
        total = Sums(info, dense, few, dp, devices)

    sent = (dot(dk_far, w_key, NT) + dot(dv_far, w_value, NT)).astype(BF)
    kept = (dot(dk_near, w_key, NT) + dot(dv_near, w_value, NT)).astype(BF)
    came = swap(sent.reshape(chips, prompt_rows, width), "expert", 1)
    after = total.cores([kept]) if stepwise else kept
    shares = run(
        halves_kernel, "halves", info, [kept.reshape(chips, prompt_rows, width), came],
        [shape_of((prompt_rows, width), BF)] * chips, deps=[after],
    )

    grad_w_out, in_pieces = expert_weights(
        info, [(x_odd[0], c_odd[0]), (x_slots[1], c_slots[1])], w_router, w_in, w_out, room, dp,
        before=(sums[0], sums[1][0]), last=True, deps=[shares[0]],
    )
    shares, in_pieces, grad_w_out = lax.optimization_barrier((shares, in_pieces, grad_w_out))
    shares = [shares[0]] + [swap(shares[m], "expert", 2 * m) for m in range(1, chips)]
    after = [grad_w_out]
    if stepwise:
        after = [total.planes(after)]
        after = [total.groups(after + shares)]
        total.own[0], in_pieces = lax.optimization_barrier((total.own[0], in_pieces))
    grad_input, = run(
        input_kernel, "input", info,
        [grad_q, grad_kc, grad_vc, w_query, w_key, w_value, ordered, gain_one, grad_middle] + shares,
        [wide32], deps=after,
    )
    if stepwise:
        total.own, grad_input = lax.optimization_barrier((total.own, grad_input))
        total.gather()
    in_pieces = lax.all_to_all(in_pieces[0], "dp", split_axis=0, concat_axis=0, tiled=True)
    after = []
    if stepwise:
        query_sum, key_sum, value_sum, proj_sum, grad_router, grad_gain_two, grad_gain_one = (
            total.finish(expert_count, gain_one, [w_query, w_key, w_value])
        )
        after = [query_sum]
    else:
        query_sum, key_sum, value_sum, proj_sum, few = lax.psum(
            [part.astype(F32) for part in dense + [few]], ("dp", "expert")
        )
        grad_router, grad_gain_two = few[:expert_count].T, few[expert_count :][:1]
        grad_gain_one = gained(
            [(w_query, query_sum), (w_key, key_sum), (w_value, value_sum)], gain_one
        )
    grad_w_in, = run(
        columns_kernel, "columns", info, [in_pieces],
        [shape_of((local, width // dp, w_in.shape[2]), F32)], deps=after,
    )
    return (
        outputs[None],
        grad_input[None],
        grad_gain_one[0],
        query_sum,
        key_sum,
        value_sum,
        proj_sum,
        grad_gain_two[0],
        grad_router,
        grad_w_in,
        grad_w_out,
    )


def solution(mesh):
    return jax.shard_map(
        per_device,
        mesh=mesh,
        in_specs=(
            P("dp", "expert", None),
            P(),
            P(),
            P(),
            P(),
            P(),
            P(),
            P(),
            P("expert", None, None),
            P("expert", None, None),
            P("dp", "expert", None),
            P("dp", "expert", None),
            P("dp", "expert"),
            P("dp", "expert", None),
        ),
        out_specs=(
            P("dp", "expert", None),
            P("dp", "expert", None),
            P(),
            P(),
            P(),
            P(),
            P(),
            P(),
            P(),
            P("expert", "dp", None),
            P("expert", "dp", None),
        ),
        check_vma=False,
    )
```

```python
import jax
import jax.numpy as jnp
from jax import lax
from jax.experimental import pallas as pl
from jax.experimental.pallas import tpu as pltpu
from jax.sharding import PartitionSpec as P

H = 12
HD = 64
TOP = 2
NPR = 2
CLEN = 128
PR_DEV = 128
PAIR = 2 * HD
TWO = 2 * PR_DEV

NEGATIVE = -1e30
BF = jnp.bfloat16
F32 = jnp.float32
SCALE = HD ** (-0.5)
MIB = 1024 * 1024

NN = ((1,), (0,))
NT = ((1,), (1,))
TN = ((0,), (0,))

HIGH, LOW, ROUTE = 0, 2, 4
TABLE = 16


def dot(a, b, dims=NN):
    return lax.dot_general(a, b, (dims, ((), ())), preferred_element_type=F32)


def iota(shape, dim):
    return lax.broadcasted_iota(jnp.int32, shape, dim)


def shape_of(shape, dtype):
    return jax.ShapeDtypeStruct(shape, dtype)


WEIGHT = 1.0
TIMES = {
    "norm": 2.7,
    "table": 4.5,
    "attention_forward": 15.0,
    "middle": 5.1,
    "dispatch_cot": 7.0,
    "expert_forward": 20.0,
    "expert_backward": 20.0,
    "dispatch": 30.0,
    "expert_weights": 1.0,
    "combine": 3.0,
    "attention_backward": 15.0,
    "sum_cores": 0.3,
    "halves": 0.3,
    "expert_weights_last": 30.0,
    "sum_chips": 2.6,
    "sum_groups": 1.8,
    "input": 1.0,
    "spread_sums": 1.0,
    "columns": 1.0,
    "join": 2.0,
    "keys_and_values": 3.5,
    "dense_gradients": 60.0,
}


def cost(name):
    flops = int(TIMES[name] * WEIGHT * 1.1e9)
    return pl.CostEstimate(flops=flops, bytes_accessed=0, transcendentals=0)


def run(kernel, name, info, operands, outs, deps=(), scratch=()):
    n_in, n_dep, n_out = len(operands), len(deps), len(outs)

    def body(info_ref, *refs):
        ins = refs[:n_in]
        results = refs[n_in + n_dep : n_in + n_dep + n_out]
        kernel(info_ref, ins, results, refs[n_in + n_dep + n_out :])

    vmem = pl.BlockSpec(memory_space=pltpu.VMEM)
    return pl.pallas_call(
        body,
        in_specs=[pl.BlockSpec(memory_space=pltpu.SMEM)]
        + [vmem] * n_in
        + [pl.BlockSpec(memory_space=pl.ANY)] * n_dep,
        out_specs=[vmem] * n_out,
        out_shape=list(outs),
        scratch_shapes=list(scratch),
        compiler_params=pltpu.CompilerParams(vmem_limit_bytes=56 * MIB),
        cost_estimate=cost(name),
        name=name,
    )(info, *operands, *deps)


def fill_bias(bias_ref, device, chips):
    for b in range(2 * chips):
        mask = 2 * (b % chips) + b // chips
        offset = (jnp.bitwise_xor(device, mask) - device) * PR_DEV
        seen = iota((PR_DEV, PR_DEV), 0) + offset <= iota((PR_DEV, PR_DEV), 1)
        bias_ref[b * PR_DEV : (b + 1) * PR_DEV, :] = jnp.where(seen, 0.0, NEGATIVE)


def two_heads(rows):
    keep = (iota((TWO, PAIR), 0) < PR_DEV) == (iota((TWO, PAIR), 1) < HD)
    return jnp.where(keep, jnp.concatenate([rows, rows], axis=0), jnp.zeros((), rows.dtype))


def join_heads(both):
    first = iota((PAIR, PR_DEV), 0) < HD
    return jnp.where(first, both[:, :PR_DEV], both[:, PR_DEV:]).T


def twice(block):
    return jnp.concatenate([block, block], axis=1)


def top_of(parts):
    top = jnp.max(parts[0], axis=0, keepdims=True)
    for part in parts[1:]:
        top = jnp.maximum(top, jnp.max(part, axis=0, keepdims=True))
    return top


def sum_of(parts):
    total = jnp.sum(parts[0], axis=0, keepdims=True)
    for part in parts[1:]:
        total = total + jnp.sum(part, axis=0, keepdims=True)
    return total


def added(parts):
    total = parts[0]
    for part in parts[1:]:
        total = total + part
    return total


def scores_of(keys, q2, bias_ref, group, span):
    parts = []
    for i, k in enumerate(keys):
        st = dot(k, q2, NT)
        if group < NPR:
            st = st + twice(bias_ref[i * span : (i + 1) * span, :])
        elif i == 2:
            st = st + twice(bias_ref[:PR_DEV, :])
        parts.append(st)
    return parts


def attention_forward_kernel(
    info, q_ref, ka_ref, kb_ref, va_ref, vb_ref, kc_ref, vc_ref, o_ref, lse_ref, bias_ref
):
    chips = ka_ref.shape[0]
    span = chips * PR_DEV
    device, chosen = info[0], info[1]

    @pl.when(pl.program_id(0) == 0)
    def _():
        fill_bias(bias_ref, device, chips)

    for group in range(3):
        rows = slice(group * PR_DEV, (group + 1) * PR_DEV)
        q2 = two_heads(q_ref[rows, :] * jnp.asarray(SCALE, BF))
        which = group if group < NPR else chosen
        keys = [ref[:, which].reshape(span, PAIR) for ref in (ka_ref, kb_ref)]
        values = [ref[:, which].reshape(span, PAIR) for ref in (va_ref, vb_ref)]
        if group == NPR:
            keys.append(kc_ref[...])
            values.append(vc_ref[...])
        scores = scores_of(keys, q2, bias_ref, group, span)
        top = top_of(scores)
        probs = [jnp.exp(st - top) for st in scores]
        total = sum_of(probs)
        both = added([dot(v, p.astype(BF), TN) for v, p in zip(values, probs)])
        both = both * (1.0 / total)
        o_ref[rows, :] = join_heads(both).astype(BF)
        lse_ref[0, group : group + 1, :] = top + jnp.log(total)


def attention_backward_kernel(
    info, q_ref, ka_ref, kb_ref, va_ref, vb_ref, kc_ref, vc_ref, do_ref, lse_ref,
    dq_ref, dka_ref, dkb_ref, dva_ref, dvb_ref, dkc_ref, dvc_ref, bias_ref, dk_acc, dv_acc,
):
    chips = ka_ref.shape[0]
    span = chips * PR_DEV
    device, chosen = info[0], info[1]

    @pl.when(pl.program_id(0) == 0)
    def _():
        fill_bias(bias_ref, device, chips)

    for group in range(3):
        rows = slice(group * PR_DEV, (group + 1) * PR_DEV)
        q2 = two_heads(q_ref[rows, :] * jnp.asarray(SCALE, BF))
        do2 = two_heads(do_ref[rows, :])
        lse = lse_ref[0, group : group + 1, :]
        which = group if group < NPR else chosen
        keys = [ref[:, which].reshape(span, PAIR) for ref in (ka_ref, kb_ref)]
        values = [ref[:, which].reshape(span, PAIR) for ref in (va_ref, vb_ref)]
        if group == NPR:
            keys.append(kc_ref[...])
            values.append(vc_ref[...])
        probs = [jnp.exp(st - lse) for st in scores_of(keys, q2, bias_ref, group, span)]
        grads = [dot(v, do2, NT) for v in values]
        delta = sum_of([p * g for p, g in zip(probs, grads)])
        ds = [(p * (g - delta)).astype(BF) for p, g in zip(probs, grads)]
        dq = added([dot(k, d, TN) for k, d in zip(keys, ds)])
        dq_ref[rows, :] = (join_heads(dq) * SCALE).astype(BF)
        for i in range(2):
            dk = dot(ds[i], q2).reshape(chips, PR_DEV, PAIR)
            dv = dot(probs[i].astype(BF), do2).reshape(chips, PR_DEV, PAIR)
            at = slice(i * chips, (i + 1) * chips)
            if group < NPR:
                dk_acc[at, group] = dk
                dv_acc[at, group] = dv
            else:
                dk_acc[at, chosen] += dk
                dv_acc[at, chosen] += dv
        if group == NPR:
            dkc_ref[...] = dot(ds[2], q2).astype(BF)
            dvc_ref[...] = dot(probs[2].astype(BF), do2).astype(BF)
    dka_ref[...] = dk_acc[:chips].astype(BF)
    dkb_ref[...] = dk_acc[chips:].astype(BF)
    dva_ref[...] = dv_acc[:chips].astype(BF)
    dvb_ref[...] = dv_acc[chips:].astype(BF)


def attention_specs(chips, rows, first=0):
    q_spec = pl.BlockSpec((rows, PAIR), lambda h, info: (0, first + h))
    k_spec = pl.BlockSpec((chips, NPR, PR_DEV, PAIR), lambda h, info: (0, 0, 0, first + h))
    c_spec = pl.BlockSpec((CLEN, PAIR), lambda h, info: (0, first + h))
    l_spec = pl.BlockSpec((1, 3, TWO), lambda h, info: (first + h, 0, 0))
    return q_spec, k_spec, c_spec, l_spec


def drop_refs(kernel, n_in, n_dep):
    def body(info, *refs):
        kernel(info, *refs[:n_in], *refs[n_in + n_dep :])

    return body


def attention_forward(info, q, keys, values, kc, vc, deps=()):
    k = keys[0]
    chips, rows, pairs = k.shape[0], q.shape[0], q.shape[1] // PAIR
    q_spec, k_spec, c_spec, l_spec = attention_specs(chips, rows)
    return pl.pallas_call(
        drop_refs(attention_forward_kernel, 7, len(deps)),
        grid_spec=pltpu.PrefetchScalarGridSpec(
            num_scalar_prefetch=1,
            grid=(pairs,),
            in_specs=[q_spec] + [k_spec] * 4 + [c_spec, c_spec]
            + [pl.BlockSpec(memory_space=pl.ANY)] * len(deps),
            out_specs=[q_spec, l_spec],
            scratch_shapes=[pltpu.VMEM((2 * chips * PR_DEV, PR_DEV), F32)],
        ),
        out_shape=[shape_of(q.shape, BF), shape_of((pairs, 3, TWO), F32)],
        compiler_params=pltpu.CompilerParams(vmem_limit_bytes=56 * MIB),
        cost_estimate=cost("attention_forward"),
        name="attention_forward",
    )(info, q, *keys, *values, kc, vc, *deps)


def attention_backward(info, q, keys, values, kc, vc, do, lse, first, pairs, before=(), deps=()):
    k = keys[0]
    chips, rows = k.shape[0], q.shape[0]
    q_spec, k_spec, c_spec, l_spec = attention_specs(chips, rows, first)
    deps = list(before) + list(deps)
    return pl.pallas_call(
        drop_refs(attention_backward_kernel, 9, len(deps)),
        grid_spec=pltpu.PrefetchScalarGridSpec(
            num_scalar_prefetch=1,
            grid=(pairs,),
            in_specs=[q_spec] + [k_spec] * 4 + [c_spec, c_spec, q_spec, l_spec]
            + [pl.BlockSpec(memory_space=pl.ANY)] * len(deps),
            out_specs=[q_spec] + [k_spec] * 4 + [c_spec, c_spec],
            scratch_shapes=[
                pltpu.VMEM((2 * chips * PR_DEV, PR_DEV), F32),
                pltpu.VMEM((2 * chips, NPR, PR_DEV, PAIR), F32),
                pltpu.VMEM((2 * chips, NPR, PR_DEV, PAIR), F32),
            ],
        ),
        out_shape=[shape_of(q.shape, BF)]
        + [shape_of(k.shape, BF)] * 4
        + [shape_of(kc.shape, BF)] * 2,
        input_output_aliases={10 + i: i for i in range(len(before))},
        compiler_params=pltpu.CompilerParams(vmem_limit_bytes=60 * MIB),
        cost_estimate=cost("attention_backward"),
        name="attention_backward",
    )(info, q, *keys, *values, kc, vc, do, lse, *deps)


def swap(value, axis, mask):
    size = lax.axis_size(axis)
    return lax.ppermute(value, axis, [(i, i ^ mask) for i in range(size)])


def far_groups(own, dp):
    return [swap(own, "dp", m) for m in range(2, dp, 2)]


def with_neighbours(far):
    return [tokens for even in far for tokens in (even, swap(even, "dp", 1))]


def exchange(blocks):
    return lax.all_to_all(blocks, "expert", split_axis=0, concat_axis=0, tiled=True)


def root(values):
    return lax.rsqrt(jnp.mean(values * values, axis=-1, keepdims=True) + 1e-06)


def norm_back(norm, scale, grad):
    return scale * (grad - norm * jnp.mean(grad * norm, axis=-1, keepdims=True))


def source_row(row):
    inner = jnp.bitwise_and(row, PR_DEV - 1) * NPR + lax.shift_right_logical(row, 7)
    return jnp.where(row < NPR * PR_DEV, inner, row)


def order_matrix(n):
    return (source_row(iota((n, n), 0)) == iota((n, n), 1)).astype(BF)


def order_matrix_t(n):
    return (source_row(iota((n, n), 1)) == iota((n, n), 0)).astype(BF)


def norm_kernel(info, ins, outs, scratch):
    x, gain = ins
    prompt, hidden_ref, ordered = outs
    tokens = dot(order_matrix(x.shape[0]), x[...])
    hidden = (tokens * root(tokens) * gain[...]).astype(BF)
    prompt[...] = hidden[: NPR * PR_DEV]
    hidden_ref[...] = hidden
    ordered[...] = tokens.astype(BF)


def target(rows, k):
    return (rows[HIGH + k : HIGH + k + 1] * 16.0 + rows[LOW + k : LOW + k + 1]).astype(jnp.int32)


def picks_of(rows, slots):
    at = iota((slots, rows.shape[1]), 0)
    return [at == target(rows, k) for k in range(TOP)]


def low(mask):
    return jnp.where(mask, 1.0, 0.0).astype(BF)


def other_routes(rows, picks):
    low_rows = rows[:8].astype(BF)
    first = dot(low_rows, low(picks[0]), NT)[ROUTE + 1 : ROUTE + 2]
    return first + dot(low_rows, low(picks[1]), NT)[ROUTE : ROUTE + 1]


def send_slots(out, sent, per, at=0):
    for m in range(out.shape[0]):
        out[m, at : at + per, :] = sent[m * per : (m + 1) * per]


def clear_others(out):
    for m in range(out.shape[0]):
        out[m, out.shape[1] - TABLE :, :] = jnp.zeros((TABLE, out.shape[2]), BF)


def send_others(out, others, per, at=0):
    row = out.shape[1] - TABLE
    for m in range(out.shape[0]):
        out[m, row:, at : at + per] = jnp.broadcast_to(
            others[:, m * per : (m + 1) * per], (TABLE, per)
        ).astype(BF)


def table_kernel(per, room, capacity):
    def kernel(info, ins, outs, scratch):
        cot, route, slot = ins
        message, cols, out = outs
        n, width = cot.shape
        order = order_matrix(n)
        ordered = dot(order, cot[...]).astype(BF)
        r, s = route[...], slot[...]
        where = jnp.where(s < capacity, r * room + s, -16)
        high = lax.shift_right_arithmetic(where, 4).astype(F32)
        rest = jnp.bitwise_and(where, 15).astype(F32)
        r = r.astype(F32)
        lane = iota((n, 128), 1)
        table = jnp.zeros((n, 128), F32)
        for first, values in ((HIGH, high), (LOW, rest), (ROUTE, r)):
            for k in range(TOP):
                table = jnp.where(lane == first + k, values[:, k : k + 1], table)
        table = dot(order, table.astype(BF))
        cols[...] = table
        rows = table.T[:TABLE]
        message[:n, :] = ordered
        message[n:, :] = jnp.zeros((TABLE, width), BF)
        message[n:, :n] = rows.astype(BF)
        picks = picks_of(rows, per * out.shape[0])
        send_slots(out, dot(low(jnp.logical_or(*picks)), ordered).astype(BF), per)
        clear_others(out)
        send_others(out, other_routes(rows, picks), per)

    return kernel


def table_rows(message):
    n = message.shape[0] - TABLE
    return message[n:, :n].astype(F32)


def dispatch_cot_kernel(per):
    def kernel(info, ins, outs, scratch):
        out, = outs
        n = ins[0].shape[0] - TABLE
        clear_others(out)
        for g, message in enumerate(ins):
            rows = table_rows(message)
            picks = picks_of(rows, per * out.shape[0])
            sent = dot(low(jnp.logical_or(*picks)), message[:n, :]).astype(BF)
            send_slots(out, sent, per, g * per)
            send_others(out, other_routes(rows, picks), per, g * per)

    return kernel


def dispatch_kernel(per):
    def kernel(info, ins, outs, scratch):
        out, = outs
        groups = len(ins) // 2
        odd = groups // 2
        clear_others(out)
        for g in range(groups):
            message = ins[g]
            n = message.shape[0] - TABLE
            rows = table_rows(message)
            picks = picks_of(rows, per * out.shape[0])
            pick = low(jnp.logical_or(*picks))
            if g % 2:
                at = g // 2 * per
                send_slots(out, dot(pick, message[:n, :]).astype(BF), per, at)
                send_others(out, other_routes(rows, picks), per, at)
            sent = dot(pick, ins[groups + g][...]).astype(BF)
            send_slots(out, sent, per, (odd + g) * per)

    return kernel


def middle_kernel(per):
    def kernel(info, ins, outs, scratch):
        ordered, attended, w_out_proj, gain, w_router, cols, message = ins
        middle_ref, second_ref, gates_ref, out = outs
        middle = ordered[...].astype(F32) + dot(attended[...], w_out_proj[...])
        middle_ref[...] = middle
        second = (middle * root(middle) * gain[...]).astype(BF)
        second_ref[...] = second
        picks = picks_of(table_rows(message), per * out.shape[0])
        send_slots(out, dot(low(jnp.logical_or(*picks)), second).astype(BF), per)
        logits = dot(second, w_router[...])
        column = iota(logits.shape, 1).astype(F32)
        chosen = [
            jnp.sum(
                jnp.where(column == cols[:, ROUTE + k : ROUTE + k + 1], logits, 0.0),
                axis=1,
                keepdims=True,
            )
            for k in range(TOP)
        ]
        lane = iota(gates_ref.shape, 1)
        first = 1.0 / (1.0 + jnp.exp(chosen[1] - chosen[0]))
        then = 1.0 / (1.0 + jnp.exp(chosen[0] - chosen[1]))
        gates_ref[...] = jnp.where(lane == 0, first, then)

    return kernel


def combine_kernel():
    def kernel(info, ins, outs, scratch):
        middle_ref, second_ref, gates, cols, message, attended, w_out_proj, w_router, gain = ins[:9]
        came, came_grad = ins[9:]
        out_ref, grad_middle_ref, grad_attended_ref, grad_proj_ref, few_ref = outs
        n, width = middle_ref.shape
        slots = came.shape[0] * came.shape[1]
        middle, second = middle_ref[...], second_ref[...]
        cot = message[:n, :].astype(F32)
        table = cols[...]
        at = iota((n, slots), 1)
        picks = []
        for k in range(TOP):
            where = table[:, HIGH + k : HIGH + k + 1] * 16.0 + table[:, LOW + k : LOW + k + 1]
            picks.append(at == where.astype(jnp.int32))
        returned = came[...].reshape(slots, width)
        fetched = [dot(low(pick), returned) for pick in picks]
        gate = [gates[:, k : k + 1] for k in range(TOP)]
        outputs = (middle + (gate[0] * fetched[0] + gate[1] * fetched[1])).astype(BF)
        out_ref[...] = dot(order_matrix_t(n), outputs).astype(BF)
        grad_gate = [jnp.sum(cot * f, axis=1, keepdims=True) for f in fetched]
        mean_gate = gate[0] * grad_gate[0] + gate[1] * grad_gate[1]
        experts = w_router.shape[1]
        column = iota((n, experts), 1).astype(F32)
        grad_logits = jnp.zeros((n, experts), F32)
        for k in range(TOP):
            grad_logits = jnp.where(
                column == table[:, ROUTE + k : ROUTE + k + 1],
                gate[k] * (grad_gate[k] - mean_gate),
                grad_logits,
            )
        grad_logits = grad_logits.astype(BF)
        grad_second = dot(
            low(jnp.logical_or(*picks)), came_grad[...].reshape(slots, width)
        ) + dot(
            grad_logits, w_router[...], NT
        )
        scale = root(middle)
        norm = middle * scale
        few_ref[:experts, :] = dot(grad_logits, second, TN).astype(BF)
        few_ref[experts:, :] = jnp.broadcast_to(
            jnp.sum(grad_second * norm, axis=0, keepdims=True), (16, width)
        ).astype(BF)
        grad_middle = cot + norm_back(norm, scale, grad_second * gain[...])
        grad_middle_ref[...] = grad_middle
        grad_attn = grad_middle.astype(BF)
        grad_attended_ref[...] = dot(grad_attn, w_out_proj[...], NT).astype(BF)
        grad_proj_ref[...] = dot(attended[...], grad_attn, TN).astype(BF)

    return kernel


def input_kernel(info, ins, outs, scratch):
    grad_q, grad_kc, grad_vc, w_query, w_key, w_value, ordered, gain, grad_middle = ins[:9]
    parts = ins[9:]
    out, = outs
    shares = parts[0][...].astype(F32)
    for part in parts[1:]:
        shares = shares + part[...].astype(F32)
    grad_hidden = dot(grad_q[...], w_query[...], NT) + jnp.concatenate(
        [shares, dot(grad_kc[...], w_key[...], NT) + dot(grad_vc[...], w_value[...], NT)], axis=0
    )
    tokens = ordered[...].astype(F32)
    scale = root(tokens)
    grad = grad_middle[...] + norm_back(tokens * scale, scale, grad_hidden * gain[...])
    back = order_matrix_t(grad.shape[0])
    high = grad.astype(BF)
    rest = grad - high.astype(F32)
    mid = rest.astype(BF)
    last = (rest - mid.astype(F32)).astype(BF)
    out[...] = (dot(back, high) + dot(back, mid)) + dot(back, last)


def halves_kernel(info, ins, outs, scratch):
    kept, came = ins
    for m, out in enumerate(outs):
        out[...] = (kept[m].astype(F32) + came[m].astype(F32)).astype(BF)


def join_kernel(info, ins, outs, scratch):
    out, = outs
    rows = ins[0].shape[0]
    for i, piece in enumerate(ins):
        out[i * rows : (i + 1) * rows, :] = piece[...]


def keys_and_values(rows, w_key, w_value, deps=()):
    width = rows.shape[1]
    chips = rows.shape[0] // (NPR * PR_DEV)
    many = 2
    block = many * NPR * PR_DEV
    steps = chips // many

    def kernel(rows_ref, w_key_ref, w_value_ref, *refs):
        k_ref, v_ref = refs[len(deps) :]
        values = rows_ref[...]
        k_ref[...] = dot(values, w_key_ref[...]).astype(BF).reshape(many, NPR, PR_DEV, width)
        v_ref[...] = dot(values, w_value_ref[...]).astype(BF).reshape(many, NPR, PR_DEV, width)

    weight = pl.BlockSpec((width, width), lambda i: (0, 0))
    out = pl.BlockSpec((many, NPR, PR_DEV, width), lambda i: (i, 0, 0, 0))
    return pl.pallas_call(
        kernel,
        grid=(steps,),
        in_specs=[pl.BlockSpec((block, width), lambda i: (i, 0)), weight, weight]
        + [pl.BlockSpec(memory_space=pl.ANY)] * len(deps),
        out_specs=[out, out],
        out_shape=[shape_of((chips, NPR, PR_DEV, width), BF)] * 2,
        compiler_params=pltpu.CompilerParams(vmem_limit_bytes=56 * MIB),
        cost_estimate=cost("keys_and_values"),
        name="keys_and_values",
    )(rows, w_key, w_value, *deps)


def shares_of(dk, dv, w_key, w_value):
    chips, width = dk.shape[0], w_key.shape[0]
    rows = chips * NPR * PR_DEV
    total = dot(dk.reshape(rows, width), w_key, NT) + dot(dv.reshape(rows, width), w_value, NT)
    return total.astype(BF).reshape(chips, NPR * PR_DEV, width)


def dense_gradients(info, hidden, rows, dq, dks, dvs, dkc, dvc, proj, few):
    width = hidden.shape[1]
    n_keys = len(rows)
    span = rows[0].shape[0]
    step = width // 3
    half = width // 2
    extra = few.shape[0]
    total = 4 * width + extra

    def kernel(info_ref, hidden_ref, *refs):
        row_refs = refs[:n_keys]
        dq_ref = refs[n_keys]
        dk_refs = refs[n_keys + 1 : 2 * n_keys + 1]
        dv_refs = refs[2 * n_keys + 1 : 3 * n_keys + 1]
        dkc_ref, dvc_ref, proj_ref, few_ref, mine, theirs = refs[3 * n_keys + 1 :]
        j = pl.program_id(0)
        core = info_ref[3]
        query = dot(hidden_ref[...], dq_ref[...], TN)
        both = dot(
            hidden_ref[NPR * PR_DEV :, :],
            jnp.concatenate([dkc_ref[...], dvc_ref[...]], axis=1),
            TN,
        )
        for row_ref, dk_ref, dv_ref in zip(row_refs, dk_refs, dv_refs):
            both = both + dot(
                row_ref[...],
                jnp.concatenate(
                    [dk_ref[...].reshape(span, step), dv_ref[...].reshape(span, step)], axis=1
                ),
                TN,
            )
        pieces = [
            query.astype(BF),
            both[:, :step].astype(BF),
            both[:, step:].astype(BF),
            proj_ref[...],
            few_ref[...],
        ]

        def put(out, at, start, size):
            row = 0
            for piece in pieces:
                out[row : row + piece.shape[0], at : at + size] = piece[:, start : start + size]
                row += piece.shape[0]

        rest = half - step
        for side, (low_out, high_out) in enumerate(((mine, theirs), (theirs, mine))):

            @pl.when(jnp.logical_and(core == side, j == 0))
            def _():
                put(low_out, 0, 0, step)

            @pl.when(jnp.logical_and(core == side, j == 1))
            def _():
                put(low_out, step, 0, rest)
                put(high_out, 0, rest, step - rest)

            @pl.when(jnp.logical_and(core == side, j == 2))
            def _():
                put(high_out, step - rest, 0, step)

    def const(shape):
        return pl.BlockSpec(shape, lambda j, info: (0,) * len(shape), pipeline_mode=pl.Buffered(1))

    def columns(rows_of):
        return pl.BlockSpec((rows_of, step), lambda j, info: (0, j))

    keys = pl.BlockSpec(dks[0].shape[:3] + (step,), lambda j, info: (0, 0, 0, j))
    out = pl.BlockSpec((total, half), lambda j, info: (0, 0))
    return pl.pallas_call(
        kernel,
        grid_spec=pltpu.PrefetchScalarGridSpec(
            num_scalar_prefetch=1,
            grid=(3,),
            in_specs=[const(hidden.shape)]
            + [const(r.shape) for r in rows]
            + [columns(dq.shape[0])]
            + [keys] * (2 * n_keys)
            + [columns(CLEN), columns(CLEN), columns(width), columns(extra)],
            out_specs=[out, out],
        ),
        out_shape=[shape_of((total, half), BF)] * 2,
        compiler_params=pltpu.CompilerParams(vmem_limit_bytes=60 * MIB),
        cost_estimate=cost("dense_gradients"),
        name="dense_gradients",
    )(info, hidden, *rows, dq, *dks, *dvs, dkc, dvc, proj, few)


def gelu_parts(a):
    square = a * a
    t = jnp.tanh(a * (0.7978845608 + (0.7978845608 * 0.044715) * square))
    half = 0.5 * a
    value = half + half * t
    slope = (0.5 + 0.5 * t) + half * (1.0 - t * t) * (
        0.7978845608 + (0.7978845608 * 3.0 * 0.044715) * square
    )
    return value, slope


def gather_rows(into, blocks, first, room):
    for m in range(blocks.shape[0]):
        into[m * room : (m + 1) * room, :] = blocks[m, pl.ds(pl.multiple_of(first, 16), room), :]


def other_column(others, blocks, first, room):
    at = blocks.shape[1] - TABLE
    span = min(blocks.shape[2], -(-at // 128) * 128)
    eye = iota((room, span), 1) == iota((room, span), 0) + first
    for m in range(blocks.shape[0]):
        row = blocks[m, at : at + TABLE, :span][:1].astype(F32)
        column = jnp.sum(jnp.where(eye, row, 0.0), axis=1, keepdims=True)
        others[m * room : (m + 1) * room, :] = jnp.broadcast_to(column, (room, 128))


def gated(rows, cots, others, w_router, mine):
    logits = dot(rows, w_router)
    column = iota(logits.shape, 1)
    own = jnp.sum(jnp.where(column == mine, logits, 0.0), axis=1, keepdims=True)
    other = others[:, : logits.shape[1]].astype(jnp.int32)
    theirs = jnp.sum(jnp.where(column == other, logits, 0.0), axis=1, keepdims=True)
    gate = 1.0 / (1.0 + jnp.exp(theirs - own))
    return (gate * cots.astype(F32)).astype(BF)


def expert_forward(x_slots, w_in, w_out, room, deps=()):
    devices, per, _ = x_slots.shape
    local, width, units = w_in.shape
    rows = devices * room
    chunk = min(units, 768)

    def kernel(x_ref, w_in_ref, w_out_ref, *refs):
        slope_ref, out, x = refs[len(deps) :]
        l = pl.program_id(0)
        gather_rows(x, x_ref, l * room, room)
        parts = [slice(at, at + chunk) for at in range(0, units, chunk)]
        pre = [dot(x[...], w_in_ref[0, :, part]) for part in parts]
        total = jnp.zeros((rows, width), F32)
        for part, act in zip(parts, pre):
            value, slope = gelu_parts(act)
            slope_ref[0, :, part] = slope.astype(BF)
            total = total + dot(value.astype(BF), w_out_ref[0, part, :])
        for m in range(devices):
            out[m, pl.ds(pl.multiple_of(l * room, 16), room), :] = total[
                m * room : (m + 1) * room, :
            ].astype(BF)

    slots = pl.BlockSpec(x_slots.shape, lambda l: (0, 0, 0))
    return pl.pallas_call(
        kernel,
        grid=(local,),
        in_specs=[
            slots,
            pl.BlockSpec((1, width, units), lambda l: (l, 0, 0)),
            pl.BlockSpec((1, units, width), lambda l: (l, 0, 0)),
        ]
        + [pl.BlockSpec(memory_space=pl.ANY)] * len(deps),
        out_specs=[pl.BlockSpec((1, rows, units), lambda l: (l, 0, 0)), slots],
        out_shape=[shape_of((local, rows, units), BF), shape_of(x_slots.shape, BF)],
        scratch_shapes=[pltpu.VMEM((rows, width), BF)],
        compiler_params=pltpu.CompilerParams(vmem_limit_bytes=56 * MIB),
        cost_estimate=cost("expert_forward"),
        name="expert_forward",
    )(x_slots, w_in, w_out, *deps)


def expert_backward(info, x_slots, c_slots, slope, w_router, w_in, w_out, room, deps=()):
    devices, per, _ = x_slots.shape
    local, width, units = w_in.shape
    rows = devices * room
    chunk = min(units, 768)

    def kernel(info_ref, x_ref, c_ref, router_ref, slope_ref, w_in_ref, w_out_ref, *refs):
        out, x, grad, others = refs[len(deps) :]
        l = pl.program_id(0)
        gather_rows(x, x_ref, l * room, room)
        gather_rows(grad, c_ref, l * room, room)
        other_column(others, c_ref, l * room, room)
        grad[...] = gated(
            x[...], grad[...], others[...], router_ref[...], info_ref[0] * local + l
        )
        parts = [slice(at, at + chunk) for at in range(0, units, chunk)]
        grad_act = [dot(grad[...], w_out_ref[0, part, :], NT) for part in parts]
        total = jnp.zeros((rows, width), F32)
        for part, act in zip(parts, grad_act):
            grad_pre = (act * slope_ref[0, :, part].astype(F32)).astype(BF)
            total = total + dot(grad_pre, w_in_ref[0, :, part], NT)
        for m in range(devices):
            out[m, pl.ds(pl.multiple_of(l * room, 16), room), :] = total[
                m * room : (m + 1) * room, :
            ].astype(BF)

    slots = pl.BlockSpec(x_slots.shape, lambda l, info: (0, 0, 0))
    return pl.pallas_call(
        kernel,
        grid_spec=pltpu.PrefetchScalarGridSpec(
            num_scalar_prefetch=1,
            grid=(local,),
            in_specs=[
                slots,
                pl.BlockSpec(c_slots.shape, lambda l, info: (0, 0, 0)),
                pl.BlockSpec(w_router.shape, lambda l, info: (0, 0)),
                pl.BlockSpec((1, rows, units), lambda l, info: (l, 0, 0)),
                pl.BlockSpec((1, width, units), lambda l, info: (l, 0, 0)),
                pl.BlockSpec((1, units, width), lambda l, info: (l, 0, 0)),
            ]
            + [pl.BlockSpec(memory_space=pl.ANY)] * len(deps),
            out_specs=slots,
            scratch_shapes=[
                pltpu.VMEM((rows, width), BF),
                pltpu.VMEM((rows, width), BF),
                pltpu.VMEM((rows, 128), F32),
            ],
        ),
        out_shape=shape_of(x_slots.shape, BF),
        compiler_params=pltpu.CompilerParams(vmem_limit_bytes=56 * MIB),
        cost_estimate=cost("expert_backward"),
        name="expert_backward",
    )(info, x_slots, c_slots, w_router, slope, w_in, w_out, *deps)


def expert_weights(info, groups, w_router, w_in, w_out, room, dp, before=None, last=False, deps=()):
    devices = groups[0][0].shape[0]
    local, width, units = w_in.shape
    part, share = units // dp, width // dp
    rows = devices * room
    flat, places = [], []
    for x, x_base, c, c_base in groups:
        at = []
        for array in (x, c):
            known = [i for i, other in enumerate(flat) if other is array]
            if not known:
                flat.append(array)
            at.append(known[0] if known else len(flat) - 1)
        places.append((at[0], x_base, at[1], c_base))
    n_flat = len(flat)
    sums = [] if before is None else list(before)

    def kernel(info_ref, *refs):
        slots = refs[:n_flat]
        router_ref, w_in_ref, w_out_ref = refs[n_flat : n_flat + 3]
        refs = refs[n_flat + 3 :]
        earlier = refs[: len(sums)]
        refs = refs[len(sums) + len(deps) :]
        out_ref, in_refs = refs[0], refs[1:-4]
        x, grad, others, total = refs[-4:]
        l = pl.program_id(0)
        for g, (x_at, x_base, c_at, c_base) in enumerate(places):
            gather_rows(x, slots[x_at], x_base + l * room, room)
            gather_rows(grad, slots[c_at], c_base + l * room, room)
            other_column(others, slots[c_at], c_base + l * room, room)
            grad[...] = gated(
                x[...], grad[...], others[...], router_ref[...], info_ref[0] * local + l
            )
            value, slope = gelu_parts(dot(x[...], w_in_ref[0]))
            grad_act = dot(grad[...], w_out_ref[0], NT)
            grad_pre = (grad_act * slope).astype(BF)
            part_in = dot(x[...], grad_pre, TN)
            part_out = dot(value.astype(BF), grad[...], TN)
            if g > 0:
                total[...] += part_in
                out_ref[0] += part_out
            elif earlier:
                total[...] = earlier[1][0] + part_in
                out_ref[0] = earlier[0][0] + part_out
            else:
                total[...] = part_in
                out_ref[0] = part_out
        if last:
            for k in range(dp):
                in_refs[0][k, 0] = total[k * share : (k + 1) * share, :].astype(BF)
        else:
            in_refs[0][0] = total[...]

    def const(shape):
        return pl.BlockSpec(shape, lambda l, info: (0,) * len(shape), pipeline_mode=pl.Buffered(1))

    square = pl.BlockSpec((1, part, width), lambda l, info: (l, 0, 0))
    square_in = pl.BlockSpec((1, width, part), lambda l, info: (l, 0, 0))
    if last:
        in_specs = [pl.BlockSpec((dp, 1, share, part), lambda l, info: (0, l, 0, 0))]
        in_shapes = [shape_of((dp, local, share, part), BF)]
    else:
        in_specs = [square_in]
        in_shapes = [shape_of((local, width, part), F32)]
    got = pl.pallas_call(
        kernel,
        grid_spec=pltpu.PrefetchScalarGridSpec(
            num_scalar_prefetch=1,
            grid=(local,),
            in_specs=[const(x.shape) for x in flat]
            + [
                const(w_router.shape),
                pl.BlockSpec((1, width, part), lambda l, info: (l, 0, info[2])),
                pl.BlockSpec((1, part, width), lambda l, info: (l, info[2], 0)),
            ]
            + [square, square_in][: len(sums)]
            + [pl.BlockSpec(memory_space=pl.ANY)] * len(deps),
            out_specs=[square] + in_specs,
            scratch_shapes=[
                pltpu.VMEM((rows, width), BF),
                pltpu.VMEM((rows, width), BF),
                pltpu.VMEM((rows, 128), F32),
                pltpu.VMEM((width, part), F32),
            ],
        ),
        out_shape=[shape_of((local, part, width), F32)] + in_shapes,
        compiler_params=pltpu.CompilerParams(vmem_limit_bytes=60 * MIB),
        cost_estimate=cost("expert_weights_last" if last else "expert_weights"),
        name="expert_weights_last" if last else "expert_weights",
    )(info, *flat, w_router, w_in, w_out, *sums, *deps)
    return got[0], got[1:]


def columns_kernel(info, ins, outs, scratch):
    out, = outs
    pieces, = ins
    part = pieces.shape[3]
    for k in range(pieces.shape[0]):
        out[:, :, k * part : (k + 1) * part] = pieces[k].astype(F32)


class Sums:
    def __init__(self, info, mine, theirs, n, dp, devices):
        self.info, self.n, self.dp, self.devices = info, n, dp, devices
        self.half = mine.shape[1]
        self.rows = self.width = 2 * self.half
        self.chips = devices // 2
        self.tall = self.rows // self.chips
        self.short = self.tall // dp
        self.extra = mine.shape[0] - n * self.rows
        self.value = mine
        self.came = swap(theirs, "expert", 1)

    @staticmethod
    def fits(rows, width, dp, devices):
        short = rows // (devices // 2) // dp
        return short % 16 == 0 and width % 256 == 0 and short * dp * (devices // 2) == rows

    def cores(self, deps=()):
        n, rows, tall, half, extra = self.n, self.rows, self.tall, self.half, self.extra

        def kernel(info_ref, ins, outs, scratch):
            kept, got = ins
            for m, out in enumerate(outs):
                for i in range(n):
                    start = i * rows + jnp.bitwise_xor(info_ref[4], m) * tall
                    at = pl.ds(pl.multiple_of(start, 16), tall)
                    out[i * tall : (i + 1) * tall, :] = (
                        kept[at, :].astype(F32) + got[at, :].astype(F32)
                    ).astype(BF)
                if extra:
                    out[n * tall :, :] = (
                        kept[n * rows :, :].astype(F32) + got[n * rows :, :].astype(F32)
                    ).astype(BF)

        pieces = run(
            kernel, "sum_cores", self.info, [self.value, self.came],
            [shape_of((n * tall + extra, half), BF)] * self.chips, deps=deps,
        )
        self.pieces = [pieces[0]] + [
            swap(pieces[m], "expert", 2 * m) for m in range(1, self.chips)
        ]
        return pieces[0]

    def planes(self, deps=()):
        n, tall, short, half, extra = self.n, self.tall, self.short, self.half, self.extra

        def kernel(info_ref, ins, outs, scratch):
            total, = scratch
            total[...] = added([piece[...].astype(F32) for piece in ins]).astype(BF)
            for k, out in enumerate(outs):
                for i in range(n):
                    start = i * tall + jnp.bitwise_xor(info_ref[2], k) * short
                    out[i * short : (i + 1) * short, :] = total[
                        pl.ds(pl.multiple_of(start, 16), short), :
                    ]
                if extra:
                    out[n * short :, :] = total[n * tall :, :]

        pieces = run(
            kernel, "sum_chips", self.info, self.pieces,
            [shape_of((n * short + extra, half), BF)] * self.dp,
            scratch=[pltpu.VMEM((n * tall + extra, half), BF)], deps=deps,
        )
        self.pieces = [pieces[0]] + [swap(pieces[k], "dp", k) for k in range(1, self.dp)]
        return pieces[0]

    def groups(self, deps=()):
        n, short, half, extra = self.n, self.short, self.half, self.extra

        def kernel(info_ref, ins, outs, scratch):
            value = added([piece[...].astype(F32) for piece in ins]).astype(BF)
            outs[0][...] = value[: n * short]
            if extra:
                outs[1][...] = value[n * short :]

        got = run(
            kernel, "sum_groups", self.info, self.pieces,
            [shape_of((n * short, half), BF)] + ([shape_of((extra, half), BF)] if extra else []),
            deps=deps,
        )
        self.few = list(got[1:])
        self.own = [got[0]] + [swap(got[0], "dp", k) for k in range(1, self.dp)]
        return got[0]

    def gather(self):
        spread = jnp.concatenate(self.own, axis=0)
        self.spread = jnp.concatenate(
            [spread] + [swap(spread, "expert", 2 * m) for m in range(1, self.chips)] + self.few, axis=0
        )
        self.other = swap(self.spread, "expert", 1)

    def finish(self, columns, gain, weights, deps=()):
        n, short, tall, half, extra = self.n, self.short, self.tall, self.half, self.extra
        chips, dp, rows = self.chips, self.dp, self.rows

        def kernel(info_ref, ins, outs, scratch):
            for c, ref in enumerate(ins[:2]):
                lanes = pl.ds(pl.multiple_of(jnp.bitwise_xor(info_ref[3], c) * half, 128), half)
                for m in range(chips):
                    for k in range(dp):
                        start = jnp.bitwise_xor(info_ref[4], m) * tall
                        start = start + jnp.bitwise_xor(info_ref[2], k) * short
                        at = pl.ds(pl.multiple_of(start, 16), short)
                        for i in range(n):
                            place = ((m * dp + k) * n + i) * short
                            outs[i][at, lanes] = ref[place : place + short, :].astype(F32)
                scratch[0][:, lanes] = ref[chips * dp * n * short :, :].astype(F32)
            outs[n][...] = scratch[0][:columns, :].T
            outs[n + 1][...] = scratch[0][columns : columns + 1, :]
            outs[n + 2][...] = gained(zip(ins[3:], outs), ins[2][...])

        row = shape_of((1, self.width), F32)
        return run(
            kernel, "spread_sums", self.info, [self.spread, self.other, gain] + list(weights),
            [shape_of((rows, self.width), F32)] * n + [shape_of((self.width, columns), F32), row, row],
            scratch=[pltpu.VMEM((extra, self.width), F32)], deps=deps,
        )


def gained(pairs, gain):
    total = 0.0
    for weight, grad in pairs:
        total = total + jnp.sum(weight[...].astype(F32) * grad[...], axis=1, keepdims=True)
    return jnp.broadcast_to(total, (total.shape[0], 128)).T[:1] / gain


def per_device(
    inputs,
    gain_one,
    w_query,
    w_key,
    w_value,
    w_out_proj,
    gain_two,
    w_router,
    w_in,
    w_out,
    routes,
    slot_index,
    prompt_of,
    cotangent,
):
    row_count, width = inputs.shape[1], inputs.shape[2]
    dp, devices = lax.axis_size("dp"), lax.axis_size("expert")
    z, device = lax.axis_index("dp"), lax.axis_index("expert")
    chips = devices // 2
    prompt_rows = NPR * PR_DEV
    expert_count, local = w_router.shape[1], w_in.shape[0]
    capacity = max(2, 5 * row_count * TOP // (4 * expert_count))
    room = -(-capacity // 16) * 16
    per = local * room
    info = jnp.stack(
        [device, prompt_of[0, 0], z, lax.rem(device, 2), lax.div(device, 2)]
    ).astype(jnp.int32)
    gain_one = gain_one[None, :]
    gain_two = gain_two[None, :]
    wide = shape_of((row_count, width), BF)
    wide32 = shape_of((row_count, width), F32)
    narrow = shape_of((row_count, 128), F32)
    x_shape = shape_of((devices, per, width), BF)
    c_shape = shape_of((devices, per + TABLE, width), BF)

    hidden_p, hidden, ordered = run(
        norm_kernel, "norm", info, [inputs[0], gain_one],
        [shape_of((prompt_rows, width), BF), wide, wide],
    )
    near = [hidden_p] + [swap(hidden_p, "expert", 2 * m) for m in range(1, chips)]

    message, cols, c_sent = run(
        table_kernel(per, room, capacity), "table", info,
        [cotangent[0], routes[0], slot_index[0]],
        [shape_of((row_count + TABLE, width), BF), narrow, c_shape],
        deps=[hidden_p],
    )
    hidden_c = hidden[prompt_rows:]
    queries = dot(hidden, w_query).astype(BF)
    key_c = dot(hidden_c, w_key).astype(BF)
    value_c = dot(hidden_c, w_value).astype(BF)
    near, cols, queries, key_c, value_c = lax.optimization_barrier(
        (near, cols, queries, key_c, value_c)
    )
    near, = run(join_kernel, "join", info, near, [shape_of((chips * prompt_rows, width), BF)])
    other = swap(near, "expert", 1)
    messages = far_groups(message, dp)
    c_sent, near = lax.optimization_barrier((c_sent, near))
    c_slots = [exchange(c_sent)]

    key_near, value_near = keys_and_values(near, w_key, w_value)
    key_other, value_other = keys_and_values(other, w_key, w_value, deps=[key_near])
    keys, values = [key_near, key_other], [value_near, value_other]
    attended, lse = attention_forward(info, queries, keys, values, key_c, value_c)
    c_slots, messages, attended = lax.optimization_barrier((c_slots, messages, attended))

    middle, second, gates, x_sent = run(
        middle_kernel(per), "middle", info,
        [ordered, attended, w_out_proj, gain_two, w_router, cols, message],
        [wide32, wide, narrow, x_shape],
    )
    x_slots = [exchange(x_sent)]
    seconds = far_groups(second, dp)
    c_rest = run(
        dispatch_cot_kernel(per), "dispatch_cot", info, messages,
        [shape_of((devices, len(messages) * per + TABLE, width), BF)], deps=[middle],
    )
    x_slots, c_rest = lax.optimization_barrier((x_slots, c_rest))
    c_even, = [exchange(sent) for sent in c_rest]

    slope, out_sent = expert_forward(x_slots[0], w_in, w_out, room)
    seconds, slope, c_slots[0], x_slots[0] = lax.optimization_barrier(
        (seconds, slope, c_slots[0], x_slots[0])
    )
    c_odd = [swap(c_slots[0], "dp", 1)]
    x_odd = [swap(x_slots[0], "dp", 1)]
    seconds = with_neighbours(seconds)
    messages = with_neighbours(messages)
    returned = exchange(out_sent)
    grad_sent = expert_backward(
        info, x_slots[0], c_slots[0], slope, w_router, w_in, w_out, room, deps=[c_even]
    )
    returned, grad_sent = lax.optimization_barrier((returned, grad_sent))
    grad_returned = exchange(grad_sent)

    sums = expert_weights(
        info, [(x_slots[0], 0, c_slots[0], 0)], w_router, w_in, w_out, room, dp,
        deps=[grad_sent],
    )
    far = dp - 2
    odd = far // 2
    rest, = run(
        dispatch_kernel(per), "dispatch", info, messages + seconds,
        [shape_of((devices, (odd + far) * per + TABLE, width), BF)], deps=[sums[0]],
    )

    outputs, grad_middle, grad_attended, grad_proj, few = run(
        combine_kernel(), "combine", info,
        [middle, second, gates, cols, message, attended, w_out_proj, w_router, gain_two]
        + [returned, grad_returned],
        [wide, wide32, wide, shape_of((width, width), BF), shape_of((expert_count + 16, width), BF)],
        deps=[rest],
    )
    rest = exchange(rest)

    pairs = width // PAIR

    def back(first, count, before=(), deps=()):
        return attention_backward(
            info, queries, keys, values, key_c, value_c, grad_attended, lse, first, count,
            before=before, deps=deps,
        )

    got = back(0, pairs, deps=())
    grad_q, dk_near, dk_far, dv_near, dv_far, grad_kc, grad_vc = got
    grad_q, dk_near, dk_far, dv_near, dv_far, x_odd, c_odd = lax.optimization_barrier(
        (grad_q, dk_near, dk_far, dv_near, dv_far, x_odd, c_odd)
    )
    stepwise = Sums.fits(width, width, dp, devices)
    if stepwise:
        mine, theirs = dense_gradients(
            info, hidden, [near, other], grad_q, [dk_near, dk_far], [dv_near, dv_far],
            grad_kc, grad_vc, grad_proj, few,
        )
        total = Sums(info, mine, theirs, 4, dp, devices)
    else:
        flat = [part.reshape(chips * prompt_rows, width) for part in (dk_near, dk_far, dv_near, dv_far)]
        grad_query = dot(hidden, grad_q, TN)
        grad_key = dot(near, flat[0], TN) + dot(other, flat[1], TN) + dot(hidden_c, grad_kc, TN)
        grad_value = dot(near, flat[2], TN) + dot(other, flat[3], TN) + dot(hidden_c, grad_vc, TN)
        dense = [grad_query, grad_key, grad_value, grad_proj, few]

    sent = shares_of(dk_far, dv_far, w_key, w_value)
    kept = shares_of(dk_near, dv_near, w_key, w_value)
    came = swap(sent, "expert", 1)
    after = total.cores([kept]) if stepwise else kept
    shares = run(
        halves_kernel, "halves", info, [kept, came],
        [shape_of((prompt_rows, width), BF)] * chips, deps=[after],
    )

    others = [(x_odd[0], 0, c_odd[0], 0)]
    for g in range(far):
        c_from, c_base = (rest, g // 2 * per) if g % 2 else (c_even, g // 2 * per)
        others.append((rest, (odd + g) * per, c_from, c_base))
    grad_w_out, in_pieces = expert_weights(
        info, others, w_router, w_in, w_out, room, dp,
        before=(sums[0], sums[1][0]), last=True, deps=[shares[0]],
    )
    shares, in_pieces, grad_w_out = lax.optimization_barrier((shares, in_pieces, grad_w_out))
    after = [grad_w_out]
    if stepwise:
        after = [total.planes(after)]
    shares = [shares[0]] + [swap(shares[m], "expert", 2 * m) for m in range(1, chips)]
    if stepwise:
        after = [total.groups(after + shares)]
        total.own[0], in_pieces = lax.optimization_barrier((total.own[0], in_pieces))
    grad_input, = run(
        input_kernel, "input", info,
        [grad_q, grad_kc, grad_vc, w_query, w_key, w_value, ordered, gain_one, grad_middle] + shares,
        [wide32], deps=after,
    )
    if stepwise:
        total.own, grad_input = lax.optimization_barrier((total.own, grad_input))
        total.gather()
    in_pieces = lax.all_to_all(in_pieces[0], "dp", split_axis=0, concat_axis=0, tiled=True)
    grad_w_in, = run(
        columns_kernel, "columns", info, [in_pieces],
        [shape_of((local, width // dp, w_in.shape[2]), F32)]
    )
    if stepwise:
        query_sum, key_sum, value_sum, proj_sum, grad_router, grad_gain_two, grad_gain_one = (
            total.finish(
                expert_count, gain_one, [w_query, w_key, w_value], deps=[grad_w_in]
            )
        )
    else:
        query_sum, key_sum, value_sum, proj_sum, few = lax.psum(
            [part.astype(F32) for part in dense], ("dp", "expert")
        )
        grad_router, grad_gain_two = few[:expert_count].T, few[expert_count :][:1]
        grad_gain_one = gained(
            [(w_query, query_sum), (w_key, key_sum), (w_value, value_sum)], gain_one
        )
    return (
        outputs[None],
        grad_input[None],
        grad_gain_one[0],
        query_sum,
        key_sum,
        value_sum,
        proj_sum,
        grad_gain_two[0],
        grad_router,
        grad_w_in,
        grad_w_out,
    )


def solution(mesh):
    return jax.shard_map(
        per_device,
        mesh=mesh,
        in_specs=(
            P("dp", "expert", None),
            P(),
            P(),
            P(),
            P(),
            P(),
            P(),
            P(),
            P("expert", None, None),
            P("expert", None, None),
            P("dp", "expert", None),
            P("dp", "expert", None),
            P("dp", "expert"),
            P("dp", "expert", None),
        ),
        out_specs=(
            P("dp", "expert", None),
            P("dp", "expert", None),
            P(),
            P(),
            P(),
            P(),
            P(),
            P(),
            P(),
            P("expert", "dp", None),
            P("expert", "dp", None),
        ),
        check_vma=False,
    )
```

```python
import jax
import jax.numpy as jnp
from jax import lax
from jax.experimental import pallas as pl
from jax.experimental.pallas import tpu as pltpu
from jax.sharding import PartitionSpec as P

H = 12
HD = 64
TOP = 2
NPR = 2
CLEN = 128
PR_DEV = 128
PAIR = 2 * HD
TWO = 2 * PR_DEV

NEGATIVE = -1e30
BF = jnp.bfloat16
F32 = jnp.float32
SCALE = HD ** (-0.5)
MIB = 1024 * 1024

NN = ((1,), (0,))
NT = ((1,), (1,))
TN = ((0,), (0,))

HIGH, LOW, ROUTE = 0, 2, 4
TABLE = 16


def dot(a, b, dims=NN):
    return lax.dot_general(a, b, (dims, ((), ())), preferred_element_type=F32)


def iota(shape, dim):
    return lax.broadcasted_iota(jnp.int32, shape, dim)


def shape_of(shape, dtype):
    return jax.ShapeDtypeStruct(shape, dtype)


WEIGHT = 1.0
TIMES = {
    "norm": 2.7,
    "table": 4.5,
    "attention_forward": 15.0,
    "middle": 5.1,
    "expert_forward": 20.0,
    "expert_backward": 20.0,
    "dispatch": 30.0,
    "expert_weights": 1.0,
    "combine": 3.0,
    "attention_backward": 15.0,
    "sum_cores": 0.3,
    "halves": 0.3,
    "expert_weights_last": 30.0,
    "sum_chips": 2.6,
    "sum_groups": 1.8,
    "input": 1.0,
    "spread_sums": 60.0,
    "columns": 1.0,
    "join": 2.0,
    "keys_and_values": 3.5,
    "dense_gradients": 60.0,
}


def cost(name):
    flops = int(TIMES[name] * WEIGHT * 1.1e9)
    return pl.CostEstimate(flops=flops, bytes_accessed=0, transcendentals=0)


def run(kernel, name, info, operands, outs, deps=(), scratch=()):
    n_in, n_dep, n_out = len(operands), len(deps), len(outs)

    def body(info_ref, *refs):
        ins = refs[:n_in]
        results = refs[n_in + n_dep : n_in + n_dep + n_out]
        kernel(info_ref, ins, results, refs[n_in + n_dep + n_out :])

    vmem = pl.BlockSpec(memory_space=pltpu.VMEM)
    return pl.pallas_call(
        body,
        in_specs=[pl.BlockSpec(memory_space=pltpu.SMEM)]
        + [vmem] * n_in
        + [pl.BlockSpec(memory_space=pl.ANY)] * n_dep,
        out_specs=[vmem] * n_out,
        out_shape=list(outs),
        scratch_shapes=list(scratch),
        compiler_params=pltpu.CompilerParams(vmem_limit_bytes=56 * MIB),
        cost_estimate=cost(name),
        name=name,
    )(info, *operands, *deps)


def fill_bias(bias_ref, device, chips):
    for b in range(2 * chips):
        mask = 2 * (b % chips) + b // chips
        offset = (jnp.bitwise_xor(device, mask) - device) * PR_DEV
        seen = iota((PR_DEV, PR_DEV), 0) + offset <= iota((PR_DEV, PR_DEV), 1)
        bias_ref[b * PR_DEV : (b + 1) * PR_DEV, :] = jnp.where(seen, 0.0, NEGATIVE)


def two_heads(rows):
    keep = (iota((TWO, PAIR), 0) < PR_DEV) == (iota((TWO, PAIR), 1) < HD)
    return jnp.where(keep, jnp.concatenate([rows, rows], axis=0), jnp.zeros((), rows.dtype))


def join_heads(both):
    first = iota((PAIR, PR_DEV), 0) < HD
    return jnp.where(first, both[:, :PR_DEV], both[:, PR_DEV:]).T


def twice(block):
    return jnp.concatenate([block, block], axis=1)


def top_of(parts):
    top = jnp.max(parts[0], axis=0, keepdims=True)
    for part in parts[1:]:
        top = jnp.maximum(top, jnp.max(part, axis=0, keepdims=True))
    return top


def sum_of(parts):
    total = jnp.sum(parts[0], axis=0, keepdims=True)
    for part in parts[1:]:
        total = total + jnp.sum(part, axis=0, keepdims=True)
    return total


def added(parts):
    total = parts[0]
    for part in parts[1:]:
        total = total + part
    return total


def scores_of(keys, q2, bias_ref, group, span):
    parts = []
    for i, k in enumerate(keys):
        st = dot(k, q2, NT)
        if group < NPR:
            st = st + twice(bias_ref[i * span : (i + 1) * span, :])
        elif i == 2:
            st = st + twice(bias_ref[:PR_DEV, :])
        parts.append(st)
    return parts


def attention_forward_kernel(
    info, q_ref, ka_ref, kb_ref, va_ref, vb_ref, kc_ref, vc_ref, o_ref, lse_ref, bias_ref
):
    chips = ka_ref.shape[0]
    span = chips * PR_DEV
    device, chosen = info[0], info[1]

    @pl.when(pl.program_id(0) == 0)
    def _():
        fill_bias(bias_ref, device, chips)

    for group in range(3):
        rows = slice(group * PR_DEV, (group + 1) * PR_DEV)
        q2 = two_heads(q_ref[rows, :] * jnp.asarray(SCALE, BF))
        which = group if group < NPR else chosen
        keys = [ref[:, which].reshape(span, PAIR) for ref in (ka_ref, kb_ref)]
        values = [ref[:, which].reshape(span, PAIR) for ref in (va_ref, vb_ref)]
        if group == NPR:
            keys.append(kc_ref[...])
            values.append(vc_ref[...])
        scores = scores_of(keys, q2, bias_ref, group, span)
        top = top_of(scores)
        probs = [jnp.exp(st - top) for st in scores]
        total = sum_of(probs)
        both = added([dot(v, p.astype(BF), TN) for v, p in zip(values, probs)])
        both = both * (1.0 / total)
        o_ref[rows, :] = join_heads(both).astype(BF)
        lse_ref[0, group : group + 1, :] = top + jnp.log(total)


def attention_backward_kernel(
    info, q_ref, ka_ref, kb_ref, va_ref, vb_ref, kc_ref, vc_ref, do_ref, lse_ref, delta_ref,
    dq_ref, dka_ref, dkb_ref, dva_ref, dvb_ref, dkc_ref, dvc_ref, bias_ref, dk_acc, dv_acc,
):
    chips = ka_ref.shape[0]
    span = chips * PR_DEV
    device, chosen = info[0], info[1]

    @pl.when(pl.program_id(0) == 0)
    def _():
        fill_bias(bias_ref, device, chips)

    for group in range(3):
        rows = slice(group * PR_DEV, (group + 1) * PR_DEV)
        q2 = two_heads(q_ref[rows, :] * jnp.asarray(SCALE, BF))
        do2 = two_heads(do_ref[rows, :])
        lse = lse_ref[0, group : group + 1, :]
        which = group if group < NPR else chosen
        keys = [ref[:, which].reshape(span, PAIR) for ref in (ka_ref, kb_ref)]
        values = [ref[:, which].reshape(span, PAIR) for ref in (va_ref, vb_ref)]
        if group == NPR:
            keys.append(kc_ref[...])
            values.append(vc_ref[...])
        probs = [jnp.exp(st - lse) for st in scores_of(keys, q2, bias_ref, group, span)]
        grads = [dot(v, do2, NT) for v in values]
        delta = delta_ref[0, group : group + 1, :]
        ds = [(p * (g - delta)).astype(BF) for p, g in zip(probs, grads)]
        dq = added([dot(k, d, TN) for k, d in zip(keys, ds)])
        dq_ref[rows, :] = (join_heads(dq) * SCALE).astype(BF)
        for i in range(2):
            dk = dot(ds[i], q2).reshape(chips, PR_DEV, PAIR)
            dv = dot(probs[i].astype(BF), do2).reshape(chips, PR_DEV, PAIR)
            at = slice(i * chips, (i + 1) * chips)
            if group < NPR:
                dk_acc[at, group] = dk
                dv_acc[at, group] = dv
            else:
                dk_acc[at, chosen] += dk
                dv_acc[at, chosen] += dv
        if group == NPR:
            dkc_ref[...] = dot(ds[2], q2).astype(BF)
            dvc_ref[...] = dot(probs[2].astype(BF), do2).astype(BF)
    dka_ref[...] = dk_acc[:chips].astype(BF)
    dkb_ref[...] = dk_acc[chips:].astype(BF)
    dva_ref[...] = dv_acc[:chips].astype(BF)
    dvb_ref[...] = dv_acc[chips:].astype(BF)


def attention_specs(chips, rows, first=0):
    q_spec = pl.BlockSpec((rows, PAIR), lambda h, info: (0, first + h))
    k_spec = pl.BlockSpec((chips, NPR, PR_DEV, PAIR), lambda h, info: (0, 0, 0, first + h))
    c_spec = pl.BlockSpec((CLEN, PAIR), lambda h, info: (0, first + h))
    l_spec = pl.BlockSpec((1, 3, TWO), lambda h, info: (first + h, 0, 0))
    return q_spec, k_spec, c_spec, l_spec


def drop_refs(kernel, n_in, n_dep):
    def body(info, *refs):
        kernel(info, *refs[:n_in], *refs[n_in + n_dep :])

    return body


def attention_forward(info, q, keys, values, kc, vc, deps=()):
    k = keys[0]
    chips, rows, pairs = k.shape[0], q.shape[0], q.shape[1] // PAIR
    q_spec, k_spec, c_spec, l_spec = attention_specs(chips, rows)
    return pl.pallas_call(
        drop_refs(attention_forward_kernel, 7, len(deps)),
        grid_spec=pltpu.PrefetchScalarGridSpec(
            num_scalar_prefetch=1,
            grid=(pairs,),
            in_specs=[q_spec] + [k_spec] * 4 + [c_spec, c_spec]
            + [pl.BlockSpec(memory_space=pl.ANY)] * len(deps),
            out_specs=[q_spec, l_spec],
            scratch_shapes=[pltpu.VMEM((2 * chips * PR_DEV, PR_DEV), F32)],
        ),
        out_shape=[shape_of(q.shape, BF), shape_of((pairs, 3, TWO), F32)],
        compiler_params=pltpu.CompilerParams(vmem_limit_bytes=56 * MIB),
        cost_estimate=cost("attention_forward"),
        name="attention_forward",
    )(info, q, *keys, *values, kc, vc, *deps)


def attention_backward(info, q, keys, values, kc, vc, do, lse, delta, first, pairs, before=(), deps=()):
    k = keys[0]
    chips, rows = k.shape[0], q.shape[0]
    q_spec, k_spec, c_spec, l_spec = attention_specs(chips, rows, first)
    deps = list(before) + list(deps)
    return pl.pallas_call(
        drop_refs(attention_backward_kernel, 10, len(deps)),
        grid_spec=pltpu.PrefetchScalarGridSpec(
            num_scalar_prefetch=1,
            grid=(pairs,),
            in_specs=[q_spec] + [k_spec] * 4 + [c_spec, c_spec, q_spec, l_spec, l_spec]
            + [pl.BlockSpec(memory_space=pl.ANY)] * len(deps),
            out_specs=[q_spec] + [k_spec] * 4 + [c_spec, c_spec],
            scratch_shapes=[
                pltpu.VMEM((2 * chips * PR_DEV, PR_DEV), F32),
                pltpu.VMEM((2 * chips, NPR, PR_DEV, PAIR), F32),
                pltpu.VMEM((2 * chips, NPR, PR_DEV, PAIR), F32),
            ],
        ),
        out_shape=[shape_of(q.shape, BF)]
        + [shape_of(k.shape, BF)] * 4
        + [shape_of(kc.shape, BF)] * 2,
        input_output_aliases={11 + i: i for i in range(len(before))},
        compiler_params=pltpu.CompilerParams(vmem_limit_bytes=60 * MIB),
        cost_estimate=cost("attention_backward"),
        name="attention_backward",
    )(info, q, *keys, *values, kc, vc, do, lse, delta, *deps)


def swap(value, axis, mask):
    size = lax.axis_size(axis)
    return lax.ppermute(value, axis, [(i, i ^ mask) for i in range(size)])


def far_groups(own, dp):
    return [swap(own, "dp", m) for m in range(2, dp, 2)]


def with_neighbours(far):
    return [tokens for even in far for tokens in (even, swap(even, "dp", 1))]


def exchange(blocks):
    return lax.all_to_all(blocks, "expert", split_axis=0, concat_axis=0, tiled=True)


def root(values):
    return lax.rsqrt(jnp.mean(values * values, axis=-1, keepdims=True) + 1e-06)


def norm_back(norm, scale, grad):
    return scale * (grad - norm * jnp.mean(grad * norm, axis=-1, keepdims=True))


def source_row(row):
    inner = jnp.bitwise_and(row, PR_DEV - 1) * NPR + lax.shift_right_logical(row, 7)
    return jnp.where(row < NPR * PR_DEV, inner, row)


def order_matrix(n):
    return (source_row(iota((n, n), 0)) == iota((n, n), 1)).astype(BF)


def order_matrix_t(n):
    return (source_row(iota((n, n), 1)) == iota((n, n), 0)).astype(BF)


def norm_kernel(info, ins, outs, scratch):
    x, gain = ins
    prompt, hidden_ref, ordered = outs
    tokens = dot(order_matrix(x.shape[0]), x[...])
    hidden = (tokens * root(tokens) * gain[...]).astype(BF)
    prompt[...] = hidden[: NPR * PR_DEV]
    hidden_ref[...] = hidden
    ordered[...] = tokens.astype(BF)


def target(rows, k):
    return (rows[HIGH + k : HIGH + k + 1] * 16.0 + rows[LOW + k : LOW + k + 1]).astype(jnp.int32)


def picks_of(rows, slots):
    at = iota((slots, rows.shape[1]), 0)
    return [at == target(rows, k) for k in range(TOP)]


def low(mask):
    return jnp.where(mask, 1.0, 0.0).astype(BF)


def other_routes(rows, picks):
    low_rows = rows[:8].astype(BF)
    first = dot(low_rows, low(picks[0]), NT)[ROUTE + 1 : ROUTE + 2]
    return first + dot(low_rows, low(picks[1]), NT)[ROUTE : ROUTE + 1]


def send_slots(out, sent, per, at=0):
    for m in range(out.shape[0]):
        out[m, at : at + per, :] = sent[m * per : (m + 1) * per]


def clear_others(out):
    for m in range(out.shape[0]):
        out[m, out.shape[1] - TABLE :, :] = jnp.zeros((TABLE, out.shape[2]), BF)


def send_others(out, others, per, at=0):
    row = out.shape[1] - TABLE
    for m in range(out.shape[0]):
        out[m, row:, at : at + per] = jnp.broadcast_to(
            others[:, m * per : (m + 1) * per], (TABLE, per)
        ).astype(BF)


def table_kernel(per, room, capacity):
    def kernel(info, ins, outs, scratch):
        cot, route, slot = ins
        message, cols, out = outs
        n, width = cot.shape
        order = order_matrix(n)
        ordered = dot(order, cot[...]).astype(BF)
        r, s = route[...], slot[...]
        where = jnp.where(s < capacity, r * room + s, -16)
        high = lax.shift_right_arithmetic(where, 4).astype(F32)
        rest = jnp.bitwise_and(where, 15).astype(F32)
        r = r.astype(F32)
        lane = iota((n, 128), 1)
        table = jnp.zeros((n, 128), F32)
        for first, values in ((HIGH, high), (LOW, rest), (ROUTE, r)):
            for k in range(TOP):
                table = jnp.where(lane == first + k, values[:, k : k + 1], table)
        table = dot(order, table.astype(BF))
        cols[...] = table
        rows = table.T[:TABLE]
        message[:n, :] = ordered
        message[n:, :] = jnp.zeros((TABLE, width), BF)
        message[n:, :n] = rows.astype(BF)
        picks = picks_of(rows, per * out.shape[0])
        send_slots(out, dot(low(jnp.logical_or(*picks)), ordered).astype(BF), per)
        clear_others(out)
        send_others(out, other_routes(rows, picks), per)

    return kernel


def table_rows(message):
    n = message.shape[0] - TABLE
    return message[n:, :n].astype(F32)


def dispatch_kernel(per):
    def kernel(info, ins, outs, scratch):
        out, = outs
        groups = len(ins) // 2
        clear_others(out)
        for g in range(groups):
            message = ins[g]
            n = message.shape[0] - TABLE
            rows = table_rows(message)
            picks = picks_of(rows, per * out.shape[0])
            pick = low(jnp.logical_or(*picks))
            send_slots(out, dot(pick, message[:n, :]).astype(BF), per, g * per)
            send_others(out, other_routes(rows, picks), per, g * per)
            sent = dot(pick, ins[groups + g][...]).astype(BF)
            send_slots(out, sent, per, (groups + g) * per)

    return kernel


def middle_kernel(per):
    def kernel(info, ins, outs, scratch):
        ordered, attended, w_out_proj, gain, w_router, cols, message = ins
        middle_ref, second_ref, gates_ref, out = outs
        middle = ordered[...].astype(F32) + dot(attended[...], w_out_proj[...])
        middle_ref[...] = middle
        second = (middle * root(middle) * gain[...]).astype(BF)
        second_ref[...] = second
        picks = picks_of(table_rows(message), per * out.shape[0])
        send_slots(out, dot(low(jnp.logical_or(*picks)), second).astype(BF), per)
        logits = dot(second, w_router[...])
        column = iota(logits.shape, 1).astype(F32)
        chosen = [
            jnp.sum(
                jnp.where(column == cols[:, ROUTE + k : ROUTE + k + 1], logits, 0.0),
                axis=1,
                keepdims=True,
            )
            for k in range(TOP)
        ]
        lane = iota(gates_ref.shape, 1)
        first = 1.0 / (1.0 + jnp.exp(chosen[1] - chosen[0]))
        then = 1.0 / (1.0 + jnp.exp(chosen[0] - chosen[1]))
        gates_ref[...] = jnp.where(lane == 0, first, then)

    return kernel


def combine_kernel():
    def kernel(info, ins, outs, scratch):
        middle_ref, second_ref, gates, cols, message, attended, w_out_proj, w_router, gain = ins[:9]
        came, came_grad = ins[9:]
        out_ref, grad_middle_ref, grad_attended_ref, grad_proj_ref, few_ref, delta_ref = outs
        n, width = middle_ref.shape
        slots = came.shape[0] * came.shape[1]
        middle, second = middle_ref[...], second_ref[...]
        cot = message[:n, :].astype(F32)
        table = cols[...]
        at = iota((n, slots), 1)
        picks = []
        for k in range(TOP):
            where = table[:, HIGH + k : HIGH + k + 1] * 16.0 + table[:, LOW + k : LOW + k + 1]
            picks.append(at == where.astype(jnp.int32))
        returned = came[...].reshape(slots, width)
        fetched = [dot(low(pick), returned) for pick in picks]
        gate = [gates[:, k : k + 1] for k in range(TOP)]
        outputs = (middle + (gate[0] * fetched[0] + gate[1] * fetched[1])).astype(BF)
        out_ref[...] = dot(order_matrix_t(n), outputs).astype(BF)
        grad_gate = [jnp.sum(cot * f, axis=1, keepdims=True) for f in fetched]
        mean_gate = gate[0] * grad_gate[0] + gate[1] * grad_gate[1]
        experts = w_router.shape[1]
        column = iota((n, experts), 1).astype(F32)
        grad_logits = jnp.zeros((n, experts), F32)
        for k in range(TOP):
            grad_logits = jnp.where(
                column == table[:, ROUTE + k : ROUTE + k + 1],
                gate[k] * (grad_gate[k] - mean_gate),
                grad_logits,
            )
        grad_logits = grad_logits.astype(BF)
        grad_second = dot(
            low(jnp.logical_or(*picks)), came_grad[...].reshape(slots, width)
        ) + dot(
            grad_logits, w_router[...], NT
        )
        scale = root(middle)
        norm = middle * scale
        few_ref[:experts, :] = dot(grad_logits, second, TN).astype(BF)
        few_ref[experts:, :] = jnp.broadcast_to(
            jnp.sum(grad_second * norm, axis=0, keepdims=True), (16, width)
        ).astype(BF)
        grad_middle = cot + norm_back(norm, scale, grad_second * gain[...])
        grad_middle_ref[...] = grad_middle
        grad_attn = grad_middle.astype(BF)
        grad_attended = dot(grad_attn, w_out_proj[...], NT).astype(BF)
        grad_attended_ref[...] = grad_attended
        product = grad_attended.astype(F32) * attended[...].astype(F32)
        high = product.astype(BF)
        heads = 2 * delta_ref.shape[0]
        head = low(lax.shift_right_logical(iota((16, width), 1), 6) == iota((16, width), 0))
        delta = dot(head, high, NT) + dot(head, (product - high.astype(F32)).astype(BF), NT)
        for h in range(heads):
            for group in range(3):
                delta_ref[h // 2, group : group + 1, h % 2 * PR_DEV : (h % 2 + 1) * PR_DEV] = delta[
                    h : h + 1, group * PR_DEV : (group + 1) * PR_DEV
                ]
        grad_proj_ref[...] = dot(attended[...], grad_attn, TN).astype(BF)

    return kernel


def input_kernel(info, ins, outs, scratch):
    grad_q, grad_kc, grad_vc, w_query, w_key, w_value, ordered, gain, grad_middle = ins[:9]
    parts = ins[9:]
    out, = outs
    shares = parts[0][...].astype(F32)
    for part in parts[1:]:
        shares = shares + part[...].astype(F32)
    grad_hidden = dot(grad_q[...], w_query[...], NT) + jnp.concatenate(
        [shares, dot(grad_kc[...], w_key[...], NT) + dot(grad_vc[...], w_value[...], NT)], axis=0
    )
    tokens = ordered[...].astype(F32)
    scale = root(tokens)
    grad = grad_middle[...] + norm_back(tokens * scale, scale, grad_hidden * gain[...])
    back = order_matrix_t(grad.shape[0])
    high = grad.astype(BF)
    rest = grad - high.astype(F32)
    mid = rest.astype(BF)
    last = (rest - mid.astype(F32)).astype(BF)
    out[...] = (dot(back, high) + dot(back, mid)) + dot(back, last)


def halves_kernel(info, ins, outs, scratch):
    kept, came = ins
    for m, out in enumerate(outs):
        out[...] = (kept[m].astype(F32) + came[m].astype(F32)).astype(BF)


def join_kernel(info, ins, outs, scratch):
    out, = outs
    rows = ins[0].shape[0]
    for i, piece in enumerate(ins):
        out[i * rows : (i + 1) * rows, :] = piece[...]


def keys_and_values(rows, w_key, w_value, deps=()):
    width = rows.shape[1]
    chips = rows.shape[0] // (NPR * PR_DEV)
    many = 2
    block = many * NPR * PR_DEV
    steps = chips // many

    def kernel(rows_ref, w_key_ref, w_value_ref, *refs):
        k_ref, v_ref = refs[len(deps) :]
        values = rows_ref[...]
        k_ref[...] = dot(values, w_key_ref[...]).astype(BF).reshape(many, NPR, PR_DEV, width)
        v_ref[...] = dot(values, w_value_ref[...]).astype(BF).reshape(many, NPR, PR_DEV, width)

    weight = pl.BlockSpec((width, width), lambda i: (0, 0))
    out = pl.BlockSpec((many, NPR, PR_DEV, width), lambda i: (i, 0, 0, 0))
    return pl.pallas_call(
        kernel,
        grid=(steps,),
        in_specs=[pl.BlockSpec((block, width), lambda i: (i, 0)), weight, weight]
        + [pl.BlockSpec(memory_space=pl.ANY)] * len(deps),
        out_specs=[out, out],
        out_shape=[shape_of((chips, NPR, PR_DEV, width), BF)] * 2,
        compiler_params=pltpu.CompilerParams(vmem_limit_bytes=56 * MIB),
        cost_estimate=cost("keys_and_values"),
        name="keys_and_values",
    )(rows, w_key, w_value, *deps)


def shares_of(dk, dv, w_key, w_value):
    chips, width = dk.shape[0], w_key.shape[0]
    rows = chips * NPR * PR_DEV
    total = dot(dk.reshape(rows, width), w_key, NT) + dot(dv.reshape(rows, width), w_value, NT)
    return total.astype(BF).reshape(chips, NPR * PR_DEV, width)


def dense_gradients(info, hidden, rows, dq, dks, dvs, dkc, dvc, proj, few):
    width = hidden.shape[1]
    n_keys = len(rows)
    span = rows[0].shape[0]
    step = width // 3
    half = width // 2
    extra = few.shape[0]
    total = 4 * width + extra

    def kernel(info_ref, hidden_ref, *refs):
        row_refs = refs[:n_keys]
        dq_ref = refs[n_keys]
        dk_refs = refs[n_keys + 1 : 2 * n_keys + 1]
        dv_refs = refs[2 * n_keys + 1 : 3 * n_keys + 1]
        dkc_ref, dvc_ref, proj_ref, few_ref, mine, theirs = refs[3 * n_keys + 1 :]
        j = pl.program_id(0)
        core = info_ref[3]
        query = dot(hidden_ref[...], dq_ref[...], TN)
        both = dot(
            hidden_ref[NPR * PR_DEV :, :],
            jnp.concatenate([dkc_ref[...], dvc_ref[...]], axis=1),
            TN,
        )
        for row_ref, dk_ref, dv_ref in zip(row_refs, dk_refs, dv_refs):
            both = both + dot(
                row_ref[...],
                jnp.concatenate(
                    [dk_ref[...].reshape(span, step), dv_ref[...].reshape(span, step)], axis=1
                ),
                TN,
            )
        pieces = [
            query.astype(BF),
            both[:, :step].astype(BF),
            both[:, step:].astype(BF),
            proj_ref[...],
            few_ref[...],
        ]

        def put(out, at, start, size):
            row = 0
            for piece in pieces:
                out[row : row + piece.shape[0], at : at + size] = piece[:, start : start + size]
                row += piece.shape[0]

        rest = half - step
        for side, (low_out, high_out) in enumerate(((mine, theirs), (theirs, mine))):

            @pl.when(jnp.logical_and(core == side, j == 0))
            def _():
                put(low_out, 0, 0, step)

            @pl.when(jnp.logical_and(core == side, j == 1))
            def _():
                put(low_out, step, 0, rest)
                put(high_out, 0, rest, step - rest)

            @pl.when(jnp.logical_and(core == side, j == 2))
            def _():
                put(high_out, step - rest, 0, step)

    def const(shape):
        return pl.BlockSpec(shape, lambda j, info: (0,) * len(shape), pipeline_mode=pl.Buffered(1))

    def columns(rows_of):
        return pl.BlockSpec((rows_of, step), lambda j, info: (0, j))

    keys = pl.BlockSpec(dks[0].shape[:3] + (step,), lambda j, info: (0, 0, 0, j))
    out = pl.BlockSpec((total, half), lambda j, info: (0, 0))
    return pl.pallas_call(
        kernel,
        grid_spec=pltpu.PrefetchScalarGridSpec(
            num_scalar_prefetch=1,
            grid=(3,),
            in_specs=[const(hidden.shape)]
            + [const(r.shape) for r in rows]
            + [columns(dq.shape[0])]
            + [keys] * (2 * n_keys)
            + [columns(CLEN), columns(CLEN), columns(width), columns(extra)],
            out_specs=[out, out],
        ),
        out_shape=[shape_of((total, half), BF)] * 2,
        compiler_params=pltpu.CompilerParams(vmem_limit_bytes=60 * MIB),
        cost_estimate=cost("dense_gradients"),
        name="dense_gradients",
    )(info, hidden, *rows, dq, *dks, *dvs, dkc, dvc, proj, few)


def gelu_parts(a):
    square = a * a
    t = jnp.tanh(a * (0.7978845608 + (0.7978845608 * 0.044715) * square))
    half = 0.5 * a
    value = half + half * t
    slope = (0.5 + 0.5 * t) + half * (1.0 - t * t) * (
        0.7978845608 + (0.7978845608 * 3.0 * 0.044715) * square
    )
    return value, slope


def gather_rows(into, blocks, first, room):
    for m in range(blocks.shape[0]):
        into[m * room : (m + 1) * room, :] = blocks[m, pl.ds(pl.multiple_of(first, 16), room), :]


def other_column(others, blocks, first, room):
    at = blocks.shape[1] - TABLE
    span = min(blocks.shape[2], -(-at // 128) * 128)
    eye = iota((room, span), 1) == iota((room, span), 0) + first
    for m in range(blocks.shape[0]):
        row = blocks[m, at : at + TABLE, :span][:1].astype(F32)
        column = jnp.sum(jnp.where(eye, row, 0.0), axis=1, keepdims=True)
        others[m * room : (m + 1) * room, :] = jnp.broadcast_to(column, (room, 128))


def gated(rows, cots, others, w_router, mine):
    logits = dot(rows, w_router)
    column = iota(logits.shape, 1)
    own = jnp.sum(jnp.where(column == mine, logits, 0.0), axis=1, keepdims=True)
    other = others[:, : logits.shape[1]].astype(jnp.int32)
    theirs = jnp.sum(jnp.where(column == other, logits, 0.0), axis=1, keepdims=True)
    gate = 1.0 / (1.0 + jnp.exp(theirs - own))
    return (gate * cots.astype(F32)).astype(BF)


def expert_forward(x_slots, w_in, w_out, room, deps=()):
    devices, per, _ = x_slots.shape
    local, width, units = w_in.shape
    rows = devices * room
    chunk = min(units, 768)

    def kernel(x_ref, w_in_ref, w_out_ref, *refs):
        slope_ref, out, x = refs[len(deps) :]
        l = pl.program_id(0)
        gather_rows(x, x_ref, l * room, room)
        parts = [slice(at, at + chunk) for at in range(0, units, chunk)]
        pre = [dot(x[...], w_in_ref[0, :, part]) for part in parts]
        total = jnp.zeros((rows, width), F32)
        for part, act in zip(parts, pre):
            value, slope = gelu_parts(act)
            slope_ref[0, :, part] = slope.astype(BF)
            total = total + dot(value.astype(BF), w_out_ref[0, part, :])
        for m in range(devices):
            out[m, pl.ds(pl.multiple_of(l * room, 16), room), :] = total[
                m * room : (m + 1) * room, :
            ].astype(BF)

    slots = pl.BlockSpec(x_slots.shape, lambda l: (0, 0, 0))
    return pl.pallas_call(
        kernel,
        grid=(local,),
        in_specs=[
            slots,
            pl.BlockSpec((1, width, units), lambda l: (l, 0, 0)),
            pl.BlockSpec((1, units, width), lambda l: (l, 0, 0)),
        ]
        + [pl.BlockSpec(memory_space=pl.ANY)] * len(deps),
        out_specs=[pl.BlockSpec((1, rows, units), lambda l: (l, 0, 0)), slots],
        out_shape=[shape_of((local, rows, units), BF), shape_of(x_slots.shape, BF)],
        scratch_shapes=[pltpu.VMEM((rows, width), BF)],
        compiler_params=pltpu.CompilerParams(vmem_limit_bytes=56 * MIB),
        cost_estimate=cost("expert_forward"),
        name="expert_forward",
    )(x_slots, w_in, w_out, *deps)


def expert_backward(info, x_slots, c_slots, slope, w_router, w_in, w_out, room, deps=()):
    devices, per, _ = x_slots.shape
    local, width, units = w_in.shape
    rows = devices * room
    chunk = min(units, 768)

    def kernel(info_ref, x_ref, c_ref, router_ref, slope_ref, w_in_ref, w_out_ref, *refs):
        out, x, grad, others = refs[len(deps) :]
        l = pl.program_id(0)
        gather_rows(x, x_ref, l * room, room)
        gather_rows(grad, c_ref, l * room, room)
        other_column(others, c_ref, l * room, room)
        grad[...] = gated(
            x[...], grad[...], others[...], router_ref[...], info_ref[0] * local + l
        )
        parts = [slice(at, at + chunk) for at in range(0, units, chunk)]
        grad_act = [dot(grad[...], w_out_ref[0, part, :], NT) for part in parts]
        total = jnp.zeros((rows, width), F32)
        for part, act in zip(parts, grad_act):
            grad_pre = (act * slope_ref[0, :, part].astype(F32)).astype(BF)
            total = total + dot(grad_pre, w_in_ref[0, :, part], NT)
        for m in range(devices):
            out[m, pl.ds(pl.multiple_of(l * room, 16), room), :] = total[
                m * room : (m + 1) * room, :
            ].astype(BF)

    slots = pl.BlockSpec(x_slots.shape, lambda l, info: (0, 0, 0))
    return pl.pallas_call(
        kernel,
        grid_spec=pltpu.PrefetchScalarGridSpec(
            num_scalar_prefetch=1,
            grid=(local,),
            in_specs=[
                slots,
                pl.BlockSpec(c_slots.shape, lambda l, info: (0, 0, 0)),
                pl.BlockSpec(w_router.shape, lambda l, info: (0, 0)),
                pl.BlockSpec((1, rows, units), lambda l, info: (l, 0, 0)),
                pl.BlockSpec((1, width, units), lambda l, info: (l, 0, 0)),
                pl.BlockSpec((1, units, width), lambda l, info: (l, 0, 0)),
            ]
            + [pl.BlockSpec(memory_space=pl.ANY)] * len(deps),
            out_specs=slots,
            scratch_shapes=[
                pltpu.VMEM((rows, width), BF),
                pltpu.VMEM((rows, width), BF),
                pltpu.VMEM((rows, 128), F32),
            ],
        ),
        out_shape=shape_of(x_slots.shape, BF),
        compiler_params=pltpu.CompilerParams(vmem_limit_bytes=56 * MIB),
        cost_estimate=cost("expert_backward"),
        name="expert_backward",
    )(info, x_slots, c_slots, w_router, slope, w_in, w_out, *deps)


def expert_weights(info, groups, w_router, w_in, w_out, room, dp, before=None, last=False, deps=()):
    devices = groups[0][0].shape[0]
    local, width, units = w_in.shape
    part, share = units // dp, width // dp
    rows = devices * room
    flat, places = [], []
    for x, x_base, c, c_base in groups:
        at = []
        for array in (x, c):
            known = [i for i, other in enumerate(flat) if other is array]
            if not known:
                flat.append(array)
            at.append(known[0] if known else len(flat) - 1)
        places.append((at[0], x_base, at[1], c_base))
    n_flat = len(flat)
    sums = [] if before is None else list(before)

    def kernel(info_ref, *refs):
        slots = refs[:n_flat]
        router_ref, w_in_ref, w_out_ref = refs[n_flat : n_flat + 3]
        refs = refs[n_flat + 3 :]
        earlier = refs[: len(sums)]
        refs = refs[len(sums) + len(deps) :]
        out_ref, in_refs = refs[0], refs[1:-4]
        xs, grads, all_others, total = refs[-4:]
        l = pl.program_id(0)
        for g, (x_at, x_base, c_at, c_base) in enumerate(places):
            x, grad, others = xs.at[g], grads.at[g], all_others.at[g]
            gather_rows(x, slots[x_at], x_base + l * room, room)
            gather_rows(grad, slots[c_at], c_base + l * room, room)
            other_column(others, slots[c_at], c_base + l * room, room)
            grad[...] = gated(
                x[...], grad[...], others[...], router_ref[...], info_ref[0] * local + l
            )
            value, slope = gelu_parts(dot(x[...], w_in_ref[0]))
            grad_act = dot(grad[...], w_out_ref[0], NT)
            grad_pre = (grad_act * slope).astype(BF)
            part_in = dot(x[...], grad_pre, TN)
            part_out = dot(value.astype(BF), grad[...], TN)
            if g > 0:
                total[...] += part_in
                out_ref[0] += part_out
            elif earlier:
                total[...] = earlier[1][0] + part_in
                out_ref[0] = earlier[0][0] + part_out
            else:
                total[...] = part_in
                out_ref[0] = part_out
        if last:
            for k in range(dp):
                start = pl.multiple_of(jnp.bitwise_xor(info_ref[2], k) * share, 16)
                in_refs[k][0] = total[pl.ds(start, share), :].astype(BF)
        else:
            in_refs[0][0] = total[...]

    def const(shape):
        return pl.BlockSpec(shape, lambda l, info: (0,) * len(shape), pipeline_mode=pl.Buffered(1))

    square = pl.BlockSpec((1, part, width), lambda l, info: (l, 0, 0))
    square_in = pl.BlockSpec((1, width, part), lambda l, info: (l, 0, 0))
    if last:
        in_specs = [pl.BlockSpec((1, share, part), lambda l, info: (l, 0, 0))] * dp
        in_shapes = [shape_of((local, share, part), BF)] * dp
    else:
        in_specs = [square_in]
        in_shapes = [shape_of((local, width, part), F32)]
    got = pl.pallas_call(
        kernel,
        grid_spec=pltpu.PrefetchScalarGridSpec(
            num_scalar_prefetch=1,
            grid=(local,),
            in_specs=[const(x.shape) for x in flat]
            + [
                const(w_router.shape),
                pl.BlockSpec((1, width, part), lambda l, info: (l, 0, info[2])),
                pl.BlockSpec((1, part, width), lambda l, info: (l, info[2], 0)),
            ]
            + [square, square_in][: len(sums)]
            + [pl.BlockSpec(memory_space=pl.ANY)] * len(deps),
            out_specs=[square] + in_specs,
            scratch_shapes=[
                pltpu.VMEM((len(places), rows, width), BF),
                pltpu.VMEM((len(places), rows, width), BF),
                pltpu.VMEM((len(places), rows, 128), F32),
                pltpu.VMEM((width, part), F32),
            ],
        ),
        out_shape=[shape_of((local, part, width), F32)] + in_shapes,
        compiler_params=pltpu.CompilerParams(vmem_limit_bytes=60 * MIB),
        cost_estimate=cost("expert_weights_last" if last else "expert_weights"),
        name="expert_weights_last" if last else "expert_weights",
    )(info, *flat, w_router, w_in, w_out, *sums, *deps)
    return got[0], got[1:]


def columns_kernel(info, ins, outs, scratch):
    out, = outs
    part = ins[0].shape[2]
    for k, piece in enumerate(ins):
        start = pl.multiple_of(jnp.bitwise_xor(info[2], k) * part, 128)
        out[:, :, pl.ds(start, part)] = piece[...].astype(F32)


class Sums:
    def __init__(self, info, mine, theirs, n, dp, devices):
        self.info, self.n, self.dp, self.devices = info, n, dp, devices
        self.half = mine.shape[1]
        self.rows = self.width = 2 * self.half
        self.chips = devices // 2
        self.tall = self.rows // self.chips
        self.short = self.tall // dp
        self.extra = mine.shape[0] - n * self.rows
        self.value = mine
        self.came = swap(theirs, "expert", 1)

    @staticmethod
    def fits(rows, width, dp, devices):
        short = rows // (devices // 2) // dp
        return short % 16 == 0 and width % 256 == 0 and short * dp * (devices // 2) == rows

    def cores(self, deps=()):
        n, rows, tall, half, extra = self.n, self.rows, self.tall, self.half, self.extra

        def kernel(info_ref, ins, outs, scratch):
            kept, got = ins
            for m, out in enumerate(outs):
                for i in range(n):
                    start = i * rows + jnp.bitwise_xor(info_ref[4], m) * tall
                    at = pl.ds(pl.multiple_of(start, 16), tall)
                    out[i * tall : (i + 1) * tall, :] = (
                        kept[at, :].astype(F32) + got[at, :].astype(F32)
                    ).astype(BF)
                if extra:
                    out[n * tall :, :] = (
                        kept[n * rows :, :].astype(F32) + got[n * rows :, :].astype(F32)
                    ).astype(BF)

        pieces = run(
            kernel, "sum_cores", self.info, [self.value, self.came],
            [shape_of((n * tall + extra, half), BF)] * self.chips, deps=deps,
        )
        self.pieces = [pieces[0]] + [
            swap(pieces[m], "expert", 2 * m) for m in range(1, self.chips)
        ]
        return pieces[0]

    def planes(self, deps=()):
        n, tall, short, half, extra = self.n, self.tall, self.short, self.half, self.extra

        def kernel(info_ref, ins, outs, scratch):
            total, = scratch
            total[...] = added([piece[...].astype(F32) for piece in ins]).astype(BF)
            out, = outs
            for k in range(out.shape[0]):
                for i in range(n):
                    start = i * tall + k * short
                    out[k, i * short : (i + 1) * short, :] = total[start : start + short, :]
                if extra:
                    out[k, n * short :, :] = total[n * tall :, :]

        sent, = run(
            kernel, "sum_chips", self.info, self.pieces,
            [shape_of((self.dp, n * short + extra, half), BF)],
            scratch=[pltpu.VMEM((n * tall + extra, half), BF)], deps=deps,
        )
        self.pieces = lax.all_to_all(sent, "dp", split_axis=0, concat_axis=0, tiled=True)
        return sent

    def groups(self, beside, deps=()):
        n, short, half, extra, dp = self.n, self.short, self.half, self.extra, self.dp

        def kernel(info_ref, ins, outs, scratch):
            value = added([ins[0][k].astype(F32) for k in range(dp)]).astype(BF)
            for k in range(dp):
                outs[0][k] = value[: n * short]
            outs[1][...] = value[n * short :]

        own, self.few = run(
            kernel, "sum_groups", self.info, [self.pieces],
            [shape_of((dp, n * short, half), BF), shape_of((extra, half), BF)], deps=deps,
        )
        own, beside = lax.optimization_barrier((own, beside))
        self.own = lax.all_to_all(own, "dp", split_axis=0, concat_axis=0, tiled=True)
        return own, beside

    def gather(self):
        spread = self.own.reshape(self.dp * self.n * self.short, self.half)
        self.spread = jnp.concatenate(
            [spread] + [swap(spread, "expert", 2 * m) for m in range(1, self.chips)] + [self.few],
            axis=0,
        )
        self.other = swap(self.spread, "expert", 1)

    def finish(self, columns, gain, weights):
        got = self.put(0, self.spread, columns, gain, weights, ())
        return self.put(1, self.other, columns, gain, weights, got)

    def put(self, side, spread, columns, gain, weights, before):
        n, short, tall, half, extra = self.n, self.short, self.tall, self.half, self.extra
        chips, dp, rows, width = self.chips, self.dp, self.rows, self.width
        n_weights, n_before = len(weights), len(before)

        def kernel(info_ref, ref, gain_ref, *refs):
            weight_refs = refs[:n_weights]
            earlier = refs[n_weights : n_weights + n_before]
            outs = refs[n_weights + n_before :]
            for m in range(chips):
                for k in range(dp):
                    start = jnp.bitwise_xor(info_ref[4], m) * tall + k * short
                    at = pl.ds(pl.multiple_of(start, 16), short)
                    for i in range(n):
                        place = ((m * dp + k) * n + i) * short
                        outs[i][at, :] = ref[place : place + short, :].astype(F32)
            few = ref[chips * dp * n * short :, :].astype(F32)
            outs[n][...] = few[:columns, :].T
            outs[n + 1][...] = few[columns : columns + 1, :]
            along = gained(zip(weight_refs, outs), gain_ref[...])
            outs[n + 2][...] = earlier[-1][...] + along if earlier else along

        def half_of(block, axis):
            def index(i, info):
                core = jnp.bitwise_xor(info[3], side)
                return (core, 0) if axis == 0 else (0, core)

            return pl.BlockSpec(block, index)

        def const(shape):
            return pl.BlockSpec(shape, lambda i, info: (0, 0))

        square, row = half_of((rows, half), 1), const((1, width))
        outs = [shape_of((rows, width), F32)] * n
        outs = outs + [shape_of((width, columns), F32), shape_of((1, width), F32)]
        return pl.pallas_call(
            kernel,
            grid_spec=pltpu.PrefetchScalarGridSpec(
                num_scalar_prefetch=1,
                grid=(1,),
                in_specs=[const(spread.shape), row]
                + [square] * n_weights
                + [pl.BlockSpec(memory_space=pl.ANY)] * max(n_before - 1, 0)
                + [row] * min(n_before, 1),
                out_specs=[square] * n + [half_of((half, columns), 0), half_of((1, half), 1), row],
            ),
            out_shape=outs + [shape_of((1, width), F32)],
            input_output_aliases={3 + n_weights + i: i for i in range(n_before - 1)},
            compiler_params=pltpu.CompilerParams(vmem_limit_bytes=56 * MIB),
            cost_estimate=cost("spread_sums"),
            name="spread_sums",
        )(self.info, spread, gain, *weights, *before)


def gained(pairs, gain):
    total = 0.0
    for weight, grad in pairs:
        total = total + jnp.sum(weight[...].astype(F32) * grad[...], axis=1, keepdims=True)
    return jnp.broadcast_to(total, (total.shape[0], 128)).T[:1] / gain


def per_device(
    inputs,
    gain_one,
    w_query,
    w_key,
    w_value,
    w_out_proj,
    gain_two,
    w_router,
    w_in,
    w_out,
    routes,
    slot_index,
    prompt_of,
    cotangent,
):
    row_count, width = inputs.shape[1], inputs.shape[2]
    dp, devices = lax.axis_size("dp"), lax.axis_size("expert")
    z, device = lax.axis_index("dp"), lax.axis_index("expert")
    chips = devices // 2
    prompt_rows = NPR * PR_DEV
    expert_count, local = w_router.shape[1], w_in.shape[0]
    capacity = max(2, 5 * row_count * TOP // (4 * expert_count))
    room = -(-capacity // 16) * 16
    per = local * room
    info = jnp.stack(
        [device, prompt_of[0, 0], z, lax.rem(device, 2), lax.div(device, 2)]
    ).astype(jnp.int32)
    gain_one = gain_one[None, :]
    gain_two = gain_two[None, :]
    wide = shape_of((row_count, width), BF)
    wide32 = shape_of((row_count, width), F32)
    narrow = shape_of((row_count, 128), F32)
    x_shape = shape_of((devices, per, width), BF)
    c_shape = shape_of((devices, per + TABLE, width), BF)

    hidden_p, hidden, ordered = run(
        norm_kernel, "norm", info, [inputs[0], gain_one],
        [shape_of((prompt_rows, width), BF), wide, wide],
    )
    near = [hidden_p] + [swap(hidden_p, "expert", 2 * m) for m in range(1, chips)]

    message, cols, c_sent = run(
        table_kernel(per, room, capacity), "table", info,
        [cotangent[0], routes[0], slot_index[0]],
        [shape_of((row_count + TABLE, width), BF), narrow, c_shape],
        deps=[hidden_p],
    )
    hidden_c = hidden[prompt_rows:]
    queries = dot(hidden, w_query).astype(BF)
    key_c = dot(hidden_c, w_key).astype(BF)
    value_c = dot(hidden_c, w_value).astype(BF)
    near, cols, queries, key_c, value_c = lax.optimization_barrier(
        (near, cols, queries, key_c, value_c)
    )
    near, = run(join_kernel, "join", info, near, [shape_of((chips * prompt_rows, width), BF)])
    other = swap(near, "expert", 1)
    messages = far_groups(message, dp)
    c_sent, near = lax.optimization_barrier((c_sent, near))
    c_slots = [exchange(c_sent)]

    key_near, value_near = keys_and_values(near, w_key, w_value)
    key_other, value_other = keys_and_values(other, w_key, w_value, deps=[key_near])
    keys, values = [key_near, key_other], [value_near, value_other]
    attended, lse = attention_forward(info, queries, keys, values, key_c, value_c)
    c_slots, messages, attended = lax.optimization_barrier((c_slots, messages, attended))

    middle, second, gates, x_sent = run(
        middle_kernel(per), "middle", info,
        [ordered, attended, w_out_proj, gain_two, w_router, cols, message],
        [wide32, wide, narrow, x_shape],
    )
    x_slots = [exchange(x_sent)]
    seconds = far_groups(second, dp)
    slope, out_sent = expert_forward(x_slots[0], w_in, w_out, room)
    seconds, slope, c_slots[0], x_slots[0] = lax.optimization_barrier(
        (seconds, slope, c_slots[0], x_slots[0])
    )
    c_odd = [swap(c_slots[0], "dp", 1)]
    x_odd = [swap(x_slots[0], "dp", 1)]
    seconds = with_neighbours(seconds)
    messages = with_neighbours(messages)
    returned = exchange(out_sent)
    grad_sent = expert_backward(
        info, x_slots[0], c_slots[0], slope, w_router, w_in, w_out, room
    )
    returned, grad_sent = lax.optimization_barrier((returned, grad_sent))
    grad_returned = exchange(grad_sent)

    sums = expert_weights(
        info, [(x_slots[0], 0, c_slots[0], 0)], w_router, w_in, w_out, room, dp,
        deps=[grad_sent],
    )
    far = dp - 2
    rest, = run(
        dispatch_kernel(per), "dispatch", info, messages + seconds,
        [shape_of((devices, 2 * far * per + TABLE, width), BF)], deps=[sums[0]],
    )

    outputs, grad_middle, grad_attended, grad_proj, few, delta = run(
        combine_kernel(), "combine", info,
        [middle, second, gates, cols, message, attended, w_out_proj, w_router, gain_two]
        + [returned, grad_returned],
        [wide, wide32, wide, shape_of((width, width), BF), shape_of((expert_count + 16, width), BF),
         shape_of((width // PAIR, 3, TWO), F32)],
        deps=[rest],
    )
    rest = exchange(rest)

    pairs = width // PAIR

    def back(first, count, before=(), deps=()):
        return attention_backward(
            info, queries, keys, values, key_c, value_c, grad_attended, lse, delta, first, count,
            before=before, deps=deps,
        )

    got = back(0, pairs, deps=())
    grad_q, dk_near, dk_far, dv_near, dv_far, grad_kc, grad_vc = got
    grad_q, dk_near, dk_far, dv_near, dv_far, x_odd, c_odd = lax.optimization_barrier(
        (grad_q, dk_near, dk_far, dv_near, dv_far, x_odd, c_odd)
    )
    stepwise = Sums.fits(width, width, dp, devices)
    if stepwise:
        mine, theirs = dense_gradients(
            info, hidden, [near, other], grad_q, [dk_near, dk_far], [dv_near, dv_far],
            grad_kc, grad_vc, grad_proj, few,
        )
        total = Sums(info, mine, theirs, 4, dp, devices)
    else:
        flat = [part.reshape(chips * prompt_rows, width) for part in (dk_near, dk_far, dv_near, dv_far)]
        grad_query = dot(hidden, grad_q, TN)
        grad_key = dot(near, flat[0], TN) + dot(other, flat[1], TN) + dot(hidden_c, grad_kc, TN)
        grad_value = dot(near, flat[2], TN) + dot(other, flat[3], TN) + dot(hidden_c, grad_vc, TN)
        dense = [grad_query, grad_key, grad_value, grad_proj, few]

    sent = shares_of(dk_far, dv_far, w_key, w_value)
    kept = shares_of(dk_near, dv_near, w_key, w_value)
    came = swap(sent, "expert", 1)
    after = total.cores([kept]) if stepwise else kept
    shares = run(
        halves_kernel, "halves", info, [kept, came],
        [shape_of((prompt_rows, width), BF)] * chips, deps=[after],
    )

    others = [(x_odd[0], 0, c_odd[0], 0)]
    for g in range(far):
        others.append((rest, (far + g) * per, rest, g * per))
    grad_w_out, in_pieces = expert_weights(
        info, others, w_router, w_in, w_out, room, dp,
        before=(sums[0], sums[1][0]), last=True, deps=[shares[0]],
    )
    shares, in_pieces, grad_w_out = lax.optimization_barrier((shares, in_pieces, grad_w_out))
    after = [grad_w_out]
    if stepwise:
        after = [total.planes(after)]
    shares = [shares[0]] + [swap(shares[m], "expert", 2 * m) for m in range(1, chips)]
    if stepwise:
        own, shares = total.groups(shares, after)
        after = [own]
    grad_input, = run(
        input_kernel, "input", info,
        [grad_q, grad_kc, grad_vc, w_query, w_key, w_value, ordered, gain_one, grad_middle] + shares,
        [wide32], deps=after,
    )
    if stepwise:
        total.own, grad_input, in_pieces = lax.optimization_barrier(
            (total.own, grad_input, in_pieces)
        )
        total.gather()
    far_first = [swap(in_pieces[k], "dp", k) for k in range(dp - 1, 0, -1)]
    in_pieces = [in_pieces[0]] + far_first[::-1]
    after = []
    if stepwise:
        query_sum, key_sum, value_sum, proj_sum, grad_router, grad_gain_two, grad_gain_one = (
            total.finish(expert_count, gain_one, [w_query, w_key, w_value])
        )
        after = [query_sum]
    else:
        query_sum, key_sum, value_sum, proj_sum, few = lax.psum(
            [part.astype(F32) for part in dense], ("dp", "expert")
        )
        grad_router, grad_gain_two = few[:expert_count].T, few[expert_count :][:1]
        grad_gain_one = gained(
            [(w_query, query_sum), (w_key, key_sum), (w_value, value_sum)], gain_one
        )
    grad_w_in, = run(
        columns_kernel, "columns", info, in_pieces,
        [shape_of((local, width // dp, w_in.shape[2]), F32)], deps=after,
    )
    return (
        outputs[None],
        grad_input[None],
        grad_gain_one[0],
        query_sum,
        key_sum,
        value_sum,
        proj_sum,
        grad_gain_two[0],
        grad_router,
        grad_w_in,
        grad_w_out,
    )


def solution(mesh):
    return jax.shard_map(
        per_device,
        mesh=mesh,
        in_specs=(
            P("dp", "expert", None),
            P(),
            P(),
            P(),
            P(),
            P(),
            P(),
            P(),
            P("expert", None, None),
            P("expert", None, None),
            P("dp", "expert", None),
            P("dp", "expert", None),
            P("dp", "expert"),
            P("dp", "expert", None),
        ),
        out_specs=(
            P("dp", "expert", None),
            P("dp", "expert", None),
            P(),
            P(),
            P(),
            P(),
            P(),
            P(),
            P(),
            P("expert", "dp", None),
            P("expert", "dp", None),
        ),
        check_vma=False,
    )
```

```python
import jax
import jax.numpy as jnp
from jax import lax
from jax.experimental import pallas as pl
from jax.experimental.pallas import tpu as pltpu
from jax.sharding import PartitionSpec as P

H = 12
HD = 64
TOP = 2
NPR = 2
CLEN = 128
PR_DEV = 128
PAIR = 2 * HD
TWO = 2 * PR_DEV

NEGATIVE = -1e30
BF = jnp.bfloat16
F32 = jnp.float32
SCALE = HD ** (-0.5)
MIB = 1024 * 1024

NN = ((1,), (0,))
NT = ((1,), (1,))
TN = ((0,), (0,))

HIGH, LOW, ROUTE = 0, 2, 4
TABLE = 16


def dot(a, b, dims=NN):
    return lax.dot_general(a, b, (dims, ((), ())), preferred_element_type=F32)


def iota(shape, dim):
    return lax.broadcasted_iota(jnp.int32, shape, dim)


def shape_of(shape, dtype):
    return jax.ShapeDtypeStruct(shape, dtype)


WEIGHT = 1.0
TIMES = {
    "norm": 2.7,
    "table": 4.5,
    "attention_forward": 15.0,
    "middle": 5.1,
    "dispatch_cot": 7.0,
    "expert_forward": 20.0,
    "expert_backward": 20.0,
    "dispatch": 30.0,
    "expert_weights": 1.0,
    "combine": 3.0,
    "attention_backward": 15.0,
    "sum_cores": 0.3,
    "halves": 0.3,
    "expert_weights_last": 30.0,
    "sum_chips": 2.6,
    "sum_groups": 1.8,
    "input": 1.0,
    "spread_sums": 60.0,
    "columns": 1.0,
    "join": 2.0,
    "keys_and_values": 3.5,
    "dense_gradients": 60.0,
}


LARGE = ("middle", "dispatch_cot", "dispatch", "combine", "input")


def cost(name):
    flops = int(TIMES[name] * WEIGHT * 1.1e9)
    return pl.CostEstimate(flops=flops, bytes_accessed=0, transcendentals=0)


def run(kernel, name, info, operands, outs, deps=(), scratch=()):
    n_in, n_dep, n_out = len(operands), len(deps), len(outs)

    def body(info_ref, *refs):
        ins = refs[:n_in]
        results = refs[n_in + n_dep : n_in + n_dep + n_out]
        kernel(info_ref, ins, results, refs[n_in + n_dep + n_out :])

    vmem = pl.BlockSpec(memory_space=pltpu.VMEM)
    return pl.pallas_call(
        body,
        in_specs=[pl.BlockSpec(memory_space=pltpu.SMEM)]
        + [vmem] * n_in
        + [pl.BlockSpec(memory_space=pl.ANY)] * n_dep,
        out_specs=[vmem] * n_out,
        out_shape=list(outs),
        scratch_shapes=list(scratch),
        compiler_params=pltpu.CompilerParams(vmem_limit_bytes=(56 if name in LARGE else 24) * MIB),
        cost_estimate=cost(name),
        name=name,
    )(info, *operands, *deps)


def fill_bias(bias_ref, device, chips):
    for b in range(2 * chips):
        mask = 2 * (b % chips) + b // chips
        offset = (jnp.bitwise_xor(device, mask) - device) * PR_DEV
        seen = iota((PR_DEV, PR_DEV), 0) + offset <= iota((PR_DEV, PR_DEV), 1)
        bias_ref[b * PR_DEV : (b + 1) * PR_DEV, :] = jnp.where(seen, 0.0, NEGATIVE)


def two_heads(rows):
    keep = (iota((TWO, PAIR), 0) < PR_DEV) == (iota((TWO, PAIR), 1) < HD)
    return jnp.where(keep, jnp.concatenate([rows, rows], axis=0), jnp.zeros((), rows.dtype))


def join_heads(both):
    first = iota((PAIR, PR_DEV), 0) < HD
    return jnp.where(first, both[:, :PR_DEV], both[:, PR_DEV:]).T


def twice(block):
    return jnp.concatenate([block, block], axis=1)


def top_of(parts):
    top = jnp.max(parts[0], axis=0, keepdims=True)
    for part in parts[1:]:
        top = jnp.maximum(top, jnp.max(part, axis=0, keepdims=True))
    return top


def sum_of(parts):
    total = jnp.sum(parts[0], axis=0, keepdims=True)
    for part in parts[1:]:
        total = total + jnp.sum(part, axis=0, keepdims=True)
    return total


def added(parts):
    total = parts[0]
    for part in parts[1:]:
        total = total + part
    return total


def scores_of(keys, q2, bias_ref, group, span):
    parts = []
    for i, k in enumerate(keys):
        st = dot(k, q2, NT)
        if group < NPR:
            st = st + twice(bias_ref[i * span : (i + 1) * span, :])
        elif i == 2:
            st = st + twice(bias_ref[:PR_DEV, :])
        parts.append(st)
    return parts


def attention_forward_kernel(
    info, q_ref, ka_ref, kb_ref, va_ref, vb_ref, kc_ref, vc_ref, o_ref, lse_ref, bias_ref
):
    chips = ka_ref.shape[0]
    span = chips * PR_DEV
    device, chosen = info[0], info[1]

    @pl.when(pl.program_id(0) == 0)
    def _():
        fill_bias(bias_ref, device, chips)

    for group in range(3):
        rows = slice(group * PR_DEV, (group + 1) * PR_DEV)
        q2 = two_heads(q_ref[rows, :] * jnp.asarray(SCALE, BF))
        which = group if group < NPR else chosen
        keys = [ref[:, which].reshape(span, PAIR) for ref in (ka_ref, kb_ref)]
        values = [ref[:, which].reshape(span, PAIR) for ref in (va_ref, vb_ref)]
        if group == NPR:
            keys.append(kc_ref[...])
            values.append(vc_ref[...])
        scores = scores_of(keys, q2, bias_ref, group, span)
        top = top_of(scores)
        probs = [jnp.exp(st - top) for st in scores]
        total = sum_of(probs)
        both = added([dot(v, p.astype(BF), TN) for v, p in zip(values, probs)])
        both = both * (1.0 / total)
        o_ref[rows, :] = join_heads(both).astype(BF)
        lse_ref[0, group : group + 1, :] = top + jnp.log(total)


def attention_backward_kernel(
    info, q_ref, ka_ref, kb_ref, va_ref, vb_ref, kc_ref, vc_ref, do_ref, lse_ref, delta_ref,
    dq_ref, dka_ref, dkb_ref, dva_ref, dvb_ref, dkc_ref, dvc_ref, bias_ref, dk_acc, dv_acc,
):
    chips = ka_ref.shape[0]
    span = chips * PR_DEV
    device, chosen = info[0], info[1]

    @pl.when(pl.program_id(0) == 0)
    def _():
        fill_bias(bias_ref, device, chips)

    for group in range(3):
        rows = slice(group * PR_DEV, (group + 1) * PR_DEV)
        q2 = two_heads(q_ref[rows, :] * jnp.asarray(SCALE, BF))
        do2 = two_heads(do_ref[rows, :])
        lse = lse_ref[0, group : group + 1, :]
        which = group if group < NPR else chosen
        keys = [ref[:, which].reshape(span, PAIR) for ref in (ka_ref, kb_ref)]
        values = [ref[:, which].reshape(span, PAIR) for ref in (va_ref, vb_ref)]
        if group == NPR:
            keys.append(kc_ref[...])
            values.append(vc_ref[...])
        probs = [jnp.exp(st - lse) for st in scores_of(keys, q2, bias_ref, group, span)]
        grads = [dot(v, do2, NT) for v in values]
        delta = delta_ref[0, group : group + 1, :]
        ds = [(p * (g - delta)).astype(BF) for p, g in zip(probs, grads)]
        dq = added([dot(k, d, TN) for k, d in zip(keys, ds)])
        dq_ref[rows, :] = (join_heads(dq) * SCALE).astype(BF)
        for i in range(2):
            dk = dot(ds[i], q2).reshape(chips, PR_DEV, PAIR)
            dv = dot(probs[i].astype(BF), do2).reshape(chips, PR_DEV, PAIR)
            at = slice(i * chips, (i + 1) * chips)
            if group < NPR:
                dk_acc[at, group] = dk
                dv_acc[at, group] = dv
            else:
                dk_acc[at, chosen] += dk
                dv_acc[at, chosen] += dv
        if group == NPR:
            dkc_ref[...] = dot(ds[2], q2).astype(BF)
            dvc_ref[...] = dot(probs[2].astype(BF), do2).astype(BF)
    dka_ref[...] = dk_acc[:chips].astype(BF)
    dkb_ref[...] = dk_acc[chips:].astype(BF)
    dva_ref[...] = dv_acc[:chips].astype(BF)
    dvb_ref[...] = dv_acc[chips:].astype(BF)


def attention_specs(chips, rows, first=0):
    q_spec = pl.BlockSpec((rows, PAIR), lambda h, info: (0, first + h))
    k_spec = pl.BlockSpec((chips, NPR, PR_DEV, PAIR), lambda h, info: (0, 0, 0, first + h))
    c_spec = pl.BlockSpec((CLEN, PAIR), lambda h, info: (0, first + h))
    l_spec = pl.BlockSpec((1, 3, TWO), lambda h, info: (first + h, 0, 0))
    return q_spec, k_spec, c_spec, l_spec


def drop_refs(kernel, n_in, n_dep):
    def body(info, *refs):
        kernel(info, *refs[:n_in], *refs[n_in + n_dep :])

    return body


def attention_forward(info, q, keys, values, kc, vc, deps=()):
    k = keys[0]
    chips, rows, pairs = k.shape[0], q.shape[0], q.shape[1] // PAIR
    q_spec, k_spec, c_spec, l_spec = attention_specs(chips, rows)
    return pl.pallas_call(
        drop_refs(attention_forward_kernel, 7, len(deps)),
        grid_spec=pltpu.PrefetchScalarGridSpec(
            num_scalar_prefetch=1,
            grid=(pairs,),
            in_specs=[q_spec] + [k_spec] * 4 + [c_spec, c_spec]
            + [pl.BlockSpec(memory_space=pl.ANY)] * len(deps),
            out_specs=[q_spec, l_spec],
            scratch_shapes=[pltpu.VMEM((2 * chips * PR_DEV, PR_DEV), F32)],
        ),
        out_shape=[shape_of(q.shape, BF), shape_of((pairs, 3, TWO), F32)],
        compiler_params=pltpu.CompilerParams(vmem_limit_bytes=24 * MIB),
        cost_estimate=cost("attention_forward"),
        name="attention_forward",
    )(info, q, *keys, *values, kc, vc, *deps)


def attention_backward(info, q, keys, values, kc, vc, do, lse, delta, first, pairs, before=(), deps=()):
    k = keys[0]
    chips, rows = k.shape[0], q.shape[0]
    q_spec, k_spec, c_spec, l_spec = attention_specs(chips, rows, first)
    deps = list(before) + list(deps)
    return pl.pallas_call(
        drop_refs(attention_backward_kernel, 10, len(deps)),
        grid_spec=pltpu.PrefetchScalarGridSpec(
            num_scalar_prefetch=1,
            grid=(pairs,),
            in_specs=[q_spec] + [k_spec] * 4 + [c_spec, c_spec, q_spec, l_spec, l_spec]
            + [pl.BlockSpec(memory_space=pl.ANY)] * len(deps),
            out_specs=[q_spec] + [k_spec] * 4 + [c_spec, c_spec],
            scratch_shapes=[
                pltpu.VMEM((2 * chips * PR_DEV, PR_DEV), F32),
                pltpu.VMEM((2 * chips, NPR, PR_DEV, PAIR), F32),
                pltpu.VMEM((2 * chips, NPR, PR_DEV, PAIR), F32),
            ],
        ),
        out_shape=[shape_of(q.shape, BF)]
        + [shape_of(k.shape, BF)] * 4
        + [shape_of(kc.shape, BF)] * 2,
        input_output_aliases={11 + i: i for i in range(len(before))},
        compiler_params=pltpu.CompilerParams(vmem_limit_bytes=40 * MIB),
        cost_estimate=cost("attention_backward"),
        name="attention_backward",
    )(info, q, *keys, *values, kc, vc, do, lse, delta, *deps)


def swap(value, axis, mask):
    size = lax.axis_size(axis)
    return lax.ppermute(value, axis, [(i, i ^ mask) for i in range(size)])


def far_groups(own, dp):
    return [swap(own, "dp", m) for m in range(2, dp, 2)]


def with_neighbours(far):
    return [tokens for even in far for tokens in (even, swap(even, "dp", 1))]


def exchange(blocks):
    return lax.all_to_all(blocks, "expert", split_axis=0, concat_axis=0, tiled=True)


def root(values):
    return lax.rsqrt(jnp.mean(values * values, axis=-1, keepdims=True) + 1e-06)


def norm_back(norm, scale, grad):
    return scale * (grad - norm * jnp.mean(grad * norm, axis=-1, keepdims=True))


def source_row(row):
    inner = jnp.bitwise_and(row, PR_DEV - 1) * NPR + lax.shift_right_logical(row, 7)
    return jnp.where(row < NPR * PR_DEV, inner, row)


def order_matrix(n):
    return (source_row(iota((n, n), 0)) == iota((n, n), 1)).astype(BF)


def order_matrix_t(n):
    return (source_row(iota((n, n), 1)) == iota((n, n), 0)).astype(BF)


def norm_kernel(info, ins, outs, scratch):
    x, gain = ins
    prompt, hidden_ref, ordered = outs
    tokens = dot(order_matrix(x.shape[0]), x[...])
    hidden = (tokens * root(tokens) * gain[...]).astype(BF)
    prompt[...] = hidden[: NPR * PR_DEV]
    hidden_ref[...] = hidden
    ordered[...] = tokens.astype(BF)


def target(rows, k):
    return (rows[HIGH + k : HIGH + k + 1] * 16.0 + rows[LOW + k : LOW + k + 1]).astype(jnp.int32)


def picks_of(rows, slots):
    at = iota((slots, rows.shape[1]), 0)
    return [at == target(rows, k) for k in range(TOP)]


def low(mask):
    return jnp.where(mask, 1.0, 0.0).astype(BF)


def other_routes(rows, picks):
    low_rows = rows[:8].astype(BF)
    first = dot(low_rows, low(picks[0]), NT)[ROUTE + 1 : ROUTE + 2]
    return first + dot(low_rows, low(picks[1]), NT)[ROUTE : ROUTE + 1]


def send_slots(out, sent, per, at=0):
    for m in range(out.shape[0]):
        out[m, at : at + per, :] = sent[m * per : (m + 1) * per]


def clear_others(out):
    for m in range(out.shape[0]):
        out[m, out.shape[1] - TABLE :, :] = jnp.zeros((TABLE, out.shape[2]), BF)


def send_others(out, others, per, at=0):
    row = out.shape[1] - TABLE
    for m in range(out.shape[0]):
        out[m, row:, at : at + per] = jnp.broadcast_to(
            others[:, m * per : (m + 1) * per], (TABLE, per)
        ).astype(BF)


def table_kernel(per, room, capacity):
    def kernel(info, ins, outs, scratch):
        cot, route, slot = ins
        message, cols, out = outs
        n, width = cot.shape
        order = order_matrix(n)
        ordered = dot(order, cot[...]).astype(BF)
        r, s = route[...], slot[...]
        where = jnp.where(s < capacity, r * room + s, -16)
        high = lax.shift_right_arithmetic(where, 4).astype(F32)
        rest = jnp.bitwise_and(where, 15).astype(F32)
        r = r.astype(F32)
        lane = iota((n, 128), 1)
        table = jnp.zeros((n, 128), F32)
        for first, values in ((HIGH, high), (LOW, rest), (ROUTE, r)):
            for k in range(TOP):
                table = jnp.where(lane == first + k, values[:, k : k + 1], table)
        table = dot(order, table.astype(BF))
        cols[...] = table
        rows = table.T[:TABLE]
        message[:n, :] = ordered
        message[n:, :] = jnp.zeros((TABLE, width), BF)
        message[n:, :n] = rows.astype(BF)
        picks = picks_of(rows, per * out.shape[0])
        send_slots(out, dot(low(jnp.logical_or(*picks)), ordered).astype(BF), per)
        clear_others(out)
        send_others(out, other_routes(rows, picks), per)

    return kernel


def table_rows(message):
    n = message.shape[0] - TABLE
    return message[n:, :n].astype(F32)


def dispatch_cot_kernel(per):
    def kernel(info, ins, outs, scratch):
        out, = outs
        n = ins[0].shape[0] - TABLE
        clear_others(out)
        for g, message in enumerate(ins):
            rows = table_rows(message)
            picks = picks_of(rows, per * out.shape[0])
            sent = dot(low(jnp.logical_or(*picks)), message[:n, :]).astype(BF)
            send_slots(out, sent, per, g * per)
            send_others(out, other_routes(rows, picks), per, g * per)

    return kernel


def dispatch_kernel(per):
    def kernel(info, ins, outs, scratch):
        out, = outs
        groups = len(ins) // 2
        odd = groups // 2
        clear_others(out)
        for g in range(groups):
            message = ins[g]
            n = message.shape[0] - TABLE
            rows = table_rows(message)
            picks = picks_of(rows, per * out.shape[0])
            pick = low(jnp.logical_or(*picks))
            if g % 2:
                at = g // 2 * per
                send_slots(out, dot(pick, message[:n, :]).astype(BF), per, at)
                send_others(out, other_routes(rows, picks), per, at)
            sent = dot(pick, ins[groups + g][...]).astype(BF)
            send_slots(out, sent, per, (odd + g) * per)

    return kernel


def middle_kernel(per):
    def kernel(info, ins, outs, scratch):
        ordered, attended, w_out_proj, gain, w_router, cols, message = ins
        middle_ref, second_ref, gates_ref, out = outs
        middle = ordered[...].astype(F32) + dot(attended[...], w_out_proj[...])
        middle_ref[...] = middle
        second = (middle * root(middle) * gain[...]).astype(BF)
        second_ref[...] = second
        picks = picks_of(table_rows(message), per * out.shape[0])
        send_slots(out, dot(low(jnp.logical_or(*picks)), second).astype(BF), per)
        logits = dot(second, w_router[...])
        column = iota(logits.shape, 1).astype(F32)
        chosen = [
            jnp.sum(
                jnp.where(column == cols[:, ROUTE + k : ROUTE + k + 1], logits, 0.0),
                axis=1,
                keepdims=True,
            )
            for k in range(TOP)
        ]
        lane = iota(gates_ref.shape, 1)
        first = 1.0 / (1.0 + jnp.exp(chosen[1] - chosen[0]))
        then = 1.0 / (1.0 + jnp.exp(chosen[0] - chosen[1]))
        gates_ref[...] = jnp.where(lane == 0, first, then)

    return kernel


def combine_kernel():
    def kernel(info, ins, outs, scratch):
        middle_ref, second_ref, gates, cols, message, attended, w_out_proj, w_router, gain = ins[:9]
        came, came_grad = ins[9:]
        out_ref, grad_middle_ref, grad_attended_ref, grad_proj_ref, few_ref, delta_ref = outs
        n, width = middle_ref.shape
        slots = came.shape[0] * came.shape[1]
        middle, second = middle_ref[...], second_ref[...]
        cot = message[:n, :].astype(F32)
        table = cols[...]
        at = iota((n, slots), 1)
        picks = []
        for k in range(TOP):
            where = table[:, HIGH + k : HIGH + k + 1] * 16.0 + table[:, LOW + k : LOW + k + 1]
            picks.append(at == where.astype(jnp.int32))
        returned = came[...].reshape(slots, width)
        fetched = [dot(low(pick), returned) for pick in picks]
        gate = [gates[:, k : k + 1] for k in range(TOP)]
        outputs = (middle + (gate[0] * fetched[0] + gate[1] * fetched[1])).astype(BF)
        out_ref[...] = dot(order_matrix_t(n), outputs).astype(BF)
        grad_gate = [jnp.sum(cot * f, axis=1, keepdims=True) for f in fetched]
        mean_gate = gate[0] * grad_gate[0] + gate[1] * grad_gate[1]
        experts = w_router.shape[1]
        column = iota((n, experts), 1).astype(F32)
        grad_logits = jnp.zeros((n, experts), F32)
        for k in range(TOP):
            grad_logits = jnp.where(
                column == table[:, ROUTE + k : ROUTE + k + 1],
                gate[k] * (grad_gate[k] - mean_gate),
                grad_logits,
            )
        grad_logits = grad_logits.astype(BF)
        grad_second = dot(
            low(jnp.logical_or(*picks)), came_grad[...].reshape(slots, width)
        ) + dot(
            grad_logits, w_router[...], NT
        )
        scale = root(middle)
        norm = middle * scale
        few_ref[:experts, :] = dot(grad_logits, second, TN).astype(BF)
        few_ref[experts:, :] = jnp.broadcast_to(
            jnp.sum(grad_second * norm, axis=0, keepdims=True), (16, width)
        ).astype(BF)
        grad_middle = cot + norm_back(norm, scale, grad_second * gain[...])
        grad_middle_ref[...] = grad_middle
        grad_attn = grad_middle.astype(BF)
        grad_attended = dot(grad_attn, w_out_proj[...], NT).astype(BF)
        grad_attended_ref[...] = grad_attended
        product = grad_attended.astype(F32) * attended[...].astype(F32)
        high = product.astype(BF)
        heads = 2 * delta_ref.shape[0]
        head = low(lax.shift_right_logical(iota((16, width), 1), 6) == iota((16, width), 0))
        delta = dot(head, high, NT) + dot(head, (product - high.astype(F32)).astype(BF), NT)
        for h in range(heads):
            for group in range(3):
                delta_ref[h // 2, group : group + 1, h % 2 * PR_DEV : (h % 2 + 1) * PR_DEV] = delta[
                    h : h + 1, group * PR_DEV : (group + 1) * PR_DEV
                ]
        grad_proj_ref[...] = dot(attended[...], grad_attn, TN).astype(BF)

    return kernel


def input_kernel(info, ins, outs, scratch):
    grad_q, grad_kc, grad_vc, w_query, w_key, w_value, ordered, gain, grad_middle = ins[:9]
    parts = ins[9:]
    out, = outs
    shares = parts[0][...].astype(F32)
    for part in parts[1:]:
        shares = shares + part[...].astype(F32)
    grad_hidden = dot(grad_q[...], w_query[...], NT) + jnp.concatenate(
        [shares, dot(grad_kc[...], w_key[...], NT) + dot(grad_vc[...], w_value[...], NT)], axis=0
    )
    tokens = ordered[...].astype(F32)
    scale = root(tokens)
    grad = grad_middle[...] + norm_back(tokens * scale, scale, grad_hidden * gain[...])
    back = order_matrix_t(grad.shape[0])
    high = grad.astype(BF)
    rest = grad - high.astype(F32)
    mid = rest.astype(BF)
    last = (rest - mid.astype(F32)).astype(BF)
    out[...] = (dot(back, high) + dot(back, mid)) + dot(back, last)


def halves_kernel(info, ins, outs, scratch):
    kept, came = ins
    for m, out in enumerate(outs):
        out[...] = (kept[m].astype(F32) + came[m].astype(F32)).astype(BF)


def join_kernel(info, ins, outs, scratch):
    out, = outs
    rows = ins[0].shape[0]
    for i, piece in enumerate(ins):
        out[i * rows : (i + 1) * rows, :] = piece[...]


def keys_and_values(rows, w_key, w_value, deps=()):
    width = rows.shape[1]
    chips = rows.shape[0] // (NPR * PR_DEV)
    many = 2
    block = many * NPR * PR_DEV
    steps = chips // many

    def kernel(rows_ref, w_key_ref, w_value_ref, *refs):
        k_ref, v_ref = refs[len(deps) :]
        values = rows_ref[...]
        k_ref[...] = dot(values, w_key_ref[...]).astype(BF).reshape(many, NPR, PR_DEV, width)
        v_ref[...] = dot(values, w_value_ref[...]).astype(BF).reshape(many, NPR, PR_DEV, width)

    weight = pl.BlockSpec((width, width), lambda i: (0, 0))
    out = pl.BlockSpec((many, NPR, PR_DEV, width), lambda i: (i, 0, 0, 0))
    return pl.pallas_call(
        kernel,
        grid=(steps,),
        in_specs=[pl.BlockSpec((block, width), lambda i: (i, 0)), weight, weight]
        + [pl.BlockSpec(memory_space=pl.ANY)] * len(deps),
        out_specs=[out, out],
        out_shape=[shape_of((chips, NPR, PR_DEV, width), BF)] * 2,
        compiler_params=pltpu.CompilerParams(vmem_limit_bytes=16 * MIB),
        cost_estimate=cost("keys_and_values"),
        name="keys_and_values",
    )(rows, w_key, w_value, *deps)


def shares_of(dk, dv, w_key, w_value):
    chips, width = dk.shape[0], w_key.shape[0]
    rows = chips * NPR * PR_DEV
    total = dot(dk.reshape(rows, width), w_key, NT) + dot(dv.reshape(rows, width), w_value, NT)
    return total.astype(BF).reshape(chips, NPR * PR_DEV, width)


def dense_gradients(info, hidden, rows, dq, dks, dvs, dkc, dvc, proj, few):
    width = hidden.shape[1]
    n_keys = len(rows)
    span = rows[0].shape[0]
    step = width // 3
    half = width // 2
    extra = few.shape[0]
    total = 4 * width + extra

    def kernel(info_ref, hidden_ref, *refs):
        row_refs = refs[:n_keys]
        dq_ref = refs[n_keys]
        dk_refs = refs[n_keys + 1 : 2 * n_keys + 1]
        dv_refs = refs[2 * n_keys + 1 : 3 * n_keys + 1]
        dkc_ref, dvc_ref, proj_ref, few_ref, mine, theirs = refs[3 * n_keys + 1 :]
        j = pl.program_id(0)
        core = info_ref[3]
        query = dot(hidden_ref[...], dq_ref[...], TN)
        both = dot(
            hidden_ref[NPR * PR_DEV :, :],
            jnp.concatenate([dkc_ref[...], dvc_ref[...]], axis=1),
            TN,
        )
        for row_ref, dk_ref, dv_ref in zip(row_refs, dk_refs, dv_refs):
            both = both + dot(
                row_ref[...],
                jnp.concatenate(
                    [dk_ref[...].reshape(span, step), dv_ref[...].reshape(span, step)], axis=1
                ),
                TN,
            )
        pieces = [
            query.astype(BF),
            both[:, :step].astype(BF),
            both[:, step:].astype(BF),
            proj_ref[...],
            few_ref[...],
        ]

        def put(out, at, start, size):
            row = 0
            for piece in pieces:
                out[row : row + piece.shape[0], at : at + size] = piece[:, start : start + size]
                row += piece.shape[0]

        rest = half - step
        for side, (low_out, high_out) in enumerate(((mine, theirs), (theirs, mine))):

            @pl.when(jnp.logical_and(core == side, j == 0))
            def _():
                put(low_out, 0, 0, step)

            @pl.when(jnp.logical_and(core == side, j == 1))
            def _():
                put(low_out, step, 0, rest)
                put(high_out, 0, rest, step - rest)

            @pl.when(jnp.logical_and(core == side, j == 2))
            def _():
                put(high_out, step - rest, 0, step)

    def const(shape):
        return pl.BlockSpec(shape, lambda j, info: (0,) * len(shape), pipeline_mode=pl.Buffered(1))

    def columns(rows_of):
        return pl.BlockSpec((rows_of, step), lambda j, info: (0, j))

    keys = pl.BlockSpec(dks[0].shape[:3] + (step,), lambda j, info: (0, 0, 0, j))
    out = pl.BlockSpec((total, half), lambda j, info: (0, 0))
    return pl.pallas_call(
        kernel,
        grid_spec=pltpu.PrefetchScalarGridSpec(
            num_scalar_prefetch=1,
            grid=(3,),
            in_specs=[const(hidden.shape)]
            + [const(r.shape) for r in rows]
            + [columns(dq.shape[0])]
            + [keys] * (2 * n_keys)
            + [columns(CLEN), columns(CLEN), columns(width), columns(extra)],
            out_specs=[out, out],
        ),
        out_shape=[shape_of((total, half), BF)] * 2,
        compiler_params=pltpu.CompilerParams(vmem_limit_bytes=60 * MIB),
        cost_estimate=cost("dense_gradients"),
        name="dense_gradients",
    )(info, hidden, *rows, dq, *dks, *dvs, dkc, dvc, proj, few)


def gelu_parts(a):
    square = a * a
    t = jnp.tanh(a * (0.7978845608 + (0.7978845608 * 0.044715) * square))
    half = 0.5 + 0.5 * t
    value = a * half
    slope = half + value * (1.0 - t) * (0.7978845608 + (0.7978845608 * 3.0 * 0.044715) * square)
    return value, slope


def gather_rows(into, blocks, first, room):
    for m in range(blocks.shape[0]):
        into[m * room : (m + 1) * room, :] = blocks[m, pl.ds(pl.multiple_of(first, 16), room), :]


def other_column(others, blocks, first, room):
    at = blocks.shape[1] - TABLE
    span = min(blocks.shape[2], -(-at // 128) * 128)
    eye = iota((room, span), 1) == iota((room, span), 0) + first
    for m in range(blocks.shape[0]):
        row = blocks[m, at : at + TABLE, :span][:1].astype(F32)
        column = jnp.sum(jnp.where(eye, row, 0.0), axis=1, keepdims=True)
        others[m * room : (m + 1) * room, :] = jnp.broadcast_to(column, (room, 128))


def gated(rows, cots, others, w_router, mine):
    logits = dot(rows, w_router)
    column = iota(logits.shape, 1)
    own = jnp.sum(jnp.where(column == mine, logits, 0.0), axis=1, keepdims=True)
    other = others[:, : logits.shape[1]].astype(jnp.int32)
    theirs = jnp.sum(jnp.where(column == other, logits, 0.0), axis=1, keepdims=True)
    gate = 1.0 / (1.0 + jnp.exp(theirs - own))
    return (gate * cots.astype(F32)).astype(BF)


def expert_forward(x_slots, w_in, w_out, room, deps=()):
    devices, per, _ = x_slots.shape
    local, width, units = w_in.shape
    rows = devices * room
    chunk = min(units, 768)

    def kernel(x_ref, w_in_ref, w_out_ref, *refs):
        slope_ref, out, x = refs[len(deps) :]
        l = pl.program_id(0)
        gather_rows(x, x_ref, l * room, room)
        parts = [slice(at, at + chunk) for at in range(0, units, chunk)]
        pre = [dot(x[...], w_in_ref[0, :, part]) for part in parts]
        total = jnp.zeros((rows, width), F32)
        for part, act in zip(parts, pre):
            value, slope = gelu_parts(act)
            slope_ref[0, :, part] = slope.astype(BF)
            total = total + dot(value.astype(BF), w_out_ref[0, part, :])
        for m in range(devices):
            out[m, pl.ds(pl.multiple_of(l * room, 16), room), :] = total[
                m * room : (m + 1) * room, :
            ].astype(BF)

    slots = pl.BlockSpec(x_slots.shape, lambda l: (0, 0, 0))
    return pl.pallas_call(
        kernel,
        grid=(local,),
        in_specs=[
            slots,
            pl.BlockSpec((1, width, units), lambda l: (l, 0, 0)),
            pl.BlockSpec((1, units, width), lambda l: (l, 0, 0)),
        ]
        + [pl.BlockSpec(memory_space=pl.ANY)] * len(deps),
        out_specs=[pl.BlockSpec((1, rows, units), lambda l: (l, 0, 0)), slots],
        out_shape=[shape_of((local, rows, units), BF), shape_of(x_slots.shape, BF)],
        scratch_shapes=[pltpu.VMEM((rows, width), BF)],
        compiler_params=pltpu.CompilerParams(vmem_limit_bytes=48 * MIB),
        cost_estimate=cost("expert_forward"),
        name="expert_forward",
    )(x_slots, w_in, w_out, *deps)


def expert_backward(info, x_slots, c_slots, slope, w_router, w_in, w_out, room, deps=()):
    devices, per, _ = x_slots.shape
    local, width, units = w_in.shape
    rows = devices * room
    chunk = min(units, 768)

    def kernel(info_ref, x_ref, c_ref, router_ref, slope_ref, w_in_ref, w_out_ref, *refs):
        out, x, grad, others = refs[len(deps) :]
        l = pl.program_id(0)
        gather_rows(x, x_ref, l * room, room)
        gather_rows(grad, c_ref, l * room, room)
        other_column(others, c_ref, l * room, room)
        grad[...] = gated(
            x[...], grad[...], others[...], router_ref[...], info_ref[0] * local + l
        )
        parts = [slice(at, at + chunk) for at in range(0, units, chunk)]
        grad_act = [dot(grad[...], w_out_ref[0, part, :], NT) for part in parts]
        total = jnp.zeros((rows, width), F32)
        for part, act in zip(parts, grad_act):
            grad_pre = (act * slope_ref[0, :, part].astype(F32)).astype(BF)
            total = total + dot(grad_pre, w_in_ref[0, :, part], NT)
        for m in range(devices):
            out[m, pl.ds(pl.multiple_of(l * room, 16), room), :] = total[
                m * room : (m + 1) * room, :
            ].astype(BF)

    slots = pl.BlockSpec(x_slots.shape, lambda l, info: (0, 0, 0))
    return pl.pallas_call(
        kernel,
        grid_spec=pltpu.PrefetchScalarGridSpec(
            num_scalar_prefetch=1,
            grid=(local,),
            in_specs=[
                slots,
                pl.BlockSpec(c_slots.shape, lambda l, info: (0, 0, 0)),
                pl.BlockSpec(w_router.shape, lambda l, info: (0, 0)),
                pl.BlockSpec((1, rows, units), lambda l, info: (l, 0, 0)),
                pl.BlockSpec((1, width, units), lambda l, info: (l, 0, 0)),
                pl.BlockSpec((1, units, width), lambda l, info: (l, 0, 0)),
            ]
            + [pl.BlockSpec(memory_space=pl.ANY)] * len(deps),
            out_specs=slots,
            scratch_shapes=[
                pltpu.VMEM((rows, width), BF),
                pltpu.VMEM((rows, width), BF),
                pltpu.VMEM((rows, 128), F32),
            ],
        ),
        out_shape=shape_of(x_slots.shape, BF),
        compiler_params=pltpu.CompilerParams(vmem_limit_bytes=48 * MIB),
        cost_estimate=cost("expert_backward"),
        name="expert_backward",
    )(info, x_slots, c_slots, w_router, slope, w_in, w_out, *deps)


def expert_weights(info, groups, w_router, w_in, w_out, room, dp, before=None, last=False, deps=()):
    devices = groups[0][0].shape[0]
    local, width, units = w_in.shape
    part, share = units // dp, width // dp
    rows = devices * room
    flat, places = [], []
    for x, x_base, c, c_base in groups:
        at = []
        for array in (x, c):
            known = [i for i, other in enumerate(flat) if other is array]
            if not known:
                flat.append(array)
            at.append(known[0] if known else len(flat) - 1)
        places.append((at[0], x_base, at[1], c_base))
    n_flat = len(flat)
    sums = [] if before is None else list(before)

    def kernel(info_ref, *refs):
        slots = refs[:n_flat]
        router_ref, w_in_ref, w_out_ref = refs[n_flat : n_flat + 3]
        refs = refs[n_flat + 3 :]
        earlier = refs[: len(sums)]
        refs = refs[len(sums) + len(deps) :]
        out_ref, in_refs = refs[0], refs[1:-4]
        xs, grads, all_others, total = refs[-4:]
        l = pl.program_id(0)
        for g, (x_at, x_base, c_at, c_base) in enumerate(places):
            x, grad, others = xs.at[g], grads.at[g], all_others.at[g]
            gather_rows(x, slots[x_at], x_base + l * room, room)
            gather_rows(grad, slots[c_at], c_base + l * room, room)
            other_column(others, slots[c_at], c_base + l * room, room)
            grad[...] = gated(
                x[...], grad[...], others[...], router_ref[...], info_ref[0] * local + l
            )
            value, slope = gelu_parts(dot(x[...], w_in_ref[0]))
            grad_act = dot(grad[...], w_out_ref[0], NT)
            grad_pre = (grad_act * slope).astype(BF)
            part_in = dot(x[...], grad_pre, TN)
            part_out = dot(value.astype(BF), grad[...], TN)
            if g > 0:
                total[...] += part_in
                out_ref[0] += part_out
            elif earlier:
                total[...] = earlier[1][0] + part_in
                out_ref[0] = earlier[0][0] + part_out
            else:
                total[...] = part_in
                out_ref[0] = part_out
        if last:
            for k in range(dp):
                start = pl.multiple_of(jnp.bitwise_xor(info_ref[2], k) * share, 16)
                in_refs[k][0] = total[pl.ds(start, share), :].astype(BF)
        else:
            in_refs[0][0] = total[...]

    def const(shape):
        return pl.BlockSpec(shape, lambda l, info: (0,) * len(shape), pipeline_mode=pl.Buffered(1))

    square = pl.BlockSpec((1, part, width), lambda l, info: (l, 0, 0))
    square_in = pl.BlockSpec((1, width, part), lambda l, info: (l, 0, 0))
    if last:
        in_specs = [pl.BlockSpec((1, share, part), lambda l, info: (l, 0, 0))] * dp
        in_shapes = [shape_of((local, share, part), BF)] * dp
    else:
        in_specs = [square_in]
        in_shapes = [shape_of((local, width, part), F32)]
    got = pl.pallas_call(
        kernel,
        grid_spec=pltpu.PrefetchScalarGridSpec(
            num_scalar_prefetch=1,
            grid=(local,),
            in_specs=[const(x.shape) for x in flat]
            + [
                const(w_router.shape),
                pl.BlockSpec((1, width, part), lambda l, info: (l, 0, info[2])),
                pl.BlockSpec((1, part, width), lambda l, info: (l, info[2], 0)),
            ]
            + [square, square_in][: len(sums)]
            + [pl.BlockSpec(memory_space=pl.ANY)] * len(deps),
            out_specs=[square] + in_specs,
            scratch_shapes=[
                pltpu.VMEM((len(places), rows, width), BF),
                pltpu.VMEM((len(places), rows, width), BF),
                pltpu.VMEM((len(places), rows, 128), F32),
                pltpu.VMEM((width, part), F32),
            ],
        ),
        out_shape=[shape_of((local, part, width), F32)] + in_shapes,
        compiler_params=pltpu.CompilerParams(vmem_limit_bytes=60 * MIB),
        cost_estimate=cost("expert_weights_last" if last else "expert_weights"),
        name="expert_weights_last" if last else "expert_weights",
    )(info, *flat, w_router, w_in, w_out, *sums, *deps)
    return got[0], got[1:]


def columns_kernel(info, ins, outs, scratch):
    out, = outs
    part = ins[0].shape[2]
    for k, piece in enumerate(ins):
        start = pl.multiple_of(jnp.bitwise_xor(info[2], k) * part, 128)
        out[:, :, pl.ds(start, part)] = piece[...].astype(F32)


class Sums:
    def __init__(self, info, mine, theirs, n, dp, devices):
        self.info, self.n, self.dp, self.devices = info, n, dp, devices
        self.half = mine.shape[1]
        self.rows = self.width = 2 * self.half
        self.chips = devices // 2
        self.tall = self.rows // self.chips
        self.short = self.tall // dp
        self.extra = mine.shape[0] - n * self.rows
        self.value = mine
        self.came = swap(theirs, "expert", 1)

    @staticmethod
    def fits(rows, width, dp, devices):
        short = rows // (devices // 2) // dp
        return short % 16 == 0 and width % 256 == 0 and short * dp * (devices // 2) == rows

    def cores(self, deps=()):
        n, rows, tall, half, extra = self.n, self.rows, self.tall, self.half, self.extra

        def kernel(info_ref, ins, outs, scratch):
            kept, got = ins
            for m, out in enumerate(outs):
                for i in range(n):
                    start = i * rows + jnp.bitwise_xor(info_ref[4], m) * tall
                    at = pl.ds(pl.multiple_of(start, 16), tall)
                    out[i * tall : (i + 1) * tall, :] = (
                        kept[at, :].astype(F32) + got[at, :].astype(F32)
                    ).astype(BF)
                if extra:
                    out[n * tall :, :] = (
                        kept[n * rows :, :].astype(F32) + got[n * rows :, :].astype(F32)
                    ).astype(BF)

        pieces = run(
            kernel, "sum_cores", self.info, [self.value, self.came],
            [shape_of((n * tall + extra, half), BF)] * self.chips, deps=deps,
        )
        self.pieces = [pieces[0]] + [
            swap(pieces[m], "expert", 2 * m) for m in range(1, self.chips)
        ]
        return pieces[0]

    def planes(self, deps=()):
        n, tall, short, half, extra = self.n, self.tall, self.short, self.half, self.extra

        def kernel(info_ref, ins, outs, scratch):
            total, = scratch
            total[...] = added([piece[...].astype(F32) for piece in ins]).astype(BF)
            out, = outs
            for k in range(out.shape[0]):
                for i in range(n):
                    start = i * tall + k * short
                    out[k, i * short : (i + 1) * short, :] = total[start : start + short, :]
                if extra:
                    out[k, n * short :, :] = total[n * tall :, :]

        sent, = run(
            kernel, "sum_chips", self.info, self.pieces,
            [shape_of((self.dp, n * short + extra, half), BF)],
            scratch=[pltpu.VMEM((n * tall + extra, half), BF)], deps=deps,
        )
        self.pieces = lax.all_to_all(sent, "dp", split_axis=0, concat_axis=0, tiled=True)
        return sent

    def groups(self, beside, deps=()):
        n, short, half, extra, dp = self.n, self.short, self.half, self.extra, self.dp

        def kernel(info_ref, ins, outs, scratch):
            value = added([ins[0][k].astype(F32) for k in range(dp)]).astype(BF)
            for k in range(dp):
                outs[0][k] = value[: n * short]
            outs[1][...] = value[n * short :]

        own, self.few = run(
            kernel, "sum_groups", self.info, [self.pieces],
            [shape_of((dp, n * short, half), BF), shape_of((extra, half), BF)], deps=deps,
        )
        own, beside = lax.optimization_barrier((own, beside))
        self.own = lax.all_to_all(own, "dp", split_axis=0, concat_axis=0, tiled=True)
        return own, beside

    def gather(self):
        spread = self.own.reshape(self.dp * self.n * self.short, self.half)
        self.spread = jnp.concatenate(
            [spread] + [swap(spread, "expert", 2 * m) for m in range(1, self.chips)] + [self.few],
            axis=0,
        )
        self.other = swap(self.spread, "expert", 1)

    def finish(self, columns, gain, weights):
        got = self.put(0, self.spread, columns, gain, weights, ())
        return self.put(1, self.other, columns, gain, weights, got)

    def put(self, side, spread, columns, gain, weights, before):
        n, short, tall, half, extra = self.n, self.short, self.tall, self.half, self.extra
        chips, dp, rows, width = self.chips, self.dp, self.rows, self.width
        n_weights, n_before = len(weights), len(before)

        def kernel(info_ref, ref, gain_ref, *refs):
            weight_refs = refs[:n_weights]
            earlier = refs[n_weights : n_weights + n_before]
            outs = refs[n_weights + n_before :]
            for m in range(chips):
                for k in range(dp):
                    start = jnp.bitwise_xor(info_ref[4], m) * tall + k * short
                    at = pl.ds(pl.multiple_of(start, 16), short)
                    for i in range(n):
                        place = ((m * dp + k) * n + i) * short
                        outs[i][at, :] = ref[place : place + short, :].astype(F32)
            few = ref[chips * dp * n * short :, :].astype(F32)
            outs[n][...] = few[:columns, :].T
            outs[n + 1][...] = few[columns : columns + 1, :]
            along = gained(zip(weight_refs, outs), gain_ref[...])
            outs[n + 2][...] = earlier[-1][...] + along if earlier else along

        def half_of(block, axis):
            def index(i, info):
                core = jnp.bitwise_xor(info[3], side)
                return (core, 0) if axis == 0 else (0, core)

            return pl.BlockSpec(block, index)

        def const(shape):
            return pl.BlockSpec(shape, lambda i, info: (0, 0))

        square, row = half_of((rows, half), 1), const((1, width))
        outs = [shape_of((rows, width), F32)] * n
        outs = outs + [shape_of((width, columns), F32), shape_of((1, width), F32)]
        return pl.pallas_call(
            kernel,
            grid_spec=pltpu.PrefetchScalarGridSpec(
                num_scalar_prefetch=1,
                grid=(1,),
                in_specs=[const(spread.shape), row]
                + [square] * n_weights
                + [pl.BlockSpec(memory_space=pl.ANY)] * max(n_before - 1, 0)
                + [row] * min(n_before, 1),
                out_specs=[square] * n + [half_of((half, columns), 0), half_of((1, half), 1), row],
            ),
            out_shape=outs + [shape_of((1, width), F32)],
            input_output_aliases={3 + n_weights + i: i for i in range(n_before - 1)},
            compiler_params=pltpu.CompilerParams(vmem_limit_bytes=24 * MIB),
            cost_estimate=cost("spread_sums"),
            name="spread_sums",
        )(self.info, spread, gain, *weights, *before)


def gained(pairs, gain):
    total = 0.0
    for weight, grad in pairs:
        total = total + jnp.sum(weight[...].astype(F32) * grad[...], axis=1, keepdims=True)
    return jnp.broadcast_to(total, (total.shape[0], 128)).T[:1] / gain


def per_device(
    inputs,
    gain_one,
    w_query,
    w_key,
    w_value,
    w_out_proj,
    gain_two,
    w_router,
    w_in,
    w_out,
    routes,
    slot_index,
    prompt_of,
    cotangent,
):
    row_count, width = inputs.shape[1], inputs.shape[2]
    dp, devices = lax.axis_size("dp"), lax.axis_size("expert")
    z, device = lax.axis_index("dp"), lax.axis_index("expert")
    chips = devices // 2
    prompt_rows = NPR * PR_DEV
    expert_count, local = w_router.shape[1], w_in.shape[0]
    capacity = max(2, 5 * row_count * TOP // (4 * expert_count))
    room = -(-capacity // 16) * 16
    per = local * room
    info = jnp.stack(
        [device, prompt_of[0, 0], z, lax.rem(device, 2), lax.div(device, 2)]
    ).astype(jnp.int32)
    gain_one = gain_one[None, :]
    gain_two = gain_two[None, :]
    wide = shape_of((row_count, width), BF)
    wide32 = shape_of((row_count, width), F32)
    narrow = shape_of((row_count, 128), F32)
    x_shape = shape_of((devices, per, width), BF)
    c_shape = shape_of((devices, per + TABLE, width), BF)

    hidden_p, hidden, ordered = run(
        norm_kernel, "norm", info, [inputs[0], gain_one],
        [shape_of((prompt_rows, width), BF), wide, wide],
    )
    near = [hidden_p] + [swap(hidden_p, "expert", 2 * m) for m in range(1, chips)]

    message, cols, c_sent = run(
        table_kernel(per, room, capacity), "table", info,
        [cotangent[0], routes[0], slot_index[0]],
        [shape_of((row_count + TABLE, width), BF), narrow, c_shape],
        deps=[hidden_p],
    )
    hidden_c = hidden[prompt_rows:]
    queries = dot(hidden, w_query).astype(BF)
    key_c = dot(hidden_c, w_key).astype(BF)
    value_c = dot(hidden_c, w_value).astype(BF)
    near, cols, queries, key_c, value_c = lax.optimization_barrier(
        (near, cols, queries, key_c, value_c)
    )
    near, = run(join_kernel, "join", info, near, [shape_of((chips * prompt_rows, width), BF)])
    other = swap(near, "expert", 1)
    messages = far_groups(message, dp)
    c_sent, near = lax.optimization_barrier((c_sent, near))
    c_slots = [exchange(c_sent)]

    key_near, value_near = keys_and_values(near, w_key, w_value)
    key_other, value_other = keys_and_values(other, w_key, w_value, deps=[key_near])
    keys, values = [key_near, key_other], [value_near, value_other]
    attended, lse = attention_forward(info, queries, keys, values, key_c, value_c)
    c_slots, messages, attended = lax.optimization_barrier((c_slots, messages, attended))

    middle, second, gates, x_sent = run(
        middle_kernel(per), "middle", info,
        [ordered, attended, w_out_proj, gain_two, w_router, cols, message],
        [wide32, wide, narrow, x_shape],
    )
    x_slots = [exchange(x_sent)]
    seconds = far_groups(second, dp)
    c_rest = run(
        dispatch_cot_kernel(per), "dispatch_cot", info, messages,
        [shape_of((devices, len(messages) * per + TABLE, width), BF)], deps=[middle],
    )
    x_slots, c_rest = lax.optimization_barrier((x_slots, c_rest))
    c_even, = [exchange(sent) for sent in c_rest]

    slope, out_sent = expert_forward(x_slots[0], w_in, w_out, room)
    seconds, slope, c_slots[0], x_slots[0] = lax.optimization_barrier(
        (seconds, slope, c_slots[0], x_slots[0])
    )
    c_odd = [swap(c_slots[0], "dp", 1)]
    x_odd = [swap(x_slots[0], "dp", 1)]
    seconds = with_neighbours(seconds)
    messages = with_neighbours(messages)
    returned = exchange(out_sent)
    grad_sent = expert_backward(
        info, x_slots[0], c_slots[0], slope, w_router, w_in, w_out, room, deps=[c_even]
    )
    returned, grad_sent = lax.optimization_barrier((returned, grad_sent))
    grad_returned = exchange(grad_sent)

    sums = expert_weights(
        info, [(x_slots[0], 0, c_slots[0], 0)], w_router, w_in, w_out, room, dp,
        deps=[grad_sent],
    )
    far = dp - 2
    odd = far // 2
    rest, = run(
        dispatch_kernel(per), "dispatch", info, messages + seconds,
        [shape_of((devices, (odd + far) * per + TABLE, width), BF)], deps=[sums[0]],
    )

    outputs, grad_middle, grad_attended, grad_proj, few, delta = run(
        combine_kernel(), "combine", info,
        [middle, second, gates, cols, message, attended, w_out_proj, w_router, gain_two]
        + [returned, grad_returned],
        [wide, wide32, wide, shape_of((width, width), BF), shape_of((expert_count + 16, width), BF),
         shape_of((width // PAIR, 3, TWO), F32)],
        deps=[rest],
    )
    rest = exchange(rest)

    pairs = width // PAIR

    def back(first, count, before=(), deps=()):
        return attention_backward(
            info, queries, keys, values, key_c, value_c, grad_attended, lse, delta, first, count,
            before=before, deps=deps,
        )

    got = back(0, pairs, deps=())
    grad_q, dk_near, dk_far, dv_near, dv_far, grad_kc, grad_vc = got
    grad_q, dk_near, dk_far, dv_near, dv_far, x_odd, c_odd = lax.optimization_barrier(
        (grad_q, dk_near, dk_far, dv_near, dv_far, x_odd, c_odd)
    )
    stepwise = Sums.fits(width, width, dp, devices)
    if stepwise:
        mine, theirs = dense_gradients(
            info, hidden, [near, other], grad_q, [dk_near, dk_far], [dv_near, dv_far],
            grad_kc, grad_vc, grad_proj, few,
        )
        total = Sums(info, mine, theirs, 4, dp, devices)
    else:
        flat = [part.reshape(chips * prompt_rows, width) for part in (dk_near, dk_far, dv_near, dv_far)]
        grad_query = dot(hidden, grad_q, TN)
        grad_key = dot(near, flat[0], TN) + dot(other, flat[1], TN) + dot(hidden_c, grad_kc, TN)
        grad_value = dot(near, flat[2], TN) + dot(other, flat[3], TN) + dot(hidden_c, grad_vc, TN)
        dense = [grad_query, grad_key, grad_value, grad_proj, few]

    sent = shares_of(dk_far, dv_far, w_key, w_value)
    kept = shares_of(dk_near, dv_near, w_key, w_value)
    came = swap(sent, "expert", 1)
    after = total.cores([kept]) if stepwise else kept
    shares = run(
        halves_kernel, "halves", info, [kept, came],
        [shape_of((prompt_rows, width), BF)] * chips, deps=[after],
    )

    others = [(x_odd[0], 0, c_odd[0], 0)]
    for g in range(far):
        c_from, c_base = (rest, g // 2 * per) if g % 2 else (c_even, g // 2 * per)
        others.append((rest, (odd + g) * per, c_from, c_base))
    grad_w_out, in_pieces = expert_weights(
        info, others, w_router, w_in, w_out, room, dp,
        before=(sums[0], sums[1][0]), last=True, deps=[shares[0]],
    )
    shares, in_pieces, grad_w_out = lax.optimization_barrier((shares, in_pieces, grad_w_out))
    after = [grad_w_out]
    if stepwise:
        after = [total.planes(after)]
    shares = [shares[0]] + [swap(shares[m], "expert", 2 * m) for m in range(1, chips)]
    if stepwise:
        own, shares = total.groups(shares, after)
        after = [own]
    grad_input, = run(
        input_kernel, "input", info,
        [grad_q, grad_kc, grad_vc, w_query, w_key, w_value, ordered, gain_one, grad_middle] + shares,
        [wide32], deps=after,
    )
    if stepwise:
        total.own, grad_input, in_pieces = lax.optimization_barrier(
            (total.own, grad_input, in_pieces)
        )
        total.gather()
    far_first = [swap(in_pieces[k], "dp", k) for k in range(dp - 1, 0, -1)]
    in_pieces = [in_pieces[0]] + far_first[::-1]
    after = []
    if stepwise:
        query_sum, key_sum, value_sum, proj_sum, grad_router, grad_gain_two, grad_gain_one = (
            total.finish(expert_count, gain_one, [w_query, w_key, w_value])
        )
        after = [query_sum]
    else:
        query_sum, key_sum, value_sum, proj_sum, few = lax.psum(
            [part.astype(F32) for part in dense], ("dp", "expert")
        )
        grad_router, grad_gain_two = few[:expert_count].T, few[expert_count :][:1]
        grad_gain_one = gained(
            [(w_query, query_sum), (w_key, key_sum), (w_value, value_sum)], gain_one
        )
    grad_w_in, = run(
        columns_kernel, "columns", info, in_pieces,
        [shape_of((local, width // dp, w_in.shape[2]), F32)], deps=after,
    )
    return (
        outputs[None],
        grad_input[None],
        grad_gain_one[0],
        query_sum,
        key_sum,
        value_sum,
        proj_sum,
        grad_gain_two[0],
        grad_router,
        grad_w_in,
        grad_w_out,
    )


def solution(mesh):
    return jax.shard_map(
        per_device,
        mesh=mesh,
        in_specs=(
            P("dp", "expert", None),
            P(),
            P(),
            P(),
            P(),
            P(),
            P(),
            P(),
            P("expert", None, None),
            P("expert", None, None),
            P("dp", "expert", None),
            P("dp", "expert", None),
            P("dp", "expert"),
            P("dp", "expert", None),
        ),
        out_specs=(
            P("dp", "expert", None),
            P("dp", "expert", None),
            P(),
            P(),
            P(),
            P(),
            P(),
            P(),
            P(),
            P("expert", "dp", None),
            P("expert", "dp", None),
        ),
        check_vma=False,
    )
```

```python
import jax
import jax.numpy as jnp
from jax import lax
from jax.experimental import pallas as pl
from jax.experimental.pallas import tpu as pltpu
from jax.sharding import PartitionSpec as P

H = 12
HD = 64
TOP = 2
NPR = 2
CLEN = 128
PR_DEV = 128
PAIR = 2 * HD
TWO = 2 * PR_DEV

NEGATIVE = -1e30
BF = jnp.bfloat16
F32 = jnp.float32
SCALE = HD ** (-0.5)
MIB = 1024 * 1024

NN = ((1,), (0,))
NT = ((1,), (1,))
TN = ((0,), (0,))

HIGH, LOW, ROUTE = 0, 2, 4
TABLE = 16


def dot(a, b, dims=NN):
    return lax.dot_general(a, b, (dims, ((), ())), preferred_element_type=F32)


def iota(shape, dim):
    return lax.broadcasted_iota(jnp.int32, shape, dim)


def shape_of(shape, dtype):
    return jax.ShapeDtypeStruct(shape, dtype)


WEIGHT = 1.0
TIMES = {
    "norm": 2.7,
    "table": 4.5,
    "attention_forward": 15.0,
    "middle": 5.1,
    "dispatch_cot": 7.0,
    "expert_forward": 20.0,
    "expert_backward": 20.0,
    "dispatch": 30.0,
    "expert_weights": 1.0,
    "combine": 3.0,
    "attention_backward": 15.0,
    "sum_cores": 0.3,
    "halves": 0.3,
    "expert_weights_last": 30.0,
    "sum_chips": 2.6,
    "sum_groups": 1.8,
    "input": 1.0,
    "spread_sums": 60.0,
    "columns": 1.0,
    "join": 2.0,
    "keys_and_values": 3.5,
    "dense_gradients": 60.0,
}


LARGE = ("middle", "dispatch_cot", "dispatch", "combine", "input")


def cost(name):
    flops = int(TIMES[name] * WEIGHT * 1.1e9)
    return pl.CostEstimate(flops=flops, bytes_accessed=0, transcendentals=0)


def run(kernel, name, info, operands, outs, deps=(), scratch=()):
    n_in, n_dep, n_out = len(operands), len(deps), len(outs)

    def body(info_ref, *refs):
        ins = refs[:n_in]
        results = refs[n_in + n_dep : n_in + n_dep + n_out]
        kernel(info_ref, ins, results, refs[n_in + n_dep + n_out :])

    vmem = pl.BlockSpec(memory_space=pltpu.VMEM)
    return pl.pallas_call(
        body,
        in_specs=[pl.BlockSpec(memory_space=pltpu.SMEM)]
        + [vmem] * n_in
        + [pl.BlockSpec(memory_space=pl.ANY)] * n_dep,
        out_specs=[vmem] * n_out,
        out_shape=list(outs),
        scratch_shapes=list(scratch),
        compiler_params=pltpu.CompilerParams(vmem_limit_bytes=(56 if name in LARGE else 24) * MIB),
        cost_estimate=cost(name),
        name=name,
    )(info, *operands, *deps)


def fill_bias(bias_ref, device, chips):
    for b in range(2 * chips):
        mask = 2 * (b % chips) + b // chips
        offset = (jnp.bitwise_xor(device, mask) - device) * PR_DEV
        seen = iota((PR_DEV, PR_DEV), 0) + offset <= iota((PR_DEV, PR_DEV), 1)
        bias_ref[b * PR_DEV : (b + 1) * PR_DEV, :] = jnp.where(seen, 0.0, NEGATIVE)


def two_heads(rows):
    keep = (iota((TWO, PAIR), 0) < PR_DEV) == (iota((TWO, PAIR), 1) < HD)
    return jnp.where(keep, jnp.concatenate([rows, rows], axis=0), jnp.zeros((), rows.dtype))


def join_heads(both):
    first = iota((PAIR, PR_DEV), 0) < HD
    return jnp.where(first, both[:, :PR_DEV], both[:, PR_DEV:]).T


def twice(block):
    return jnp.concatenate([block, block], axis=1)


def top_of(parts):
    top = jnp.max(parts[0], axis=0, keepdims=True)
    for part in parts[1:]:
        top = jnp.maximum(top, jnp.max(part, axis=0, keepdims=True))
    return top


def sum_of(parts):
    total = jnp.sum(parts[0], axis=0, keepdims=True)
    for part in parts[1:]:
        total = total + jnp.sum(part, axis=0, keepdims=True)
    return total


def added(parts):
    total = parts[0]
    for part in parts[1:]:
        total = total + part
    return total


def scores_of(keys, q2, bias_ref, group, span):
    parts = []
    for i, k in enumerate(keys):
        st = dot(k, q2, NT)
        if group < NPR:
            st = st + twice(bias_ref[i * span : (i + 1) * span, :])
        elif i == 2:
            st = st + twice(bias_ref[:PR_DEV, :])
        parts.append(st)
    return parts


def attention_forward_kernel(
    info, q_ref, ka_ref, kb_ref, va_ref, vb_ref, kc_ref, vc_ref, o_ref, lse_ref, bias_ref
):
    chips = ka_ref.shape[0]
    span = chips * PR_DEV
    device, chosen = info[0], info[1]

    @pl.when(pl.program_id(0) == 0)
    def _():
        fill_bias(bias_ref, device, chips)

    for group in range(3):
        rows = slice(group * PR_DEV, (group + 1) * PR_DEV)
        q2 = two_heads(q_ref[rows, :] * jnp.asarray(SCALE, BF))
        which = group if group < NPR else chosen
        keys = [ref[:, which].reshape(span, PAIR) for ref in (ka_ref, kb_ref)]
        values = [ref[:, which].reshape(span, PAIR) for ref in (va_ref, vb_ref)]
        if group == NPR:
            keys.append(kc_ref[...])
            values.append(vc_ref[...])
        scores = scores_of(keys, q2, bias_ref, group, span)
        top = top_of(scores)
        probs = [jnp.exp(st - top) for st in scores]
        total = sum_of(probs)
        both = added([dot(v, p.astype(BF), TN) for v, p in zip(values, probs)])
        both = both * (1.0 / total)
        o_ref[rows, :] = join_heads(both).astype(BF)
        lse_ref[0, group : group + 1, :] = top + jnp.log(total)


def attention_backward_kernel(
    info, q_ref, ka_ref, kb_ref, va_ref, vb_ref, kc_ref, vc_ref, do_ref, lse_ref, delta_ref,
    dq_ref, dka_ref, dkb_ref, dva_ref, dvb_ref, dkc_ref, dvc_ref, bias_ref, dk_acc, dv_acc,
):
    chips = ka_ref.shape[0]
    span = chips * PR_DEV
    device, chosen = info[0], info[1]

    @pl.when(pl.program_id(0) == 0)
    def _():
        fill_bias(bias_ref, device, chips)

    for group in range(3):
        rows = slice(group * PR_DEV, (group + 1) * PR_DEV)
        q2 = two_heads(q_ref[rows, :] * jnp.asarray(SCALE, BF))
        do2 = two_heads(do_ref[rows, :])
        lse = lse_ref[0, group : group + 1, :]
        which = group if group < NPR else chosen
        keys = [ref[:, which].reshape(span, PAIR) for ref in (ka_ref, kb_ref)]
        values = [ref[:, which].reshape(span, PAIR) for ref in (va_ref, vb_ref)]
        if group == NPR:
            keys.append(kc_ref[...])
            values.append(vc_ref[...])
        probs = [jnp.exp(st - lse) for st in scores_of(keys, q2, bias_ref, group, span)]
        grads = [dot(v, do2, NT) for v in values]
        delta = delta_ref[0, group : group + 1, :]
        ds = [(p * (g - delta)).astype(BF) for p, g in zip(probs, grads)]
        dq = added([dot(k, d, TN) for k, d in zip(keys, ds)])
        dq_ref[rows, :] = (join_heads(dq) * SCALE).astype(BF)
        for i in range(2):
            dk = dot(ds[i], q2).reshape(chips, PR_DEV, PAIR)
            dv = dot(probs[i].astype(BF), do2).reshape(chips, PR_DEV, PAIR)
            at = slice(i * chips, (i + 1) * chips)
            if group < NPR:
                dk_acc[at, group] = dk
                dv_acc[at, group] = dv
            else:
                dk_acc[at, chosen] += dk
                dv_acc[at, chosen] += dv
        if group == NPR:
            dkc_ref[...] = dot(ds[2], q2).astype(BF)
            dvc_ref[...] = dot(probs[2].astype(BF), do2).astype(BF)
    dka_ref[...] = dk_acc[:chips].astype(BF)
    dkb_ref[...] = dk_acc[chips:].astype(BF)
    dva_ref[...] = dv_acc[:chips].astype(BF)
    dvb_ref[...] = dv_acc[chips:].astype(BF)


def attention_specs(chips, rows, first=0):
    q_spec = pl.BlockSpec((rows, PAIR), lambda h, info: (0, first + h))
    k_spec = pl.BlockSpec((chips, NPR, PR_DEV, PAIR), lambda h, info: (0, 0, 0, first + h))
    c_spec = pl.BlockSpec((CLEN, PAIR), lambda h, info: (0, first + h))
    l_spec = pl.BlockSpec((1, 3, TWO), lambda h, info: (first + h, 0, 0))
    return q_spec, k_spec, c_spec, l_spec


def drop_refs(kernel, n_in, n_dep):
    def body(info, *refs):
        kernel(info, *refs[:n_in], *refs[n_in + n_dep :])

    return body


def attention_forward(info, q, keys, values, kc, vc, deps=()):
    k = keys[0]
    chips, rows, pairs = k.shape[0], q.shape[0], q.shape[1] // PAIR
    q_spec, k_spec, c_spec, l_spec = attention_specs(chips, rows)
    return pl.pallas_call(
        drop_refs(attention_forward_kernel, 7, len(deps)),
        grid_spec=pltpu.PrefetchScalarGridSpec(
            num_scalar_prefetch=1,
            grid=(pairs,),
            in_specs=[q_spec] + [k_spec] * 4 + [c_spec, c_spec]
            + [pl.BlockSpec(memory_space=pl.ANY)] * len(deps),
            out_specs=[q_spec, l_spec],
            scratch_shapes=[pltpu.VMEM((2 * chips * PR_DEV, PR_DEV), F32)],
        ),
        out_shape=[shape_of(q.shape, BF), shape_of((pairs, 3, TWO), F32)],
        compiler_params=pltpu.CompilerParams(vmem_limit_bytes=24 * MIB),
        cost_estimate=cost("attention_forward"),
        name="attention_forward",
    )(info, q, *keys, *values, kc, vc, *deps)


def attention_backward(info, q, keys, values, kc, vc, do, lse, delta, first, pairs, before=(), deps=()):
    k = keys[0]
    chips, rows = k.shape[0], q.shape[0]
    q_spec, k_spec, c_spec, l_spec = attention_specs(chips, rows, first)
    deps = list(before) + list(deps)
    return pl.pallas_call(
        drop_refs(attention_backward_kernel, 10, len(deps)),
        grid_spec=pltpu.PrefetchScalarGridSpec(
            num_scalar_prefetch=1,
            grid=(pairs,),
            in_specs=[q_spec] + [k_spec] * 4 + [c_spec, c_spec, q_spec, l_spec, l_spec]
            + [pl.BlockSpec(memory_space=pl.ANY)] * len(deps),
            out_specs=[q_spec] + [k_spec] * 4 + [c_spec, c_spec],
            scratch_shapes=[
                pltpu.VMEM((2 * chips * PR_DEV, PR_DEV), F32),
                pltpu.VMEM((2 * chips, NPR, PR_DEV, PAIR), F32),
                pltpu.VMEM((2 * chips, NPR, PR_DEV, PAIR), F32),
            ],
        ),
        out_shape=[shape_of(q.shape, BF)]
        + [shape_of(k.shape, BF)] * 4
        + [shape_of(kc.shape, BF)] * 2,
        input_output_aliases={11 + i: i for i in range(len(before))},
        compiler_params=pltpu.CompilerParams(vmem_limit_bytes=60 * MIB),
        cost_estimate=cost("attention_backward"),
        name="attention_backward",
    )(info, q, *keys, *values, kc, vc, do, lse, delta, *deps)


def swap(value, axis, mask):
    size = lax.axis_size(axis)
    return lax.ppermute(value, axis, [(i, i ^ mask) for i in range(size)])


def far_groups(own, dp):
    return [swap(own, "dp", m) for m in range(2, dp, 2)]


def with_neighbours(far):
    return [tokens for even in far for tokens in (even, swap(even, "dp", 1))]


def exchange(blocks):
    return lax.all_to_all(blocks, "expert", split_axis=0, concat_axis=0, tiled=True)


def root(values):
    return lax.rsqrt(jnp.mean(values * values, axis=-1, keepdims=True) + 1e-06)


def norm_back(norm, scale, grad):
    return scale * (grad - norm * jnp.mean(grad * norm, axis=-1, keepdims=True))


def source_row(row):
    inner = jnp.bitwise_and(row, PR_DEV - 1) * NPR + lax.shift_right_logical(row, 7)
    return jnp.where(row < NPR * PR_DEV, inner, row)


def order_matrix(n):
    return (source_row(iota((n, n), 0)) == iota((n, n), 1)).astype(BF)


def order_matrix_t(n):
    return (source_row(iota((n, n), 1)) == iota((n, n), 0)).astype(BF)


def norm_kernel(info, ins, outs, scratch):
    x, gain = ins
    prompt, hidden_ref, ordered = outs
    tokens = dot(order_matrix(x.shape[0]), x[...])
    hidden = (tokens * root(tokens) * gain[...]).astype(BF)
    prompt[...] = hidden[: NPR * PR_DEV]
    hidden_ref[...] = hidden
    ordered[...] = tokens.astype(BF)


def target(rows, k):
    return (rows[HIGH + k : HIGH + k + 1] * 16.0 + rows[LOW + k : LOW + k + 1]).astype(jnp.int32)


def picks_of(rows, slots):
    at = iota((slots, rows.shape[1]), 0)
    return [at == target(rows, k) for k in range(TOP)]


def low(mask):
    return jnp.where(mask, 1.0, 0.0).astype(BF)


def other_routes(rows, picks):
    low_rows = rows[:8].astype(BF)
    first = dot(low_rows, low(picks[0]), NT)[ROUTE + 1 : ROUTE + 2]
    return first + dot(low_rows, low(picks[1]), NT)[ROUTE : ROUTE + 1]


def send_slots(out, sent, per, at=0):
    for m in range(out.shape[0]):
        out[m, at : at + per, :] = sent[m * per : (m + 1) * per]


def clear_others(out):
    for m in range(out.shape[0]):
        out[m, out.shape[1] - TABLE :, :] = jnp.zeros((TABLE, out.shape[2]), BF)


def send_others(out, others, per, at=0):
    row = out.shape[1] - TABLE
    for m in range(out.shape[0]):
        out[m, row:, at : at + per] = jnp.broadcast_to(
            others[:, m * per : (m + 1) * per], (TABLE, per)
        ).astype(BF)


def table_kernel(per, room, capacity):
    def kernel(info, ins, outs, scratch):
        cot, route, slot = ins
        message, cols, out = outs
        n, width = cot.shape
        order = order_matrix(n)
        ordered = dot(order, cot[...]).astype(BF)
        r, s = route[...], slot[...]
        where = jnp.where(s < capacity, r * room + s, -16)
        high = lax.shift_right_arithmetic(where, 4).astype(F32)
        rest = jnp.bitwise_and(where, 15).astype(F32)
        r = r.astype(F32)
        lane = iota((n, 128), 1)
        table = jnp.zeros((n, 128), F32)
        for first, values in ((HIGH, high), (LOW, rest), (ROUTE, r)):
            for k in range(TOP):
                table = jnp.where(lane == first + k, values[:, k : k + 1], table)
        table = dot(order, table.astype(BF))
        cols[...] = table
        rows = table.T[:TABLE]
        message[:n, :] = ordered
        message[n:, :] = jnp.zeros((TABLE, width), BF)
        message[n:, :n] = rows.astype(BF)
        picks = picks_of(rows, per * out.shape[0])
        send_slots(out, dot(low(jnp.logical_or(*picks)), ordered).astype(BF), per)
        clear_others(out)
        send_others(out, other_routes(rows, picks), per)

    return kernel


def table_rows(message):
    n = message.shape[0] - TABLE
    return message[n:, :n].astype(F32)


def dispatch_cot_kernel(per):
    def kernel(info, ins, outs, scratch):
        out, = outs
        n = ins[0].shape[0] - TABLE
        clear_others(out)
        for g, message in enumerate(ins):
            rows = table_rows(message)
            picks = picks_of(rows, per * out.shape[0])
            sent = dot(low(jnp.logical_or(*picks)), message[:n, :]).astype(BF)
            send_slots(out, sent, per, g * per)
            send_others(out, other_routes(rows, picks), per, g * per)

    return kernel


def dispatch_kernel(per):
    def kernel(info, ins, outs, scratch):
        out, = outs
        groups = len(ins) // 2
        odd = groups // 2
        clear_others(out)
        for g in range(groups):
            message = ins[g]
            n = message.shape[0] - TABLE
            rows = table_rows(message)
            picks = picks_of(rows, per * out.shape[0])
            pick = low(jnp.logical_or(*picks))
            if g % 2:
                at = g // 2 * per
                send_slots(out, dot(pick, message[:n, :]).astype(BF), per, at)
                send_others(out, other_routes(rows, picks), per, at)
            sent = dot(pick, ins[groups + g][...]).astype(BF)
            send_slots(out, sent, per, (odd + g) * per)

    return kernel


def middle_kernel(per):
    def kernel(info, ins, outs, scratch):
        ordered, attended, w_out_proj, gain, w_router, cols, message = ins
        middle_ref, second_ref, gates_ref, out = outs
        middle = ordered[...].astype(F32) + dot(attended[...], w_out_proj[...])
        middle_ref[...] = middle
        second = (middle * root(middle) * gain[...]).astype(BF)
        second_ref[...] = second
        picks = picks_of(table_rows(message), per * out.shape[0])
        send_slots(out, dot(low(jnp.logical_or(*picks)), second).astype(BF), per)
        logits = dot(second, w_router[...])
        column = iota(logits.shape, 1).astype(F32)
        chosen = [
            jnp.sum(
                jnp.where(column == cols[:, ROUTE + k : ROUTE + k + 1], logits, 0.0),
                axis=1,
                keepdims=True,
            )
            for k in range(TOP)
        ]
        lane = iota(gates_ref.shape, 1)
        first = 1.0 / (1.0 + jnp.exp(chosen[1] - chosen[0]))
        then = 1.0 / (1.0 + jnp.exp(chosen[0] - chosen[1]))
        gates_ref[...] = jnp.where(lane == 0, first, then)

    return kernel


def combine_kernel():
    def kernel(info, ins, outs, scratch):
        middle_ref, second_ref, gates, cols, message, attended, w_out_proj, w_router, gain = ins[:9]
        came, came_grad = ins[9:]
        out_ref, grad_middle_ref, grad_attended_ref, grad_proj_ref, few_ref, delta_ref = outs
        n, width = middle_ref.shape
        slots = came.shape[0] * came.shape[1]
        middle, second = middle_ref[...], second_ref[...]
        cot = message[:n, :].astype(F32)
        table = cols[...]
        at = iota((n, slots), 1)
        picks = []
        for k in range(TOP):
            where = table[:, HIGH + k : HIGH + k + 1] * 16.0 + table[:, LOW + k : LOW + k + 1]
            picks.append(at == where.astype(jnp.int32))
        returned = came[...].reshape(slots, width)
        fetched = [dot(low(pick), returned) for pick in picks]
        gate = [gates[:, k : k + 1] for k in range(TOP)]
        outputs = (middle + (gate[0] * fetched[0] + gate[1] * fetched[1])).astype(BF)
        out_ref[...] = dot(order_matrix_t(n), outputs).astype(BF)
        grad_gate = [jnp.sum(cot * f, axis=1, keepdims=True) for f in fetched]
        mean_gate = gate[0] * grad_gate[0] + gate[1] * grad_gate[1]
        experts = w_router.shape[1]
        column = iota((n, experts), 1).astype(F32)
        grad_logits = jnp.zeros((n, experts), F32)
        for k in range(TOP):
            grad_logits = jnp.where(
                column == table[:, ROUTE + k : ROUTE + k + 1],
                gate[k] * (grad_gate[k] - mean_gate),
                grad_logits,
            )
        grad_logits = grad_logits.astype(BF)
        grad_second = dot(
            low(jnp.logical_or(*picks)), came_grad[...].reshape(slots, width)
        ) + dot(
            grad_logits, w_router[...], NT
        )
        scale = root(middle)
        norm = middle * scale
        few_ref[:experts, :] = dot(grad_logits, second, TN).astype(BF)
        few_ref[experts:, :] = jnp.broadcast_to(
            jnp.sum(grad_second * norm, axis=0, keepdims=True), (16, width)
        ).astype(BF)
        grad_middle = cot + norm_back(norm, scale, grad_second * gain[...])
        grad_middle_ref[...] = grad_middle
        grad_attn = grad_middle.astype(BF)
        grad_attended = dot(grad_attn, w_out_proj[...], NT).astype(BF)
        grad_attended_ref[...] = grad_attended
        product = grad_attended.astype(F32) * attended[...].astype(F32)
        high = product.astype(BF)
        heads = 2 * delta_ref.shape[0]
        head = low(lax.shift_right_logical(iota((16, width), 1), 6) == iota((16, width), 0))
        delta = dot(head, high, NT) + dot(head, (product - high.astype(F32)).astype(BF), NT)
        for h in range(heads):
            for group in range(3):
                delta_ref[h // 2, group : group + 1, h % 2 * PR_DEV : (h % 2 + 1) * PR_DEV] = delta[
                    h : h + 1, group * PR_DEV : (group + 1) * PR_DEV
                ]
        grad_proj_ref[...] = dot(attended[...], grad_attn, TN).astype(BF)

    return kernel


def input_kernel(info, ins, outs, scratch):
    grad_q, grad_kc, grad_vc, w_query, w_key, w_value, ordered, gain, grad_middle = ins[:9]
    parts = ins[9:]
    out, = outs
    shares = parts[0][...].astype(F32)
    for part in parts[1:]:
        shares = shares + part[...].astype(F32)
    grad_hidden = dot(grad_q[...], w_query[...], NT) + jnp.concatenate(
        [shares, dot(grad_kc[...], w_key[...], NT) + dot(grad_vc[...], w_value[...], NT)], axis=0
    )
    tokens = ordered[...].astype(F32)
    scale = root(tokens)
    grad = grad_middle[...] + norm_back(tokens * scale, scale, grad_hidden * gain[...])
    back = order_matrix_t(grad.shape[0])
    high = grad.astype(BF)
    rest = grad - high.astype(F32)
    mid = rest.astype(BF)
    last = (rest - mid.astype(F32)).astype(BF)
    out[...] = (dot(back, high) + dot(back, mid)) + dot(back, last)


def halves_kernel(info, ins, outs, scratch):
    kept, came = ins
    for m, out in enumerate(outs):
        out[...] = (kept[m].astype(F32) + came[m].astype(F32)).astype(BF)


def join_kernel(info, ins, outs, scratch):
    out, = outs
    rows = ins[0].shape[0]
    for i, piece in enumerate(ins):
        out[i * rows : (i + 1) * rows, :] = piece[...]


def keys_and_values(rows, w_key, w_value, deps=()):
    width = rows.shape[1]
    chips = rows.shape[0] // (NPR * PR_DEV)
    many = 2
    block = many * NPR * PR_DEV
    steps = chips // many

    def kernel(rows_ref, w_key_ref, w_value_ref, *refs):
        k_ref, v_ref = refs[len(deps) :]
        values = rows_ref[...]
        k_ref[...] = dot(values, w_key_ref[...]).astype(BF).reshape(many, NPR, PR_DEV, width)
        v_ref[...] = dot(values, w_value_ref[...]).astype(BF).reshape(many, NPR, PR_DEV, width)

    weight = pl.BlockSpec((width, width), lambda i: (0, 0))
    out = pl.BlockSpec((many, NPR, PR_DEV, width), lambda i: (i, 0, 0, 0))
    return pl.pallas_call(
        kernel,
        grid=(steps,),
        in_specs=[pl.BlockSpec((block, width), lambda i: (i, 0)), weight, weight]
        + [pl.BlockSpec(memory_space=pl.ANY)] * len(deps),
        out_specs=[out, out],
        out_shape=[shape_of((chips, NPR, PR_DEV, width), BF)] * 2,
        compiler_params=pltpu.CompilerParams(vmem_limit_bytes=16 * MIB),
        cost_estimate=cost("keys_and_values"),
        name="keys_and_values",
    )(rows, w_key, w_value, *deps)


def shares_of(dk, dv, w_key, w_value):
    chips, width = dk.shape[0], w_key.shape[0]
    rows = chips * NPR * PR_DEV
    total = dot(dk.reshape(rows, width), w_key, NT) + dot(dv.reshape(rows, width), w_value, NT)
    return total.astype(BF).reshape(chips, NPR * PR_DEV, width)


def dense_gradients(info, hidden, rows, dq, dks, dvs, dkc, dvc, proj, few):
    width = hidden.shape[1]
    n_keys = len(rows)
    span = rows[0].shape[0]
    step = width // 3
    half = width // 2
    extra = few.shape[0]
    total = 4 * width + extra

    def kernel(info_ref, hidden_ref, *refs):
        row_refs = refs[:n_keys]
        dq_ref = refs[n_keys]
        dk_refs = refs[n_keys + 1 : 2 * n_keys + 1]
        dv_refs = refs[2 * n_keys + 1 : 3 * n_keys + 1]
        dkc_ref, dvc_ref, proj_ref, few_ref, mine, theirs = refs[3 * n_keys + 1 :]
        j = pl.program_id(0)
        core = info_ref[3]
        query = dot(hidden_ref[...], dq_ref[...], TN)
        both = dot(
            hidden_ref[NPR * PR_DEV :, :],
            jnp.concatenate([dkc_ref[...], dvc_ref[...]], axis=1),
            TN,
        )
        for row_ref, dk_ref, dv_ref in zip(row_refs, dk_refs, dv_refs):
            both = both + dot(
                row_ref[...],
                jnp.concatenate(
                    [dk_ref[...].reshape(span, step), dv_ref[...].reshape(span, step)], axis=1
                ),
                TN,
            )
        pieces = [
            query.astype(BF),
            both[:, :step].astype(BF),
            both[:, step:].astype(BF),
            proj_ref[...],
            few_ref[...],
        ]

        def put(out, at, start, size):
            row = 0
            for piece in pieces:
                out[row : row + piece.shape[0], at : at + size] = piece[:, start : start + size]
                row += piece.shape[0]

        rest = half - step
        for side, (low_out, high_out) in enumerate(((mine, theirs), (theirs, mine))):

            @pl.when(jnp.logical_and(core == side, j == 0))
            def _():
                put(low_out, 0, 0, step)

            @pl.when(jnp.logical_and(core == side, j == 1))
            def _():
                put(low_out, step, 0, rest)
                put(high_out, 0, rest, step - rest)

            @pl.when(jnp.logical_and(core == side, j == 2))
            def _():
                put(high_out, step - rest, 0, step)

    def const(shape):
        return pl.BlockSpec(shape, lambda j, info: (0,) * len(shape), pipeline_mode=pl.Buffered(1))

    def columns(rows_of):
        return pl.BlockSpec((rows_of, step), lambda j, info: (0, j))

    keys = pl.BlockSpec(dks[0].shape[:3] + (step,), lambda j, info: (0, 0, 0, j))
    out = pl.BlockSpec((total, half), lambda j, info: (0, 0))
    return pl.pallas_call(
        kernel,
        grid_spec=pltpu.PrefetchScalarGridSpec(
            num_scalar_prefetch=1,
            grid=(3,),
            in_specs=[const(hidden.shape)]
            + [const(r.shape) for r in rows]
            + [columns(dq.shape[0])]
            + [keys] * (2 * n_keys)
            + [columns(CLEN), columns(CLEN), columns(width), columns(extra)],
            out_specs=[out, out],
        ),
        out_shape=[shape_of((total, half), BF)] * 2,
        compiler_params=pltpu.CompilerParams(vmem_limit_bytes=60 * MIB),
        cost_estimate=cost("dense_gradients"),
        name="dense_gradients",
    )(info, hidden, *rows, dq, *dks, *dvs, dkc, dvc, proj, few)


def gelu_parts(a):
    square = a * a
    t = jnp.tanh(a * (0.7978845608 + (0.7978845608 * 0.044715) * square))
    half = 0.5 + 0.5 * t
    value = a * half
    slope = half + value * (1.0 - t) * (0.7978845608 + (0.7978845608 * 3.0 * 0.044715) * square)
    return value, slope


def gather_rows(into, blocks, first, room):
    for m in range(blocks.shape[0]):
        into[m * room : (m + 1) * room, :] = blocks[m, pl.ds(pl.multiple_of(first, 16), room), :]


def other_column(others, blocks, first, room):
    at = blocks.shape[1] - TABLE
    span = min(blocks.shape[2], -(-at // 128) * 128)
    eye = iota((room, span), 1) == iota((room, span), 0) + first
    for m in range(blocks.shape[0]):
        row = blocks[m, at : at + TABLE, :span][:1].astype(F32)
        column = jnp.sum(jnp.where(eye, row, 0.0), axis=1, keepdims=True)
        others[m * room : (m + 1) * room, :] = jnp.broadcast_to(column, (room, 128))


def gated(rows, cots, others, w_router, mine):
    logits = dot(rows, w_router)
    column = iota(logits.shape, 1)
    own = jnp.sum(jnp.where(column == mine, logits, 0.0), axis=1, keepdims=True)
    other = others[:, : logits.shape[1]].astype(jnp.int32)
    theirs = jnp.sum(jnp.where(column == other, logits, 0.0), axis=1, keepdims=True)
    gate = 1.0 / (1.0 + jnp.exp(theirs - own))
    return (gate * cots.astype(F32)).astype(BF)


def expert_forward(x_slots, w_in, w_out, room, deps=()):
    devices, per, _ = x_slots.shape
    local, width, units = w_in.shape
    rows = devices * room
    chunk = min(units, 768)

    def kernel(x_ref, w_in_ref, w_out_ref, *refs):
        slope_ref, out, x = refs[len(deps) :]
        l = pl.program_id(0)
        gather_rows(x, x_ref, l * room, room)
        parts = [slice(at, at + chunk) for at in range(0, units, chunk)]
        pre = [dot(x[...], w_in_ref[0, :, part]) for part in parts]
        total = jnp.zeros((rows, width), F32)
        for part, act in zip(parts, pre):
            value, slope = gelu_parts(act)
            slope_ref[0, :, part] = slope.astype(BF)
            total = total + dot(value.astype(BF), w_out_ref[0, part, :])
        for m in range(devices):
            out[m, pl.ds(pl.multiple_of(l * room, 16), room), :] = total[
                m * room : (m + 1) * room, :
            ].astype(BF)

    slots = pl.BlockSpec(x_slots.shape, lambda l: (0, 0, 0))
    return pl.pallas_call(
        kernel,
        grid=(local,),
        in_specs=[
            slots,
            pl.BlockSpec((1, width, units), lambda l: (l, 0, 0)),
            pl.BlockSpec((1, units, width), lambda l: (l, 0, 0)),
        ]
        + [pl.BlockSpec(memory_space=pl.ANY)] * len(deps),
        out_specs=[pl.BlockSpec((1, rows, units), lambda l: (l, 0, 0)), slots],
        out_shape=[shape_of((local, rows, units), BF), shape_of(x_slots.shape, BF)],
        scratch_shapes=[pltpu.VMEM((rows, width), BF)],
        compiler_params=pltpu.CompilerParams(vmem_limit_bytes=48 * MIB),
        cost_estimate=cost("expert_forward"),
        name="expert_forward",
    )(x_slots, w_in, w_out, *deps)


def expert_backward(info, x_slots, c_slots, slope, w_router, w_in, w_out, room, deps=()):
    devices, per, _ = x_slots.shape
    local, width, units = w_in.shape
    rows = devices * room
    chunk = min(units, 768)

    def kernel(info_ref, x_ref, c_ref, router_ref, slope_ref, w_in_ref, w_out_ref, *refs):
        out, x, grad, others = refs[len(deps) :]
        l = pl.program_id(0)
        gather_rows(x, x_ref, l * room, room)
        gather_rows(grad, c_ref, l * room, room)
        other_column(others, c_ref, l * room, room)
        grad[...] = gated(
            x[...], grad[...], others[...], router_ref[...], info_ref[0] * local + l
        )
        parts = [slice(at, at + chunk) for at in range(0, units, chunk)]
        grad_act = [dot(grad[...], w_out_ref[0, part, :], NT) for part in parts]
        total = jnp.zeros((rows, width), F32)
        for part, act in zip(parts, grad_act):
            grad_pre = (act * slope_ref[0, :, part].astype(F32)).astype(BF)
            total = total + dot(grad_pre, w_in_ref[0, :, part], NT)
        for m in range(devices):
            out[m, pl.ds(pl.multiple_of(l * room, 16), room), :] = total[
                m * room : (m + 1) * room, :
            ].astype(BF)

    slots = pl.BlockSpec(x_slots.shape, lambda l, info: (0, 0, 0))
    return pl.pallas_call(
        kernel,
        grid_spec=pltpu.PrefetchScalarGridSpec(
            num_scalar_prefetch=1,
            grid=(local,),
            in_specs=[
                slots,
                pl.BlockSpec(c_slots.shape, lambda l, info: (0, 0, 0)),
                pl.BlockSpec(w_router.shape, lambda l, info: (0, 0)),
                pl.BlockSpec((1, rows, units), lambda l, info: (l, 0, 0)),
                pl.BlockSpec((1, width, units), lambda l, info: (l, 0, 0)),
                pl.BlockSpec((1, units, width), lambda l, info: (l, 0, 0)),
            ]
            + [pl.BlockSpec(memory_space=pl.ANY)] * len(deps),
            out_specs=slots,
            scratch_shapes=[
                pltpu.VMEM((rows, width), BF),
                pltpu.VMEM((rows, width), BF),
                pltpu.VMEM((rows, 128), F32),
            ],
        ),
        out_shape=shape_of(x_slots.shape, BF),
        compiler_params=pltpu.CompilerParams(vmem_limit_bytes=48 * MIB),
        cost_estimate=cost("expert_backward"),
        name="expert_backward",
    )(info, x_slots, c_slots, w_router, slope, w_in, w_out, *deps)


def expert_weights(info, groups, w_router, w_in, w_out, room, dp, before=None, last=False, deps=()):
    devices = groups[0][0].shape[0]
    local, width, units = w_in.shape
    part, share = units // dp, width // dp
    rows = devices * room
    flat, places = [], []
    for x, x_base, c, c_base in groups:
        at = []
        for array in (x, c):
            known = [i for i, other in enumerate(flat) if other is array]
            if not known:
                flat.append(array)
            at.append(known[0] if known else len(flat) - 1)
        places.append((at[0], x_base, at[1], c_base))
    n_flat = len(flat)
    sums = [] if before is None else list(before)

    def kernel(info_ref, *refs):
        slots = refs[:n_flat]
        router_ref, w_in_ref, w_out_ref = refs[n_flat : n_flat + 3]
        refs = refs[n_flat + 3 :]
        earlier = refs[: len(sums)]
        refs = refs[len(sums) + len(deps) :]
        out_ref, in_refs = refs[0], refs[1:-4]
        xs, grads, all_others, total = refs[-4:]
        l = pl.program_id(0)
        for g, (x_at, x_base, c_at, c_base) in enumerate(places):
            x, grad, others = xs.at[g], grads.at[g], all_others.at[g]
            gather_rows(x, slots[x_at], x_base + l * room, room)
            gather_rows(grad, slots[c_at], c_base + l * room, room)
            other_column(others, slots[c_at], c_base + l * room, room)
            grad[...] = gated(
                x[...], grad[...], others[...], router_ref[...], info_ref[0] * local + l
            )
            value, slope = gelu_parts(dot(x[...], w_in_ref[0]))
            grad_act = dot(grad[...], w_out_ref[0], NT)
            grad_pre = (grad_act * slope).astype(BF)
            part_in = dot(x[...], grad_pre, TN)
            part_out = dot(value.astype(BF), grad[...], TN)
            if g > 0:
                total[...] += part_in
                out_ref[0] += part_out
            elif earlier:
                total[...] = earlier[1][0] + part_in
                out_ref[0] = earlier[0][0] + part_out
            else:
                total[...] = part_in
                out_ref[0] = part_out
        if last:
            for k in range(dp):
                start = pl.multiple_of(jnp.bitwise_xor(info_ref[2], k) * share, 16)
                in_refs[k][0] = total[pl.ds(start, share), :].astype(BF)
        else:
            in_refs[0][0] = total[...]

    def const(shape):
        return pl.BlockSpec(shape, lambda l, info: (0,) * len(shape), pipeline_mode=pl.Buffered(1))

    square = pl.BlockSpec((1, part, width), lambda l, info: (l, 0, 0))
    square_in = pl.BlockSpec((1, width, part), lambda l, info: (l, 0, 0))
    if last:
        in_specs = [pl.BlockSpec((1, share, part), lambda l, info: (l, 0, 0))] * dp
        in_shapes = [shape_of((local, share, part), BF)] * dp
    else:
        in_specs = [square_in]
        in_shapes = [shape_of((local, width, part), F32)]
    got = pl.pallas_call(
        kernel,
        grid_spec=pltpu.PrefetchScalarGridSpec(
            num_scalar_prefetch=1,
            grid=(local,),
            in_specs=[const(x.shape) for x in flat]
            + [
                const(w_router.shape),
                pl.BlockSpec((1, width, part), lambda l, info: (l, 0, info[2])),
                pl.BlockSpec((1, part, width), lambda l, info: (l, info[2], 0)),
            ]
            + [square, square_in][: len(sums)]
            + [pl.BlockSpec(memory_space=pl.ANY)] * len(deps),
            out_specs=[square] + in_specs,
            scratch_shapes=[
                pltpu.VMEM((len(places), rows, width), BF),
                pltpu.VMEM((len(places), rows, width), BF),
                pltpu.VMEM((len(places), rows, 128), F32),
                pltpu.VMEM((width, part), F32),
            ],
        ),
        out_shape=[shape_of((local, part, width), F32)] + in_shapes,
        compiler_params=pltpu.CompilerParams(vmem_limit_bytes=60 * MIB),
        cost_estimate=cost("expert_weights_last" if last else "expert_weights"),
        name="expert_weights_last" if last else "expert_weights",
    )(info, *flat, w_router, w_in, w_out, *sums, *deps)
    return got[0], got[1:]


def columns_kernel(info, ins, outs, scratch):
    out, = outs
    part = ins[0].shape[2]
    for k, piece in enumerate(ins):
        start = pl.multiple_of(jnp.bitwise_xor(info[2], k) * part, 128)
        out[:, :, pl.ds(start, part)] = piece[...].astype(F32)


class Sums:
    def __init__(self, info, mine, theirs, n, dp, devices):
        self.info, self.n, self.dp, self.devices = info, n, dp, devices
        self.half = mine.shape[1]
        self.rows = self.width = 2 * self.half
        self.chips = devices // 2
        self.tall = self.rows // self.chips
        self.short = self.tall // dp
        self.extra = mine.shape[0] - n * self.rows
        self.value = mine
        self.came = swap(theirs, "expert", 1)

    @staticmethod
    def fits(rows, width, dp, devices):
        short = rows // (devices // 2) // dp
        return short % 16 == 0 and width % 256 == 0 and short * dp * (devices // 2) == rows

    def cores(self, deps=()):
        n, rows, tall, half, extra = self.n, self.rows, self.tall, self.half, self.extra

        def kernel(info_ref, ins, outs, scratch):
            kept, got = ins
            for m, out in enumerate(outs):
                for i in range(n):
                    start = i * rows + jnp.bitwise_xor(info_ref[4], m) * tall
                    at = pl.ds(pl.multiple_of(start, 16), tall)
                    out[i * tall : (i + 1) * tall, :] = (
                        kept[at, :].astype(F32) + got[at, :].astype(F32)
                    ).astype(BF)
                if extra:
                    out[n * tall :, :] = (
                        kept[n * rows :, :].astype(F32) + got[n * rows :, :].astype(F32)
                    ).astype(BF)

        pieces = run(
            kernel, "sum_cores", self.info, [self.value, self.came],
            [shape_of((n * tall + extra, half), BF)] * self.chips, deps=deps,
        )
        self.pieces = [pieces[0]] + [
            swap(pieces[m], "expert", 2 * m) for m in range(1, self.chips)
        ]
        return pieces[0]

    def planes(self, deps=()):
        n, tall, short, half, extra = self.n, self.tall, self.short, self.half, self.extra

        def kernel(info_ref, ins, outs, scratch):
            total, = scratch
            total[...] = added([piece[...].astype(F32) for piece in ins]).astype(BF)
            out, = outs
            for k in range(out.shape[0]):
                for i in range(n):
                    start = i * tall + k * short
                    out[k, i * short : (i + 1) * short, :] = total[start : start + short, :]
                if extra:
                    out[k, n * short :, :] = total[n * tall :, :]

        sent, = run(
            kernel, "sum_chips", self.info, self.pieces,
            [shape_of((self.dp, n * short + extra, half), BF)],
            scratch=[pltpu.VMEM((n * tall + extra, half), BF)], deps=deps,
        )
        self.pieces = lax.all_to_all(sent, "dp", split_axis=0, concat_axis=0, tiled=True)
        return sent

    def groups(self, beside, deps=()):
        n, short, half, extra, dp = self.n, self.short, self.half, self.extra, self.dp

        def kernel(info_ref, ins, outs, scratch):
            value = added([ins[0][k].astype(F32) for k in range(dp)]).astype(BF)
            for k in range(dp):
                outs[0][k] = value[: n * short]
            outs[1][...] = value[n * short :]

        own, self.few = run(
            kernel, "sum_groups", self.info, [self.pieces],
            [shape_of((dp, n * short, half), BF), shape_of((extra, half), BF)], deps=deps,
        )
        own, beside = lax.optimization_barrier((own, beside))
        self.own = lax.all_to_all(own, "dp", split_axis=0, concat_axis=0, tiled=True)
        return own, beside

    def gather(self):
        spread = self.own.reshape(self.dp * self.n * self.short, self.half)
        self.spread = jnp.concatenate(
            [spread] + [swap(spread, "expert", 2 * m) for m in range(1, self.chips)] + [self.few],
            axis=0,
        )
        self.other = swap(self.spread, "expert", 1)

    def finish(self, columns, gain, weights):
        got = self.put(0, self.spread, columns, gain, weights, ())
        return self.put(1, self.other, columns, gain, weights, got)

    def put(self, side, spread, columns, gain, weights, before):
        n, short, tall, half, extra = self.n, self.short, self.tall, self.half, self.extra
        chips, dp, rows, width = self.chips, self.dp, self.rows, self.width
        n_weights, n_before = len(weights), len(before)

        def kernel(info_ref, ref, gain_ref, *refs):
            weight_refs = refs[:n_weights]
            earlier = refs[n_weights : n_weights + n_before]
            outs = refs[n_weights + n_before :]
            for m in range(chips):
                for k in range(dp):
                    start = jnp.bitwise_xor(info_ref[4], m) * tall + k * short
                    at = pl.ds(pl.multiple_of(start, 16), short)
                    for i in range(n):
                        place = ((m * dp + k) * n + i) * short
                        outs[i][at, :] = ref[place : place + short, :].astype(F32)
            few = ref[chips * dp * n * short :, :].astype(F32)
            outs[n][...] = few[:columns, :].T
            outs[n + 1][...] = few[columns : columns + 1, :]
            along = gained(zip(weight_refs, outs), gain_ref[...])
            outs[n + 2][...] = earlier[-1][...] + along if earlier else along

        def half_of(block, axis):
            def index(i, info):
                core = jnp.bitwise_xor(info[3], side)
                return (core, 0) if axis == 0 else (0, core)

            return pl.BlockSpec(block, index)

        def const(shape):
            return pl.BlockSpec(shape, lambda i, info: (0, 0))

        square, row = half_of((rows, half), 1), const((1, width))
        outs = [shape_of((rows, width), F32)] * n
        outs = outs + [shape_of((width, columns), F32), shape_of((1, width), F32)]
        return pl.pallas_call(
            kernel,
            grid_spec=pltpu.PrefetchScalarGridSpec(
                num_scalar_prefetch=1,
                grid=(1,),
                in_specs=[const(spread.shape), row]
                + [square] * n_weights
                + [pl.BlockSpec(memory_space=pl.ANY)] * max(n_before - 1, 0)
                + [row] * min(n_before, 1),
                out_specs=[square] * n + [half_of((half, columns), 0), half_of((1, half), 1), row],
            ),
            out_shape=outs + [shape_of((1, width), F32)],
            input_output_aliases={3 + n_weights + i: i for i in range(n_before - 1)},
            compiler_params=pltpu.CompilerParams(vmem_limit_bytes=24 * MIB),
            cost_estimate=cost("spread_sums"),
            name="spread_sums",
        )(self.info, spread, gain, *weights, *before)


def gained(pairs, gain):
    total = 0.0
    for weight, grad in pairs:
        total = total + jnp.sum(weight[...].astype(F32) * grad[...], axis=1, keepdims=True)
    return jnp.broadcast_to(total, (total.shape[0], 128)).T[:1] / gain


def per_device(
    inputs,
    gain_one,
    w_query,
    w_key,
    w_value,
    w_out_proj,
    gain_two,
    w_router,
    w_in,
    w_out,
    routes,
    slot_index,
    prompt_of,
    cotangent,
):
    row_count, width = inputs.shape[1], inputs.shape[2]
    dp, devices = lax.axis_size("dp"), lax.axis_size("expert")
    z, device = lax.axis_index("dp"), lax.axis_index("expert")
    chips = devices // 2
    prompt_rows = NPR * PR_DEV
    expert_count, local = w_router.shape[1], w_in.shape[0]
    capacity = max(2, 5 * row_count * TOP // (4 * expert_count))
    room = -(-capacity // 16) * 16
    per = local * room
    info = jnp.stack(
        [device, prompt_of[0, 0], z, lax.rem(device, 2), lax.div(device, 2)]
    ).astype(jnp.int32)
    gain_one = gain_one[None, :]
    gain_two = gain_two[None, :]
    wide = shape_of((row_count, width), BF)
    wide32 = shape_of((row_count, width), F32)
    narrow = shape_of((row_count, 128), F32)
    x_shape = shape_of((devices, per, width), BF)
    c_shape = shape_of((devices, per + TABLE, width), BF)

    hidden_p, hidden, ordered = run(
        norm_kernel, "norm", info, [inputs[0], gain_one],
        [shape_of((prompt_rows, width), BF), wide, wide],
    )
    near = [hidden_p] + [swap(hidden_p, "expert", 2 * m) for m in range(1, chips)]

    message, cols, c_sent = run(
        table_kernel(per, room, capacity), "table", info,
        [cotangent[0], routes[0], slot_index[0]],
        [shape_of((row_count + TABLE, width), BF), narrow, c_shape],
        deps=[hidden_p],
    )
    hidden_c = hidden[prompt_rows:]
    queries = dot(hidden, w_query).astype(BF)
    key_c = dot(hidden_c, w_key).astype(BF)
    value_c = dot(hidden_c, w_value).astype(BF)
    near, cols, queries, key_c, value_c = lax.optimization_barrier(
        (near, cols, queries, key_c, value_c)
    )
    near, = run(join_kernel, "join", info, near, [shape_of((chips * prompt_rows, width), BF)])
    other = swap(near, "expert", 1)
    messages = far_groups(message, dp)
    c_sent, near = lax.optimization_barrier((c_sent, near))
    c_slots = [exchange(c_sent)]

    key_near, value_near = keys_and_values(near, w_key, w_value)
    key_other, value_other = keys_and_values(other, w_key, w_value, deps=[key_near])
    keys, values = [key_near, key_other], [value_near, value_other]
    attended, lse = attention_forward(info, queries, keys, values, key_c, value_c)
    c_slots, messages, attended = lax.optimization_barrier((c_slots, messages, attended))

    middle, second, gates, x_sent = run(
        middle_kernel(per), "middle", info,
        [ordered, attended, w_out_proj, gain_two, w_router, cols, message],
        [wide32, wide, narrow, x_shape],
    )
    x_slots = [exchange(x_sent)]
    seconds = far_groups(second, dp)
    c_rest = run(
        dispatch_cot_kernel(per), "dispatch_cot", info, messages,
        [shape_of((devices, len(messages) * per + TABLE, width), BF)], deps=[middle],
    )
    x_slots, c_rest = lax.optimization_barrier((x_slots, c_rest))
    c_even, = [exchange(sent) for sent in c_rest]

    slope, out_sent = expert_forward(x_slots[0], w_in, w_out, room)
    seconds, slope, c_slots[0], x_slots[0] = lax.optimization_barrier(
        (seconds, slope, c_slots[0], x_slots[0])
    )
    c_odd = [swap(c_slots[0], "dp", 1)]
    x_odd = [swap(x_slots[0], "dp", 1)]
    seconds = with_neighbours(seconds)
    messages = with_neighbours(messages)
    returned = exchange(out_sent)
    grad_sent = expert_backward(
        info, x_slots[0], c_slots[0], slope, w_router, w_in, w_out, room, deps=[c_even]
    )
    returned, grad_sent = lax.optimization_barrier((returned, grad_sent))
    grad_returned = exchange(grad_sent)

    sums = expert_weights(
        info, [(x_slots[0], 0, c_slots[0], 0)], w_router, w_in, w_out, room, dp,
        deps=[grad_sent],
    )
    far = dp - 2
    odd = far // 2
    rest, = run(
        dispatch_kernel(per), "dispatch", info, messages + seconds,
        [shape_of((devices, (odd + far) * per + TABLE, width), BF)], deps=[sums[0]],
    )

    outputs, grad_middle, grad_attended, grad_proj, few, delta = run(
        combine_kernel(), "combine", info,
        [middle, second, gates, cols, message, attended, w_out_proj, w_router, gain_two]
        + [returned, grad_returned],
        [wide, wide32, wide, shape_of((width, width), BF), shape_of((expert_count + 16, width), BF),
         shape_of((width // PAIR, 3, TWO), F32)],
        deps=[rest],
    )
    rest = exchange(rest)

    pairs = width // PAIR

    def back(first, count, before=(), deps=()):
        return attention_backward(
            info, queries, keys, values, key_c, value_c, grad_attended, lse, delta, first, count,
            before=before, deps=deps,
        )

    got = back(0, pairs, deps=())
    grad_q, dk_near, dk_far, dv_near, dv_far, grad_kc, grad_vc = got
    grad_q, dk_near, dk_far, dv_near, dv_far, x_odd, c_odd = lax.optimization_barrier(
        (grad_q, dk_near, dk_far, dv_near, dv_far, x_odd, c_odd)
    )
    stepwise = Sums.fits(width, width, dp, devices)
    if stepwise:
        mine, theirs = dense_gradients(
            info, hidden, [near, other], grad_q, [dk_near, dk_far], [dv_near, dv_far],
            grad_kc, grad_vc, grad_proj, few,
        )
        total = Sums(info, mine, theirs, 4, dp, devices)
    else:
        flat = [part.reshape(chips * prompt_rows, width) for part in (dk_near, dk_far, dv_near, dv_far)]
        grad_query = dot(hidden, grad_q, TN)
        grad_key = dot(near, flat[0], TN) + dot(other, flat[1], TN) + dot(hidden_c, grad_kc, TN)
        grad_value = dot(near, flat[2], TN) + dot(other, flat[3], TN) + dot(hidden_c, grad_vc, TN)
        dense = [grad_query, grad_key, grad_value, grad_proj, few]

    sent = shares_of(dk_far, dv_far, w_key, w_value)
    kept = shares_of(dk_near, dv_near, w_key, w_value)
    came = swap(sent, "expert", 1)
    after = total.cores([kept]) if stepwise else kept
    shares = run(
        halves_kernel, "halves", info, [kept, came],
        [shape_of((prompt_rows, width), BF)] * chips, deps=[after],
    )

    others = [(x_odd[0], 0, c_odd[0], 0)]
    for g in range(far):
        c_from, c_base = (rest, g // 2 * per) if g % 2 else (c_even, g // 2 * per)
        others.append((rest, (odd + g) * per, c_from, c_base))
    grad_w_out, in_pieces = expert_weights(
        info, others, w_router, w_in, w_out, room, dp,
        before=(sums[0], sums[1][0]), last=True, deps=[shares[0]],
    )
    shares, in_pieces, grad_w_out = lax.optimization_barrier((shares, in_pieces, grad_w_out))
    after = [grad_w_out]
    if stepwise:
        after = [total.planes(after)]
    shares = [shares[0]] + [swap(shares[m], "expert", 2 * m) for m in range(1, chips)]
    if stepwise:
        own, shares = total.groups(shares, after)
        after = [own]
    grad_input, = run(
        input_kernel, "input", info,
        [grad_q, grad_kc, grad_vc, w_query, w_key, w_value, ordered, gain_one, grad_middle] + shares,
        [wide32], deps=after,
    )
    if stepwise:
        total.own, grad_input, in_pieces = lax.optimization_barrier(
            (total.own, grad_input, in_pieces)
        )
        total.gather()
    far_first = [swap(in_pieces[k], "dp", k) for k in range(dp - 1, 0, -1)]
    in_pieces = [in_pieces[0]] + far_first[::-1]
    after = []
    if stepwise:
        query_sum, key_sum, value_sum, proj_sum, grad_router, grad_gain_two, grad_gain_one = (
            total.finish(expert_count, gain_one, [w_query, w_key, w_value])
        )
        after = [query_sum]
    else:
        query_sum, key_sum, value_sum, proj_sum, few = lax.psum(
            [part.astype(F32) for part in dense], ("dp", "expert")
        )
        grad_router, grad_gain_two = few[:expert_count].T, few[expert_count :][:1]
        grad_gain_one = gained(
            [(w_query, query_sum), (w_key, key_sum), (w_value, value_sum)], gain_one
        )
    grad_w_in, = run(
        columns_kernel, "columns", info, in_pieces,
        [shape_of((local, width // dp, w_in.shape[2]), F32)], deps=after,
    )
    return (
        outputs[None],
        grad_input[None],
        grad_gain_one[0],
        query_sum,
        key_sum,
        value_sum,
        proj_sum,
        grad_gain_two[0],
        grad_router,
        grad_w_in,
        grad_w_out,
    )


def solution(mesh):
    return jax.shard_map(
        per_device,
        mesh=mesh,
        in_specs=(
            P("dp", "expert", None),
            P(),
            P(),
            P(),
            P(),
            P(),
            P(),
            P(),
            P("expert", None, None),
            P("expert", None, None),
            P("dp", "expert", None),
            P("dp", "expert", None),
            P("dp", "expert"),
            P("dp", "expert", None),
        ),
        out_specs=(
            P("dp", "expert", None),
            P("dp", "expert", None),
            P(),
            P(),
            P(),
            P(),
            P(),
            P(),
            P(),
            P("expert", "dp", None),
            P("expert", "dp", None),
        ),
        check_vma=False,
    )
```

```python
import jax
import jax.numpy as jnp
from jax import lax
from jax.experimental import pallas as pl
from jax.experimental.pallas import tpu as pltpu
from jax.sharding import PartitionSpec as P

H = 12
HD = 64
TOP = 2
NPR = 2
CLEN = 128
PR_DEV = 128
PAIR = 2 * HD
TWO = 2 * PR_DEV

NEGATIVE = -1e30
BF = jnp.bfloat16
F32 = jnp.float32
SCALE = HD ** (-0.5)
MIB = 1024 * 1024

NN = ((1,), (0,))
NT = ((1,), (1,))
TN = ((0,), (0,))

HIGH, LOW, ROUTE = 0, 2, 4
TABLE = 16


def dot(a, b, dims=NN):
    return lax.dot_general(a, b, (dims, ((), ())), preferred_element_type=F32)


def iota(shape, dim):
    return lax.broadcasted_iota(jnp.int32, shape, dim)


def shape_of(shape, dtype):
    return jax.ShapeDtypeStruct(shape, dtype)


WEIGHT = 1.0
TIMES = {
    "norm": 2.7,
    "table": 4.5,
    "attention_forward": 15.0,
    "middle": 5.1,
    "dispatch_cot": 7.0,
    "expert_forward": 20.0,
    "expert_backward": 20.0,
    "dispatch": 30.0,
    "expert_weights": 1.0,
    "combine": 3.0,
    "attention_backward": 15.0,
    "sum_cores": 0.3,
    "halves": 0.3,
    "expert_weights_last": 30.0,
    "sum_chips": 2.6,
    "sum_groups": 1.8,
    "input": 1.0,
    "spread_sums": 60.0,
    "columns": 1.0,
    "join": 2.0,
    "keys_and_values": 3.5,
    "dense_gradients": 60.0,
}


LARGE = ("middle", "dispatch_cot", "dispatch", "combine", "input")


def cost(name):
    flops = int(TIMES[name] * WEIGHT * 1.1e9)
    return pl.CostEstimate(flops=flops, bytes_accessed=0, transcendentals=0)


def run(kernel, name, info, operands, outs, deps=(), scratch=()):
    n_in, n_dep, n_out = len(operands), len(deps), len(outs)

    def body(info_ref, *refs):
        ins = refs[:n_in]
        results = refs[n_in + n_dep : n_in + n_dep + n_out]
        kernel(info_ref, ins, results, refs[n_in + n_dep + n_out :])

    vmem = pl.BlockSpec(memory_space=pltpu.VMEM)
    return pl.pallas_call(
        body,
        in_specs=[pl.BlockSpec(memory_space=pltpu.SMEM)]
        + [vmem] * n_in
        + [pl.BlockSpec(memory_space=pl.ANY)] * n_dep,
        out_specs=[vmem] * n_out,
        out_shape=list(outs),
        scratch_shapes=list(scratch),
        compiler_params=pltpu.CompilerParams(vmem_limit_bytes=(56 if name in LARGE else 24) * MIB),
        cost_estimate=cost(name),
        name=name,
    )(info, *operands, *deps)


def fill_bias(bias_ref, device, chips):
    for b in range(2 * chips):
        mask = 2 * (b % chips) + b // chips
        offset = (jnp.bitwise_xor(device, mask) - device) * PR_DEV
        seen = iota((PR_DEV, PR_DEV), 0) + offset <= iota((PR_DEV, PR_DEV), 1)
        bias_ref[b * PR_DEV : (b + 1) * PR_DEV, :] = jnp.where(seen, 0.0, NEGATIVE)


def two_heads(rows):
    keep = (iota((TWO, PAIR), 0) < PR_DEV) == (iota((TWO, PAIR), 1) < HD)
    return jnp.where(keep, jnp.concatenate([rows, rows], axis=0), jnp.zeros((), rows.dtype))


def join_heads(both):
    first = iota((PAIR, PR_DEV), 0) < HD
    return jnp.where(first, both[:, :PR_DEV], both[:, PR_DEV:]).T


def twice(block):
    return jnp.concatenate([block, block], axis=1)


def top_of(parts):
    top = jnp.max(parts[0], axis=0, keepdims=True)
    for part in parts[1:]:
        top = jnp.maximum(top, jnp.max(part, axis=0, keepdims=True))
    return top


def sum_of(parts):
    total = jnp.sum(parts[0], axis=0, keepdims=True)
    for part in parts[1:]:
        total = total + jnp.sum(part, axis=0, keepdims=True)
    return total


def added(parts):
    total = parts[0]
    for part in parts[1:]:
        total = total + part
    return total


def scores_of(keys, q2, bias_ref, group, span):
    parts = []
    for i, k in enumerate(keys):
        st = dot(k, q2, NT)
        if group < NPR:
            st = st + twice(bias_ref[i * span : (i + 1) * span, :])
        elif i == 2:
            st = st + twice(bias_ref[:PR_DEV, :])
        parts.append(st)
    return parts


def attention_forward_kernel(
    info, q_ref, ka_ref, kb_ref, va_ref, vb_ref, kc_ref, vc_ref, o_ref, lse_ref, bias_ref
):
    chips = ka_ref.shape[0]
    span = chips * PR_DEV
    device, chosen = info[0], info[1]

    @pl.when(pl.program_id(0) == 0)
    def _():
        fill_bias(bias_ref, device, chips)

    for group in range(3):
        rows = slice(group * PR_DEV, (group + 1) * PR_DEV)
        q2 = two_heads(q_ref[rows, :] * jnp.asarray(SCALE, BF))
        which = group if group < NPR else chosen
        keys = [ref[:, which].reshape(span, PAIR) for ref in (ka_ref, kb_ref)]
        values = [ref[:, which].reshape(span, PAIR) for ref in (va_ref, vb_ref)]
        if group == NPR:
            keys.append(kc_ref[...])
            values.append(vc_ref[...])
        scores = scores_of(keys, q2, bias_ref, group, span)
        top = top_of(scores)
        probs = [jnp.exp(st - top) for st in scores]
        total = sum_of(probs)
        both = added([dot(v, p.astype(BF), TN) for v, p in zip(values, probs)])
        both = both * (1.0 / total)
        o_ref[rows, :] = join_heads(both).astype(BF)
        lse_ref[0, group : group + 1, :] = top + jnp.log(total)


def attention_backward_kernel(
    info, q_ref, ka_ref, kb_ref, va_ref, vb_ref, kc_ref, vc_ref, do_ref, lse_ref, delta_ref,
    dq_ref, dka_ref, dkb_ref, dva_ref, dvb_ref, dkc_ref, dvc_ref, bias_ref, dk_acc, dv_acc,
):
    chips = ka_ref.shape[0]
    span = chips * PR_DEV
    device, chosen = info[0], info[1]

    @pl.when(pl.program_id(0) == 0)
    def _():
        fill_bias(bias_ref, device, chips)

    for group in range(3):
        rows = slice(group * PR_DEV, (group + 1) * PR_DEV)
        q2 = two_heads(q_ref[rows, :] * jnp.asarray(SCALE, BF))
        do2 = two_heads(do_ref[rows, :])
        lse = lse_ref[0, group : group + 1, :]
        which = group if group < NPR else chosen
        keys = [ref[:, which].reshape(span, PAIR) for ref in (ka_ref, kb_ref)]
        values = [ref[:, which].reshape(span, PAIR) for ref in (va_ref, vb_ref)]
        if group == NPR:
            keys.append(kc_ref[...])
            values.append(vc_ref[...])
        probs = [jnp.exp(st - lse) for st in scores_of(keys, q2, bias_ref, group, span)]
        grads = [dot(v, do2, NT) for v in values]
        delta = delta_ref[0, group : group + 1, :]
        ds = [(p * (g - delta)).astype(BF) for p, g in zip(probs, grads)]
        dq = added([dot(k, d, TN) for k, d in zip(keys, ds)])
        dq_ref[rows, :] = (join_heads(dq) * SCALE).astype(BF)
        for i in range(2):
            dk = dot(ds[i], q2).reshape(chips, PR_DEV, PAIR)
            dv = dot(probs[i].astype(BF), do2).reshape(chips, PR_DEV, PAIR)
            at = slice(i * chips, (i + 1) * chips)
            if group < NPR:
                dk_acc[at, group] = dk
                dv_acc[at, group] = dv
            else:
                dk_acc[at, chosen] += dk
                dv_acc[at, chosen] += dv
        if group == NPR:
            dkc_ref[...] = dot(ds[2], q2).astype(BF)
            dvc_ref[...] = dot(probs[2].astype(BF), do2).astype(BF)
    dka_ref[...] = dk_acc[:chips].astype(BF)
    dkb_ref[...] = dk_acc[chips:].astype(BF)
    dva_ref[...] = dv_acc[:chips].astype(BF)
    dvb_ref[...] = dv_acc[chips:].astype(BF)


def attention_specs(chips, rows, first=0):
    q_spec = pl.BlockSpec((rows, PAIR), lambda h, info: (0, first + h))
    k_spec = pl.BlockSpec((chips, NPR, PR_DEV, PAIR), lambda h, info: (0, 0, 0, first + h))
    c_spec = pl.BlockSpec((CLEN, PAIR), lambda h, info: (0, first + h))
    l_spec = pl.BlockSpec((1, 3, TWO), lambda h, info: (first + h, 0, 0))
    return q_spec, k_spec, c_spec, l_spec


def drop_refs(kernel, n_in, n_dep):
    def body(info, *refs):
        kernel(info, *refs[:n_in], *refs[n_in + n_dep :])

    return body


def attention_forward(info, q, keys, values, kc, vc, deps=()):
    k = keys[0]
    chips, rows, pairs = k.shape[0], q.shape[0], q.shape[1] // PAIR
    q_spec, k_spec, c_spec, l_spec = attention_specs(chips, rows)
    return pl.pallas_call(
        drop_refs(attention_forward_kernel, 7, len(deps)),
        grid_spec=pltpu.PrefetchScalarGridSpec(
            num_scalar_prefetch=1,
            grid=(pairs,),
            in_specs=[q_spec] + [k_spec] * 4 + [c_spec, c_spec]
            + [pl.BlockSpec(memory_space=pl.ANY)] * len(deps),
            out_specs=[q_spec, l_spec],
            scratch_shapes=[pltpu.VMEM((2 * chips * PR_DEV, PR_DEV), F32)],
        ),
        out_shape=[shape_of(q.shape, BF), shape_of((pairs, 3, TWO), F32)],
        compiler_params=pltpu.CompilerParams(vmem_limit_bytes=24 * MIB),
        cost_estimate=cost("attention_forward"),
        name="attention_forward",
    )(info, q, *keys, *values, kc, vc, *deps)


def attention_backward(info, q, keys, values, kc, vc, do, lse, delta, first, pairs, before=(), deps=()):
    k = keys[0]
    chips, rows = k.shape[0], q.shape[0]
    q_spec, k_spec, c_spec, l_spec = attention_specs(chips, rows, first)
    deps = list(before) + list(deps)
    return pl.pallas_call(
        drop_refs(attention_backward_kernel, 10, len(deps)),
        grid_spec=pltpu.PrefetchScalarGridSpec(
            num_scalar_prefetch=1,
            grid=(pairs,),
            in_specs=[q_spec] + [k_spec] * 4 + [c_spec, c_spec, q_spec, l_spec, l_spec]
            + [pl.BlockSpec(memory_space=pl.ANY)] * len(deps),
            out_specs=[q_spec] + [k_spec] * 4 + [c_spec, c_spec],
            scratch_shapes=[
                pltpu.VMEM((2 * chips * PR_DEV, PR_DEV), F32),
                pltpu.VMEM((2 * chips, NPR, PR_DEV, PAIR), F32),
                pltpu.VMEM((2 * chips, NPR, PR_DEV, PAIR), F32),
            ],
        ),
        out_shape=[shape_of(q.shape, BF)]
        + [shape_of(k.shape, BF)] * 4
        + [shape_of(kc.shape, BF)] * 2,
        input_output_aliases={11 + i: i for i in range(len(before))},
        compiler_params=pltpu.CompilerParams(vmem_limit_bytes=60 * MIB),
        cost_estimate=cost("attention_backward"),
        name="attention_backward",
    )(info, q, *keys, *values, kc, vc, do, lse, delta, *deps)


def swap(value, axis, mask):
    size = lax.axis_size(axis)
    return lax.ppermute(value, axis, [(i, i ^ mask) for i in range(size)])


def far_groups(own, dp):
    return [swap(own, "dp", m) for m in range(2, dp, 2)]


def with_neighbours(far):
    return [tokens for even in far for tokens in (even, swap(even, "dp", 1))]


def exchange(blocks):
    return lax.all_to_all(blocks, "expert", split_axis=0, concat_axis=0, tiled=True)


def root(values):
    return lax.rsqrt(jnp.mean(values * values, axis=-1, keepdims=True) + 1e-06)


def norm_back(norm, scale, grad):
    return scale * (grad - norm * jnp.mean(grad * norm, axis=-1, keepdims=True))


def source_row(row):
    inner = jnp.bitwise_and(row, PR_DEV - 1) * NPR + lax.shift_right_logical(row, 7)
    return jnp.where(row < NPR * PR_DEV, inner, row)


def order_matrix(n):
    return (source_row(iota((n, n), 0)) == iota((n, n), 1)).astype(BF)


def order_matrix_t(n):
    return (source_row(iota((n, n), 1)) == iota((n, n), 0)).astype(BF)


def norm_kernel(info, ins, outs, scratch):
    x, gain = ins
    prompt, hidden_ref, ordered = outs
    tokens = dot(order_matrix(x.shape[0]), x[...])
    hidden = (tokens * root(tokens) * gain[...]).astype(BF)
    prompt[...] = hidden[: NPR * PR_DEV]
    hidden_ref[...] = hidden
    ordered[...] = tokens.astype(BF)


def target(rows, k):
    return (rows[HIGH + k : HIGH + k + 1] * 16.0 + rows[LOW + k : LOW + k + 1]).astype(jnp.int32)


def picks_of(rows, slots):
    at = iota((slots, rows.shape[1]), 0)
    return [at == target(rows, k) for k in range(TOP)]


def low(mask):
    return jnp.where(mask, 1.0, 0.0).astype(BF)


def other_routes(rows, picks):
    low_rows = rows[:8].astype(BF)
    first = dot(low_rows, low(picks[0]), NT)[ROUTE + 1 : ROUTE + 2]
    return first + dot(low_rows, low(picks[1]), NT)[ROUTE : ROUTE + 1]


def send_slots(out, sent, per, at=0):
    for m in range(out.shape[0]):
        out[m, at : at + per, :] = sent[m * per : (m + 1) * per]


def clear_others(out):
    for m in range(out.shape[0]):
        out[m, out.shape[1] - TABLE :, :] = jnp.zeros((TABLE, out.shape[2]), BF)


def send_others(out, others, per, at=0):
    row = out.shape[1] - TABLE
    for m in range(out.shape[0]):
        out[m, row:, at : at + per] = jnp.broadcast_to(
            others[:, m * per : (m + 1) * per], (TABLE, per)
        ).astype(BF)


def table_kernel(per, room, capacity):
    def kernel(info, ins, outs, scratch):
        cot, route, slot = ins
        message, cols, out = outs
        n, width = cot.shape
        order = order_matrix(n)
        ordered = dot(order, cot[...]).astype(BF)
        r, s = route[...], slot[...]
        where = jnp.where(s < capacity, r * room + s, -16)
        high = lax.shift_right_arithmetic(where, 4).astype(F32)
        rest = jnp.bitwise_and(where, 15).astype(F32)
        r = r.astype(F32)
        lane = iota((n, 128), 1)
        table = jnp.zeros((n, 128), F32)
        for first, values in ((HIGH, high), (LOW, rest), (ROUTE, r)):
            for k in range(TOP):
                table = jnp.where(lane == first + k, values[:, k : k + 1], table)
        table = dot(order, table.astype(BF))
        cols[...] = table
        rows = table.T[:TABLE]
        message[:n, :] = ordered
        message[n:, :] = jnp.zeros((TABLE, width), BF)
        message[n:, :n] = rows.astype(BF)
        picks = picks_of(rows, per * out.shape[0])
        send_slots(out, dot(low(jnp.logical_or(*picks)), ordered).astype(BF), per)
        clear_others(out)
        send_others(out, other_routes(rows, picks), per)

    return kernel


def table_rows(message):
    n = message.shape[0] - TABLE
    return message[n:, :n].astype(F32)


def dispatch_cot_kernel(per):
    def kernel(info, ins, outs, scratch):
        out, = outs
        n = ins[0].shape[0] - TABLE
        clear_others(out)
        for g, message in enumerate(ins):
            rows = table_rows(message)
            picks = picks_of(rows, per * out.shape[0])
            sent = dot(low(jnp.logical_or(*picks)), message[:n, :]).astype(BF)
            send_slots(out, sent, per, g * per)
            send_others(out, other_routes(rows, picks), per, g * per)

    return kernel


def dispatch_kernel(per):
    def kernel(info, ins, outs, scratch):
        out, = outs
        groups = len(ins) // 2
        odd = groups // 2
        clear_others(out)
        for g in range(groups):
            message = ins[g]
            n = message.shape[0] - TABLE
            rows = table_rows(message)
            picks = picks_of(rows, per * out.shape[0])
            pick = low(jnp.logical_or(*picks))
            if g % 2:
                at = g // 2 * per
                send_slots(out, dot(pick, message[:n, :]).astype(BF), per, at)
                send_others(out, other_routes(rows, picks), per, at)
            sent = dot(pick, ins[groups + g][...]).astype(BF)
            send_slots(out, sent, per, (odd + g) * per)

    return kernel


def middle_kernel(per):
    def kernel(info, ins, outs, scratch):
        ordered, attended, w_out_proj, gain, w_router, cols, message = ins
        middle_ref, second_ref, gates_ref, out = outs
        middle = ordered[...].astype(F32) + dot(attended[...], w_out_proj[...])
        middle_ref[...] = middle
        second = (middle * root(middle) * gain[...]).astype(BF)
        second_ref[...] = second
        picks = picks_of(table_rows(message), per * out.shape[0])
        send_slots(out, dot(low(jnp.logical_or(*picks)), second).astype(BF), per)
        logits = dot(second, w_router[...])
        column = iota(logits.shape, 1).astype(F32)
        chosen = [
            jnp.sum(
                jnp.where(column == cols[:, ROUTE + k : ROUTE + k + 1], logits, 0.0),
                axis=1,
                keepdims=True,
            )
            for k in range(TOP)
        ]
        lane = iota(gates_ref.shape, 1)
        first = 1.0 / (1.0 + jnp.exp(chosen[1] - chosen[0]))
        then = 1.0 / (1.0 + jnp.exp(chosen[0] - chosen[1]))
        gates_ref[...] = jnp.where(lane == 0, first, then)

    return kernel


def combine_kernel():
    def kernel(info, ins, outs, scratch):
        middle_ref, second_ref, gates, cols, message, attended, w_out_proj, w_router, gain = ins[:9]
        came, came_grad = ins[9:]
        out_ref, grad_middle_ref, grad_attended_ref, grad_proj_ref, few_ref, delta_ref = outs
        n, width = middle_ref.shape
        slots = came.shape[0] * came.shape[1]
        middle, second = middle_ref[...], second_ref[...]
        cot = message[:n, :].astype(F32)
        table = cols[...]
        at = iota((n, slots), 1)
        picks = []
        for k in range(TOP):
            where = table[:, HIGH + k : HIGH + k + 1] * 16.0 + table[:, LOW + k : LOW + k + 1]
            picks.append(at == where.astype(jnp.int32))
        returned = came[...].reshape(slots, width)
        fetched = [dot(low(pick), returned) for pick in picks]
        gate = [gates[:, k : k + 1] for k in range(TOP)]
        outputs = (middle + (gate[0] * fetched[0] + gate[1] * fetched[1])).astype(BF)
        out_ref[...] = dot(order_matrix_t(n), outputs).astype(BF)
        grad_gate = [jnp.sum(cot * f, axis=1, keepdims=True) for f in fetched]
        mean_gate = gate[0] * grad_gate[0] + gate[1] * grad_gate[1]
        experts = w_router.shape[1]
        column = iota((n, experts), 1).astype(F32)
        grad_logits = jnp.zeros((n, experts), F32)
        for k in range(TOP):
            grad_logits = jnp.where(
                column == table[:, ROUTE + k : ROUTE + k + 1],
                gate[k] * (grad_gate[k] - mean_gate),
                grad_logits,
            )
        grad_logits = grad_logits.astype(BF)
        grad_second = dot(
            low(jnp.logical_or(*picks)), came_grad[...].reshape(slots, width)
        ) + dot(
            grad_logits, w_router[...], NT
        )
        scale = root(middle)
        norm = middle * scale
        few_ref[:experts, :] = dot(grad_logits, second, TN).astype(BF)
        few_ref[experts:, :] = jnp.broadcast_to(
            jnp.sum(grad_second * norm, axis=0, keepdims=True), (16, width)
        ).astype(BF)
        grad_middle = cot + norm_back(norm, scale, grad_second * gain[...])
        grad_middle_ref[...] = grad_middle
        grad_attn = grad_middle.astype(BF)
        grad_attended = dot(grad_attn, w_out_proj[...], NT).astype(BF)
        grad_attended_ref[...] = grad_attended
        product = grad_attended.astype(F32) * attended[...].astype(F32)
        high = product.astype(BF)
        heads = 2 * delta_ref.shape[0]
        head = low(lax.shift_right_logical(iota((16, width), 1), 6) == iota((16, width), 0))
        delta = dot(head, high, NT) + dot(head, (product - high.astype(F32)).astype(BF), NT)
        for h in range(heads):
            for group in range(3):
                delta_ref[h // 2, group : group + 1, h % 2 * PR_DEV : (h % 2 + 1) * PR_DEV] = delta[
                    h : h + 1, group * PR_DEV : (group + 1) * PR_DEV
                ]
        grad_proj_ref[...] = dot(attended[...], grad_attn, TN).astype(BF)

    return kernel


def input_kernel(info, ins, outs, scratch):
    grad_q, grad_kc, grad_vc, w_query, w_key, w_value, ordered, gain, grad_middle = ins[:9]
    parts = ins[9:]
    out, = outs
    shares = parts[0][...].astype(F32)
    for part in parts[1:]:
        shares = shares + part[...].astype(F32)
    grad_hidden = dot(grad_q[...], w_query[...], NT) + jnp.concatenate(
        [shares, dot(grad_kc[...], w_key[...], NT) + dot(grad_vc[...], w_value[...], NT)], axis=0
    )
    tokens = ordered[...].astype(F32)
    scale = root(tokens)
    grad = grad_middle[...] + norm_back(tokens * scale, scale, grad_hidden * gain[...])
    back = order_matrix_t(grad.shape[0])
    high = grad.astype(BF)
    rest = grad - high.astype(F32)
    mid = rest.astype(BF)
    last = (rest - mid.astype(F32)).astype(BF)
    out[...] = (dot(back, high) + dot(back, mid)) + dot(back, last)


def halves_kernel(info, ins, outs, scratch):
    kept, came = ins
    for m, out in enumerate(outs):
        out[...] = (kept[m].astype(F32) + came[m].astype(F32)).astype(BF)


def join_kernel(info, ins, outs, scratch):
    out, = outs
    rows = ins[0].shape[0]
    for i, piece in enumerate(ins):
        out[i * rows : (i + 1) * rows, :] = piece[...]


def keys_and_values(rows, w_key, w_value, deps=()):
    width = rows.shape[1]
    chips = rows.shape[0] // (NPR * PR_DEV)
    many = 2
    block = many * NPR * PR_DEV
    steps = chips // many

    def kernel(rows_ref, w_key_ref, w_value_ref, *refs):
        k_ref, v_ref = refs[len(deps) :]
        values = rows_ref[...]
        k_ref[...] = dot(values, w_key_ref[...]).astype(BF).reshape(many, NPR, PR_DEV, width)
        v_ref[...] = dot(values, w_value_ref[...]).astype(BF).reshape(many, NPR, PR_DEV, width)

    weight = pl.BlockSpec((width, width), lambda i: (0, 0))
    out = pl.BlockSpec((many, NPR, PR_DEV, width), lambda i: (i, 0, 0, 0))
    return pl.pallas_call(
        kernel,
        grid=(steps,),
        in_specs=[pl.BlockSpec((block, width), lambda i: (i, 0)), weight, weight]
        + [pl.BlockSpec(memory_space=pl.ANY)] * len(deps),
        out_specs=[out, out],
        out_shape=[shape_of((chips, NPR, PR_DEV, width), BF)] * 2,
        compiler_params=pltpu.CompilerParams(vmem_limit_bytes=16 * MIB),
        cost_estimate=cost("keys_and_values"),
        name="keys_and_values",
    )(rows, w_key, w_value, *deps)


def shares_of(dk, dv, w_key, w_value):
    chips, width = dk.shape[0], w_key.shape[0]
    rows = chips * NPR * PR_DEV
    total = dot(dk.reshape(rows, width), w_key, NT) + dot(dv.reshape(rows, width), w_value, NT)
    return total.astype(BF).reshape(chips, NPR * PR_DEV, width)


def dense_gradients(info, hidden, rows, dq, dks, dvs, dkc, dvc, proj, few):
    width = hidden.shape[1]
    n_keys = len(rows)
    span = rows[0].shape[0]
    step = width // 3
    half = width // 2
    extra = few.shape[0]
    total = 4 * width + extra

    def kernel(info_ref, hidden_ref, *refs):
        row_refs = refs[:n_keys]
        dq_ref = refs[n_keys]
        dk_refs = refs[n_keys + 1 : 2 * n_keys + 1]
        dv_refs = refs[2 * n_keys + 1 : 3 * n_keys + 1]
        dkc_ref, dvc_ref, proj_ref, few_ref, mine, theirs = refs[3 * n_keys + 1 :]
        j = pl.program_id(0)
        core = info_ref[3]
        query = dot(hidden_ref[...], dq_ref[...], TN)
        both = dot(
            hidden_ref[NPR * PR_DEV :, :],
            jnp.concatenate([dkc_ref[...], dvc_ref[...]], axis=1),
            TN,
        )
        for row_ref, dk_ref, dv_ref in zip(row_refs, dk_refs, dv_refs):
            both = both + dot(
                row_ref[...],
                jnp.concatenate(
                    [dk_ref[...].reshape(span, step), dv_ref[...].reshape(span, step)], axis=1
                ),
                TN,
            )
        pieces = [
            query.astype(BF),
            both[:, :step].astype(BF),
            both[:, step:].astype(BF),
            proj_ref[...],
            few_ref[...],
        ]

        def put(out, at, start, size):
            row = 0
            for piece in pieces:
                out[row : row + piece.shape[0], at : at + size] = piece[:, start : start + size]
                row += piece.shape[0]

        rest = half - step
        for side, (low_out, high_out) in enumerate(((mine, theirs), (theirs, mine))):

            @pl.when(jnp.logical_and(core == side, j == 0))
            def _():
                put(low_out, 0, 0, step)

            @pl.when(jnp.logical_and(core == side, j == 1))
            def _():
                put(low_out, step, 0, rest)
                put(high_out, 0, rest, step - rest)

            @pl.when(jnp.logical_and(core == side, j == 2))
            def _():
                put(high_out, step - rest, 0, step)

    def const(shape):
        return pl.BlockSpec(shape, lambda j, info: (0,) * len(shape), pipeline_mode=pl.Buffered(1))

    def columns(rows_of):
        return pl.BlockSpec((rows_of, step), lambda j, info: (0, j))

    keys = pl.BlockSpec(dks[0].shape[:3] + (step,), lambda j, info: (0, 0, 0, j))
    out = pl.BlockSpec((total, half), lambda j, info: (0, 0))
    return pl.pallas_call(
        kernel,
        grid_spec=pltpu.PrefetchScalarGridSpec(
            num_scalar_prefetch=1,
            grid=(3,),
            in_specs=[const(hidden.shape)]
            + [const(r.shape) for r in rows]
            + [columns(dq.shape[0])]
            + [keys] * (2 * n_keys)
            + [columns(CLEN), columns(CLEN), columns(width), columns(extra)],
            out_specs=[out, out],
        ),
        out_shape=[shape_of((total, half), BF)] * 2,
        compiler_params=pltpu.CompilerParams(vmem_limit_bytes=60 * MIB),
        cost_estimate=cost("dense_gradients"),
        name="dense_gradients",
    )(info, hidden, *rows, dq, *dks, *dvs, dkc, dvc, proj, few)


def gelu_parts(a):
    square = a * a
    t = jnp.tanh(a * (0.7978845608 + (0.7978845608 * 0.044715) * square))
    half = 0.5 + 0.5 * t
    value = a * half
    slope = half + value * (1.0 - t) * (0.7978845608 + (0.7978845608 * 3.0 * 0.044715) * square)
    return value, slope


def gather_rows(into, blocks, first, room):
    for m in range(blocks.shape[0]):
        into[m * room : (m + 1) * room, :] = blocks[m, pl.ds(pl.multiple_of(first, 16), room), :]


def other_column(others, blocks, first, room):
    at = blocks.shape[1] - TABLE
    span = min(blocks.shape[2], -(-at // 128) * 128)
    eye = iota((room, span), 1) == iota((room, span), 0) + first
    for m in range(blocks.shape[0]):
        row = blocks[m, at : at + TABLE, :span][:1].astype(F32)
        column = jnp.sum(jnp.where(eye, row, 0.0), axis=1, keepdims=True)
        others[m * room : (m + 1) * room, :] = jnp.broadcast_to(column, (room, 128))


def gated(rows, cots, others, w_router, mine):
    logits = dot(rows, w_router)
    column = iota(logits.shape, 1)
    own = jnp.sum(jnp.where(column == mine, logits, 0.0), axis=1, keepdims=True)
    other = others[:, : logits.shape[1]].astype(jnp.int32)
    theirs = jnp.sum(jnp.where(column == other, logits, 0.0), axis=1, keepdims=True)
    gate = 1.0 / (1.0 + jnp.exp(theirs - own))
    return (gate * cots.astype(F32)).astype(BF)


def expert_forward(x_slots, w_in, w_out, room, deps=()):
    devices, per, _ = x_slots.shape
    local, width, units = w_in.shape
    rows = devices * room
    chunk = min(units, 768)

    def kernel(x_ref, w_in_ref, w_out_ref, *refs):
        slope_ref, out, x = refs[len(deps) :]
        l = pl.program_id(0)
        gather_rows(x, x_ref, l * room, room)
        parts = [slice(at, at + chunk) for at in range(0, units, chunk)]
        pre = [dot(x[...], w_in_ref[0, :, part]) for part in parts]
        total = jnp.zeros((rows, width), F32)
        for part, act in zip(parts, pre):
            value, slope = gelu_parts(act)
            slope_ref[0, :, part] = slope.astype(BF)
            total = total + dot(value.astype(BF), w_out_ref[0, part, :])
        for m in range(devices):
            out[m, pl.ds(pl.multiple_of(l * room, 16), room), :] = total[
                m * room : (m + 1) * room, :
            ].astype(BF)

    slots = pl.BlockSpec(x_slots.shape, lambda l: (0, 0, 0))
    return pl.pallas_call(
        kernel,
        grid=(local,),
        in_specs=[
            slots,
            pl.BlockSpec((1, width, units), lambda l: (l, 0, 0)),
            pl.BlockSpec((1, units, width), lambda l: (l, 0, 0)),
        ]
        + [pl.BlockSpec(memory_space=pl.ANY)] * len(deps),
        out_specs=[pl.BlockSpec((1, rows, units), lambda l: (l, 0, 0)), slots],
        out_shape=[shape_of((local, rows, units), BF), shape_of(x_slots.shape, BF)],
        scratch_shapes=[pltpu.VMEM((rows, width), BF)],
        compiler_params=pltpu.CompilerParams(vmem_limit_bytes=48 * MIB),
        cost_estimate=cost("expert_forward"),
        name="expert_forward",
    )(x_slots, w_in, w_out, *deps)


def expert_backward(info, x_slots, c_slots, slope, w_router, w_in, w_out, room, deps=()):
    devices, per, _ = x_slots.shape
    local, width, units = w_in.shape
    rows = devices * room
    chunk = min(units, 768)

    def kernel(info_ref, x_ref, c_ref, router_ref, slope_ref, w_in_ref, w_out_ref, *refs):
        out, x, grad, others = refs[len(deps) :]
        l = pl.program_id(0)
        gather_rows(x, x_ref, l * room, room)
        gather_rows(grad, c_ref, l * room, room)
        other_column(others, c_ref, l * room, room)
        grad[...] = gated(
            x[...], grad[...], others[...], router_ref[...], info_ref[0] * local + l
        )
        parts = [slice(at, at + chunk) for at in range(0, units, chunk)]
        grad_act = [dot(grad[...], w_out_ref[0, part, :], NT) for part in parts]
        total = jnp.zeros((rows, width), F32)
        for part, act in zip(parts, grad_act):
            grad_pre = (act * slope_ref[0, :, part].astype(F32)).astype(BF)
            total = total + dot(grad_pre, w_in_ref[0, :, part], NT)
        for m in range(devices):
            out[m, pl.ds(pl.multiple_of(l * room, 16), room), :] = total[
                m * room : (m + 1) * room, :
            ].astype(BF)

    slots = pl.BlockSpec(x_slots.shape, lambda l, info: (0, 0, 0))
    return pl.pallas_call(
        kernel,
        grid_spec=pltpu.PrefetchScalarGridSpec(
            num_scalar_prefetch=1,
            grid=(local,),
            in_specs=[
                slots,
                pl.BlockSpec(c_slots.shape, lambda l, info: (0, 0, 0)),
                pl.BlockSpec(w_router.shape, lambda l, info: (0, 0)),
                pl.BlockSpec((1, rows, units), lambda l, info: (l, 0, 0)),
                pl.BlockSpec((1, width, units), lambda l, info: (l, 0, 0)),
                pl.BlockSpec((1, units, width), lambda l, info: (l, 0, 0)),
            ]
            + [pl.BlockSpec(memory_space=pl.ANY)] * len(deps),
            out_specs=slots,
            scratch_shapes=[
                pltpu.VMEM((rows, width), BF),
                pltpu.VMEM((rows, width), BF),
                pltpu.VMEM((rows, 128), F32),
            ],
        ),
        out_shape=shape_of(x_slots.shape, BF),
        compiler_params=pltpu.CompilerParams(vmem_limit_bytes=48 * MIB),
        cost_estimate=cost("expert_backward"),
        name="expert_backward",
    )(info, x_slots, c_slots, w_router, slope, w_in, w_out, *deps)


def expert_weights(info, groups, w_router, w_in, w_out, room, dp, before=None, last=False, deps=()):
    devices = groups[0][0].shape[0]
    local, width, units = w_in.shape
    part, share = units // dp, width // dp
    rows = devices * room
    flat, places = [], []
    for x, x_base, c, c_base in groups:
        at = []
        for array in (x, c):
            known = [i for i, other in enumerate(flat) if other is array]
            if not known:
                flat.append(array)
            at.append(known[0] if known else len(flat) - 1)
        places.append((at[0], x_base, at[1], c_base))
    n_flat = len(flat)
    sums = [] if before is None else list(before)

    def kernel(info_ref, *refs):
        slots = refs[:n_flat]
        router_ref, w_in_ref, w_out_ref = refs[n_flat : n_flat + 3]
        refs = refs[n_flat + 3 :]
        earlier = refs[: len(sums)]
        refs = refs[len(sums) + len(deps) :]
        out_ref, in_refs = refs[0], refs[1:-4]
        xs, grads, all_others, total = refs[-4:]
        l = pl.program_id(0)
        for g, (x_at, x_base, c_at, c_base) in enumerate(places):
            x, grad, others = xs.at[g], grads.at[g], all_others.at[g]
            gather_rows(x, slots[x_at], x_base + l * room, room)
            gather_rows(grad, slots[c_at], c_base + l * room, room)
            other_column(others, slots[c_at], c_base + l * room, room)
            grad[...] = gated(
                x[...], grad[...], others[...], router_ref[...], info_ref[0] * local + l
            )
            value, slope = gelu_parts(dot(x[...], w_in_ref[0]))
            grad_act = dot(grad[...], w_out_ref[0], NT)
            grad_pre = (grad_act * slope).astype(BF)
            part_in = dot(x[...], grad_pre, TN)
            part_out = dot(value.astype(BF), grad[...], TN)
            if g > 0:
                total[...] += part_in
                out_ref[0] += part_out
            elif earlier:
                total[...] = earlier[1][0] + part_in
                out_ref[0] = earlier[0][0] + part_out
            else:
                total[...] = part_in
                out_ref[0] = part_out
        if last:
            for k in range(dp):
                start = pl.multiple_of(jnp.bitwise_xor(info_ref[2], k) * share, 16)
                in_refs[k][0] = total[pl.ds(start, share), :].astype(BF)
        else:
            in_refs[0][0] = total[...]

    def const(shape):
        return pl.BlockSpec(shape, lambda l, info: (0,) * len(shape), pipeline_mode=pl.Buffered(1))

    square = pl.BlockSpec((1, part, width), lambda l, info: (l, 0, 0))
    square_in = pl.BlockSpec((1, width, part), lambda l, info: (l, 0, 0))
    if last:
        in_specs = [pl.BlockSpec((1, share, part), lambda l, info: (l, 0, 0))] * dp
        in_shapes = [shape_of((local, share, part), BF)] * dp
    else:
        in_specs = [square_in]
        in_shapes = [shape_of((local, width, part), F32)]
    got = pl.pallas_call(
        kernel,
        grid_spec=pltpu.PrefetchScalarGridSpec(
            num_scalar_prefetch=1,
            grid=(local,),
            in_specs=[const(x.shape) for x in flat]
            + [
                const(w_router.shape),
                pl.BlockSpec((1, width, part), lambda l, info: (l, 0, info[2])),
                pl.BlockSpec((1, part, width), lambda l, info: (l, info[2], 0)),
            ]
            + [square, square_in][: len(sums)]
            + [pl.BlockSpec(memory_space=pl.ANY)] * len(deps),
            out_specs=[square] + in_specs,
            scratch_shapes=[
                pltpu.VMEM((len(places), rows, width), BF),
                pltpu.VMEM((len(places), rows, width), BF),
                pltpu.VMEM((len(places), rows, 128), F32),
                pltpu.VMEM((width, part), F32),
            ],
        ),
        out_shape=[shape_of((local, part, width), F32)] + in_shapes,
        compiler_params=pltpu.CompilerParams(vmem_limit_bytes=44 * MIB),
        cost_estimate=cost("expert_weights_last" if last else "expert_weights"),
        name="expert_weights_last" if last else "expert_weights",
    )(info, *flat, w_router, w_in, w_out, *sums, *deps)
    return got[0], got[1:]


def columns_kernel(info, ins, outs, scratch):
    out, = outs
    part = ins[0].shape[2]
    for k, piece in enumerate(ins):
        start = pl.multiple_of(jnp.bitwise_xor(info[2], k) * part, 128)
        out[:, :, pl.ds(start, part)] = piece[...].astype(F32)


class Sums:
    def __init__(self, info, mine, theirs, n, dp, devices):
        self.info, self.n, self.dp, self.devices = info, n, dp, devices
        self.half = mine.shape[1]
        self.rows = self.width = 2 * self.half
        self.chips = devices // 2
        self.tall = self.rows // self.chips
        self.short = self.tall // dp
        self.extra = mine.shape[0] - n * self.rows
        self.value = mine
        self.came = swap(theirs, "expert", 1)

    @staticmethod
    def fits(rows, width, dp, devices):
        short = rows // (devices // 2) // dp
        return short % 16 == 0 and width % 256 == 0 and short * dp * (devices // 2) == rows

    def cores(self, deps=()):
        n, rows, tall, half, extra = self.n, self.rows, self.tall, self.half, self.extra

        def kernel(info_ref, ins, outs, scratch):
            kept, got = ins
            for m, out in enumerate(outs):
                for i in range(n):
                    start = i * rows + jnp.bitwise_xor(info_ref[4], m) * tall
                    at = pl.ds(pl.multiple_of(start, 16), tall)
                    out[i * tall : (i + 1) * tall, :] = (
                        kept[at, :].astype(F32) + got[at, :].astype(F32)
                    ).astype(BF)
                if extra:
                    out[n * tall :, :] = (
                        kept[n * rows :, :].astype(F32) + got[n * rows :, :].astype(F32)
                    ).astype(BF)

        pieces = run(
            kernel, "sum_cores", self.info, [self.value, self.came],
            [shape_of((n * tall + extra, half), BF)] * self.chips, deps=deps,
        )
        self.pieces = [pieces[0]] + [
            swap(pieces[m], "expert", 2 * m) for m in range(1, self.chips)
        ]
        return pieces[0]

    def planes(self, deps=()):
        n, tall, short, half, extra = self.n, self.tall, self.short, self.half, self.extra

        def kernel(info_ref, ins, outs, scratch):
            total, = scratch
            total[...] = added([piece[...].astype(F32) for piece in ins]).astype(BF)
            out, = outs
            for k in range(out.shape[0]):
                for i in range(n):
                    start = i * tall + k * short
                    out[k, i * short : (i + 1) * short, :] = total[start : start + short, :]
                if extra:
                    out[k, n * short :, :] = total[n * tall :, :]

        sent, = run(
            kernel, "sum_chips", self.info, self.pieces,
            [shape_of((self.dp, n * short + extra, half), BF)],
            scratch=[pltpu.VMEM((n * tall + extra, half), BF)], deps=deps,
        )
        self.pieces = lax.all_to_all(sent, "dp", split_axis=0, concat_axis=0, tiled=True)
        return sent

    def groups(self, beside, deps=()):
        n, short, half, extra, dp = self.n, self.short, self.half, self.extra, self.dp

        def kernel(info_ref, ins, outs, scratch):
            value = added([ins[0][k].astype(F32) for k in range(dp)]).astype(BF)
            for k in range(dp):
                outs[0][k] = value[: n * short]
            outs[1][...] = value[n * short :]

        own, self.few = run(
            kernel, "sum_groups", self.info, [self.pieces],
            [shape_of((dp, n * short, half), BF), shape_of((extra, half), BF)], deps=deps,
        )
        own, beside = lax.optimization_barrier((own, beside))
        self.own = lax.all_to_all(own, "dp", split_axis=0, concat_axis=0, tiled=True)
        return own, beside

    def gather(self):
        spread = self.own.reshape(self.dp * self.n * self.short, self.half)
        self.spread = jnp.concatenate(
            [spread] + [swap(spread, "expert", 2 * m) for m in range(1, self.chips)] + [self.few],
            axis=0,
        )
        self.other = swap(self.spread, "expert", 1)

    def finish(self, columns, gain, weights):
        got = self.put(0, self.spread, columns, gain, weights, ())
        return self.put(1, self.other, columns, gain, weights, got)

    def put(self, side, spread, columns, gain, weights, before):
        n, short, tall, half, extra = self.n, self.short, self.tall, self.half, self.extra
        chips, dp, rows, width = self.chips, self.dp, self.rows, self.width
        n_weights, n_before = len(weights), len(before)

        def kernel(info_ref, ref, gain_ref, *refs):
            weight_refs = refs[:n_weights]
            earlier = refs[n_weights : n_weights + n_before]
            outs = refs[n_weights + n_before :]
            for m in range(chips):
                for k in range(dp):
                    start = jnp.bitwise_xor(info_ref[4], m) * tall + k * short
                    at = pl.ds(pl.multiple_of(start, 16), short)
                    for i in range(n):
                        place = ((m * dp + k) * n + i) * short
                        outs[i][at, :] = ref[place : place + short, :].astype(F32)
            few = ref[chips * dp * n * short :, :].astype(F32)
            outs[n][...] = few[:columns, :].T
            outs[n + 1][...] = few[columns : columns + 1, :]
            along = gained(zip(weight_refs, outs), gain_ref[...])
            outs[n + 2][...] = earlier[-1][...] + along if earlier else along

        def half_of(block, axis):
            def index(i, info):
                core = jnp.bitwise_xor(info[3], side)
                return (core, 0) if axis == 0 else (0, core)

            return pl.BlockSpec(block, index)

        def const(shape):
            return pl.BlockSpec(shape, lambda i, info: (0, 0))

        square, row = half_of((rows, half), 1), const((1, width))
        outs = [shape_of((rows, width), F32)] * n
        outs = outs + [shape_of((width, columns), F32), shape_of((1, width), F32)]
        return pl.pallas_call(
            kernel,
            grid_spec=pltpu.PrefetchScalarGridSpec(
                num_scalar_prefetch=1,
                grid=(1,),
                in_specs=[const(spread.shape), row]
                + [square] * n_weights
                + [pl.BlockSpec(memory_space=pl.ANY)] * max(n_before - 1, 0)
                + [row] * min(n_before, 1),
                out_specs=[square] * n + [half_of((half, columns), 0), half_of((1, half), 1), row],
            ),
            out_shape=outs + [shape_of((1, width), F32)],
            input_output_aliases={3 + n_weights + i: i for i in range(n_before - 1)},
            compiler_params=pltpu.CompilerParams(vmem_limit_bytes=24 * MIB),
            cost_estimate=cost("spread_sums"),
            name="spread_sums",
        )(self.info, spread, gain, *weights, *before)


def gained(pairs, gain):
    total = 0.0
    for weight, grad in pairs:
        total = total + jnp.sum(weight[...].astype(F32) * grad[...], axis=1, keepdims=True)
    return jnp.broadcast_to(total, (total.shape[0], 128)).T[:1] / gain


def per_device(
    inputs,
    gain_one,
    w_query,
    w_key,
    w_value,
    w_out_proj,
    gain_two,
    w_router,
    w_in,
    w_out,
    routes,
    slot_index,
    prompt_of,
    cotangent,
):
    row_count, width = inputs.shape[1], inputs.shape[2]
    dp, devices = lax.axis_size("dp"), lax.axis_size("expert")
    z, device = lax.axis_index("dp"), lax.axis_index("expert")
    chips = devices // 2
    prompt_rows = NPR * PR_DEV
    expert_count, local = w_router.shape[1], w_in.shape[0]
    capacity = max(2, 5 * row_count * TOP // (4 * expert_count))
    room = -(-capacity // 16) * 16
    per = local * room
    info = jnp.stack(
        [device, prompt_of[0, 0], z, lax.rem(device, 2), lax.div(device, 2)]
    ).astype(jnp.int32)
    gain_one = gain_one[None, :]
    gain_two = gain_two[None, :]
    wide = shape_of((row_count, width), BF)
    wide32 = shape_of((row_count, width), F32)
    narrow = shape_of((row_count, 128), F32)
    x_shape = shape_of((devices, per, width), BF)
    c_shape = shape_of((devices, per + TABLE, width), BF)

    hidden_p, hidden, ordered = run(
        norm_kernel, "norm", info, [inputs[0], gain_one],
        [shape_of((prompt_rows, width), BF), wide, wide],
    )
    near = [hidden_p] + [swap(hidden_p, "expert", 2 * m) for m in range(1, chips)]

    message, cols, c_sent = run(
        table_kernel(per, room, capacity), "table", info,
        [cotangent[0], routes[0], slot_index[0]],
        [shape_of((row_count + TABLE, width), BF), narrow, c_shape],
        deps=[hidden_p],
    )
    hidden_c = hidden[prompt_rows:]
    queries = dot(hidden, w_query).astype(BF)
    key_c = dot(hidden_c, w_key).astype(BF)
    value_c = dot(hidden_c, w_value).astype(BF)
    near, cols, queries, key_c, value_c = lax.optimization_barrier(
        (near, cols, queries, key_c, value_c)
    )
    near, = run(join_kernel, "join", info, near, [shape_of((chips * prompt_rows, width), BF)])
    other = swap(near, "expert", 1)
    messages = far_groups(message, dp)
    c_sent, near = lax.optimization_barrier((c_sent, near))
    c_slots = [exchange(c_sent)]

    key_near, value_near = keys_and_values(near, w_key, w_value)
    key_other, value_other = keys_and_values(other, w_key, w_value, deps=[key_near])
    keys, values = [key_near, key_other], [value_near, value_other]
    attended, lse = attention_forward(info, queries, keys, values, key_c, value_c)
    c_slots, messages, attended = lax.optimization_barrier((c_slots, messages, attended))

    middle, second, gates, x_sent = run(
        middle_kernel(per), "middle", info,
        [ordered, attended, w_out_proj, gain_two, w_router, cols, message],
        [wide32, wide, narrow, x_shape],
    )
    x_slots = [exchange(x_sent)]
    seconds = far_groups(second, dp)
    c_rest = run(
        dispatch_cot_kernel(per), "dispatch_cot", info, messages,
        [shape_of((devices, len(messages) * per + TABLE, width), BF)], deps=[middle],
    )
    x_slots, c_rest = lax.optimization_barrier((x_slots, c_rest))
    c_even, = [exchange(sent) for sent in c_rest]

    slope, out_sent = expert_forward(x_slots[0], w_in, w_out, room)
    seconds, slope, c_slots[0], x_slots[0] = lax.optimization_barrier(
        (seconds, slope, c_slots[0], x_slots[0])
    )
    c_odd = [swap(c_slots[0], "dp", 1)]
    x_odd = [swap(x_slots[0], "dp", 1)]
    seconds = with_neighbours(seconds)
    messages = with_neighbours(messages)
    returned = exchange(out_sent)
    grad_sent = expert_backward(
        info, x_slots[0], c_slots[0], slope, w_router, w_in, w_out, room, deps=[c_even]
    )
    returned, grad_sent = lax.optimization_barrier((returned, grad_sent))
    grad_returned = exchange(grad_sent)

    sums = expert_weights(
        info, [(x_slots[0], 0, c_slots[0], 0)], w_router, w_in, w_out, room, dp,
        deps=[grad_sent],
    )
    far = dp - 2
    odd = far // 2
    rest, = run(
        dispatch_kernel(per), "dispatch", info, messages + seconds,
        [shape_of((devices, (odd + far) * per + TABLE, width), BF)], deps=[sums[0]],
    )

    outputs, grad_middle, grad_attended, grad_proj, few, delta = run(
        combine_kernel(), "combine", info,
        [middle, second, gates, cols, message, attended, w_out_proj, w_router, gain_two]
        + [returned, grad_returned],
        [wide, wide32, wide, shape_of((width, width), BF), shape_of((expert_count + 16, width), BF),
         shape_of((width // PAIR, 3, TWO), F32)],
        deps=[rest],
    )
    rest = exchange(rest)

    pairs = width // PAIR

    def back(first, count, before=(), deps=()):
        return attention_backward(
            info, queries, keys, values, key_c, value_c, grad_attended, lse, delta, first, count,
            before=before, deps=deps,
        )

    got = back(0, pairs, deps=())
    grad_q, dk_near, dk_far, dv_near, dv_far, grad_kc, grad_vc = got
    grad_q, dk_near, dk_far, dv_near, dv_far, x_odd, c_odd = lax.optimization_barrier(
        (grad_q, dk_near, dk_far, dv_near, dv_far, x_odd, c_odd)
    )
    stepwise = Sums.fits(width, width, dp, devices)
    if stepwise:
        mine, theirs = dense_gradients(
            info, hidden, [near, other], grad_q, [dk_near, dk_far], [dv_near, dv_far],
            grad_kc, grad_vc, grad_proj, few,
        )
        total = Sums(info, mine, theirs, 4, dp, devices)
    else:
        flat = [part.reshape(chips * prompt_rows, width) for part in (dk_near, dk_far, dv_near, dv_far)]
        grad_query = dot(hidden, grad_q, TN)
        grad_key = dot(near, flat[0], TN) + dot(other, flat[1], TN) + dot(hidden_c, grad_kc, TN)
        grad_value = dot(near, flat[2], TN) + dot(other, flat[3], TN) + dot(hidden_c, grad_vc, TN)
        dense = [grad_query, grad_key, grad_value, grad_proj, few]

    sent = shares_of(dk_far, dv_far, w_key, w_value)
    kept = shares_of(dk_near, dv_near, w_key, w_value)
    came = swap(sent, "expert", 1)
    after = total.cores([kept]) if stepwise else kept
    shares = run(
        halves_kernel, "halves", info, [kept, came],
        [shape_of((prompt_rows, width), BF)] * chips, deps=[after],
    )

    others = [(x_odd[0], 0, c_odd[0], 0)]
    for g in range(far):
        c_from, c_base = (rest, g // 2 * per) if g % 2 else (c_even, g // 2 * per)
        others.append((rest, (odd + g) * per, c_from, c_base))
    grad_w_out, in_pieces = expert_weights(
        info, others, w_router, w_in, w_out, room, dp,
        before=(sums[0], sums[1][0]), last=True, deps=[shares[0]],
    )
    shares, in_pieces, grad_w_out = lax.optimization_barrier((shares, in_pieces, grad_w_out))
    after = [grad_w_out]
    if stepwise:
        after = [total.planes(after)]
    shares = [shares[0]] + [swap(shares[m], "expert", 2 * m) for m in range(1, chips)]
    if stepwise:
        own, shares = total.groups(shares, after)
        after = [own]
    grad_input, = run(
        input_kernel, "input", info,
        [grad_q, grad_kc, grad_vc, w_query, w_key, w_value, ordered, gain_one, grad_middle] + shares,
        [wide32], deps=after,
    )
    if stepwise:
        total.own, grad_input, in_pieces = lax.optimization_barrier(
            (total.own, grad_input, in_pieces)
        )
        total.gather()
    far_first = [swap(in_pieces[k], "dp", k) for k in range(dp - 1, 0, -1)]
    in_pieces = [in_pieces[0]] + far_first[::-1]
    after = []
    if stepwise:
        query_sum, key_sum, value_sum, proj_sum, grad_router, grad_gain_two, grad_gain_one = (
            total.finish(expert_count, gain_one, [w_query, w_key, w_value])
        )
        after = [query_sum]
    else:
        query_sum, key_sum, value_sum, proj_sum, few = lax.psum(
            [part.astype(F32) for part in dense], ("dp", "expert")
        )
        grad_router, grad_gain_two = few[:expert_count].T, few[expert_count :][:1]
        grad_gain_one = gained(
            [(w_query, query_sum), (w_key, key_sum), (w_value, value_sum)], gain_one
        )
    grad_w_in, = run(
        columns_kernel, "columns", info, in_pieces,
        [shape_of((local, width // dp, w_in.shape[2]), F32)], deps=after,
    )
    return (
        outputs[None],
        grad_input[None],
        grad_gain_one[0],
        query_sum,
        key_sum,
        value_sum,
        proj_sum,
        grad_gain_two[0],
        grad_router,
        grad_w_in,
        grad_w_out,
    )


def solution(mesh):
    return jax.shard_map(
        per_device,
        mesh=mesh,
        in_specs=(
            P("dp", "expert", None),
            P(),
            P(),
            P(),
            P(),
            P(),
            P(),
            P(),
            P("expert", None, None),
            P("expert", None, None),
            P("dp", "expert", None),
            P("dp", "expert", None),
            P("dp", "expert"),
            P("dp", "expert", None),
        ),
        out_specs=(
            P("dp", "expert", None),
            P("dp", "expert", None),
            P(),
            P(),
            P(),
            P(),
            P(),
            P(),
            P(),
            P("expert", "dp", None),
            P("expert", "dp", None),
        ),
        check_vma=False,
    )
```
